512 devices in a mesh: group: 16 (over x, z_lo), sample: 32 (over y, z_hi, core).
Axes of the slice: x: 4, y: 4, z: 16 (z_hi: 4, z_lo: 4; z = z_hi * 4 + z_lo), core: 2. Of those that a mesh axis runs over, the one named last changes fastest.
Arguments:
- response_rows: bfloat16 [65536, 4096], P(('group', 'sample')), may hold values from -6 to 6
- prompt_rows: bfloat16 [8192, 4096], P(('group', 'sample')), may hold values from -6 to 6
- queries: bfloat16 [65536, 4096], P(('group', 'sample')), may hold values from -4.5 to 4.5
- response_keys: bfloat16 [65536, 512], P(('group', 'sample')), may hold values from -6 to 6
- prompt_keys: bfloat16 [8192, 512], P(('group', 'sample')), may hold values from -5 to 5
- cotangent: bfloat16 [65536, 4096], P(('group', 'sample')), may hold values from -96 to 96
- segment_index: int32 [512, 128], P(('group', 'sample')), may hold values from 0 to 7, never falling along the last dimension, each value on 1 to 32 neighbouring positions
- prompt_choice: int32 [512, 8], P(('group', 'sample')), may hold values from 0 to 3
- frozen_value_weight: bfloat16 [4096, 512], P('sample'), may hold values from -0.09375 to 0.09375
- value_adapter_down: bfloat16 [4096, 16], P('sample'), may hold values from -0.09375 to 0.09375
- value_adapter_up: bfloat16 [16, 512], replicated, may hold values from -1.5 to 1.5
Outputs:
- response_grad: bfloat16 [65536, 4096], P(('group', 'sample'))
- prompt_grad: bfloat16 [8192, 4096], P(('group', 'sample'))
- response_key_grad: bfloat16 [65536, 512], P(('group', 'sample'))
- prompt_key_grad: bfloat16 [8192, 512], P(('group', 'sample'))
- first_grad: float32 [4096, 16], P('sample')
- second_grad: float32 [16, 512], replicated
The draws below stay inside these ranges and needn't reach their ends.
Inputs may be any that keep to these rules, and one draw needn't show every extreme that they name: `segment_index`: within the 128 tokens of one device the response number never falls; each of the 8 responses has 1 to 32 tokens, and one has exactly 32.
All inputs are finite; a program needn't handle non-finite values.
Results may differ from the reference program's by a relative error of at most 0.015.
Values may be sent and summed in bfloat16 or wider, within the bound.
No kernel may reach another device: no remote copies, remote signals or barrier semaphores. Data moves between devices by JAX's collectives and lax.ppermute only.
A program may use at most 128 MiB of HBM per device.

```python
import math
import jax
import jax.numpy as jnp
import numpy as np
from jax import lax

D = 4096
HEADS = 32
KV_HEADS = 4
HEAD_DIM = 128
RANK = 16
PROMPTS = 4
PROMPT_LEN = 128
RESP_DEV = 128
RESPONSES = 8
RESP_MOST = 32
RESP_TOK = 65536
PROMPT_ROWS = 8192
TOKEN_TOTAL = 73728
N_GROUP = 16
N_SAMPLE = 32


def draw_queries(key, part):
    key = jax.random.fold_in(key, 7)
    first_key = jax.random.fold_in(key, 0)
    shape = (RESP_TOK, HEADS * HEAD_DIM)
    base = jnp.clip(jax.random.normal(first_key, shape, jnp.float32), -4.5, 4.5)
    return base.astype(jnp.bfloat16)


def draw_prompt_keys(key, part):
    key = jax.random.fold_in(key, 11)
    shape = (PROMPT_ROWS, KV_HEADS * HEAD_DIM)
    base = jnp.clip(jax.random.normal(key, shape, jnp.float32), -5.0, 5.0)
    return base.astype(jnp.bfloat16)


def touch_ends(result, own_key, least, high):
    longest = result.shape.index(max(result.shape))
    spots = []
    for shift in (0, 1):
        where = [jax.random.randint(jax.random.fold_in(own_key, axis), (), 0, length) for axis, length in enumerate(result.shape)]
        where[longest] = (where[longest] + shift) % result.shape[longest]
        spots.append(tuple(where))
    return result.at[spots[0]].set(least).at[spots[1]].set(high)


def levels(own_key, dims, pieces, low, largest):
    def one(axis_at, blocks):
        draws = jax.random.uniform(jax.random.fold_in(jax.random.fold_in(own_key, 6), axis_at), (blocks,), jnp.float32, low / len(pieces), largest / len(pieces))
        return jnp.repeat(jnp.exp(draws), dims[axis_at] // blocks).reshape((-1,) + (1,) * (len(dims) - axis_at - 1))

    gain = one(*pieces[0])
    for cut in pieces[1:]:
        gain = gain * one(*cut)
    return gain


def profile(count, total, bound, skew):
    loads = [(1 << 20) // math.isqrt(rank ** skew) + 1 for rank in range(2, count + 1)]
    surplus, counts = total - bound - (count - 1), [1] * (count - 1)
    while surplus > 0:
        free = [i for i in range(count - 1) if counts[i] < bound]
        mass, left = sum([loads[i] for i in free]), surplus
        for i in free:
            extra = min(bound - counts[i], max(1, left * loads[i] // mass), surplus)
            counts[i] = counts[i] + extra
            surplus = surplus - extra
    return np.array([bound] + counts)


def uneven(rng, amount, total, limit, slope):
    if amount == 2:
        one = jax.random.randint(rng, (), max(1, total - limit), min(limit, total - 1) + 1)
        return jnp.stack([one, total - one])
    lengths = jnp.asarray(profile(amount, total, limit, slope), jnp.int32)
    couples = (amount - 1) // 2
    donor, taker = lengths[1:1 + 2 * couples:2], lengths[2:2 + 2 * couples:2]
    room = jnp.minimum(donor - 1, limit - taker)
    moved = jax.random.randint(jax.random.fold_in(rng, 1), (couples,), 0, 1 << 20) % (room + 1)
    lengths = lengths.at[1:1 + 2 * couples:2].set(donor - moved).at[2:2 + 2 * couples:2].set(taker + moved)
    return lengths[jax.random.permutation(jax.random.fold_in(rng, 2), amount)]


def bell_draw(stream_key, shape, spread, reach, cuts=(), kind=jnp.bfloat16):
    entries = jax.random.normal(stream_key, shape, jnp.float32) * spread
    if len(cuts) > 0:
        entries = levels(stream_key, shape, cuts, -0.22, 0.18) * entries
    return jnp.clip(entries, min=-reach, max=reach).astype(kind)


def setup_inputs(seed: int = 0) -> dict:
    streams_of = jax.random.split(jax.random.key(seed), 12)
    return {
        "response_rows": bell_draw(streams_of[0], (RESP_TOK, D), 1.0, 6.0, ((0, 512),)),
        "prompt_rows": bell_draw(streams_of[1], (PROMPT_ROWS, D), 1.0, 6.0, ((0, 512),)),
        "queries": draw_queries(jax.random.fold_in(streams_of[11], 71), 0),
        "response_keys": bell_draw(streams_of[3], (RESP_TOK, KV_HEADS * HEAD_DIM), 1.0, 6.0, ((0, 512),)),
        "prompt_keys": draw_prompt_keys(jax.random.fold_in(streams_of[11], 71), 0),
        "cotangent": bell_draw(streams_of[5], (RESP_TOK, HEADS * HEAD_DIM), 16.0, 96.0, ((0, 512),)),
        "segment_index": jax.vmap(lambda own: jnp.searchsorted(jnp.cumsum(uneven(own, RESPONSES, RESP_DEV, RESP_MOST, 0)), jnp.arange(RESP_DEV), side="right"))(jax.random.split(streams_of[6], (N_GROUP * N_SAMPLE))).reshape((N_GROUP * N_SAMPLE, RESP_DEV)).astype(jnp.int32),
        "prompt_choice": touch_ends(jax.random.randint(streams_of[7], (N_GROUP * N_SAMPLE, RESPONSES), 0, PROMPTS), jax.random.fold_in(streams_of[7], 1), 0, PROMPTS - 1).astype(jnp.int32),
        "frozen_value_weight": bell_draw(streams_of[8], (D, KV_HEADS * HEAD_DIM), D ** -0.5, 0.09375, ((0, 32),)),
        "value_adapter_down": bell_draw(streams_of[9], (D, RANK), D ** -0.5, 0.09375, ((0, 32),)),
        "value_adapter_up": bell_draw(streams_of[10], (RANK, KV_HEADS * HEAD_DIM), RANK ** -0.5, 1.5),
    }


adapter_scale = 2.0


def project(row_block, frozen_value_weight, value_adapter_down, value_adapter_up):
    down_projection = jnp.dot(row_block, value_adapter_down, preferred_element_type=jnp.float32).astype(jnp.bfloat16)
    value_inputs = jnp.dot(row_block, frozen_value_weight, preferred_element_type=jnp.float32)
    value_inputs = value_inputs + adapter_scale * jnp.dot(down_projection, value_adapter_up, preferred_element_type=jnp.float32)
    return down_projection, value_inputs.astype(jnp.bfloat16)


def visibility(segments, choices, prompt_total):
    tokens_here = segments.shape[0]
    onehot = (segments[:, None] == jnp.arange(choices.shape[0], dtype=jnp.int32)[None, :]).astype(jnp.int32)
    token_prompt = jnp.sum(onehot * choices[None, :], axis=1)
    key_prompt = jnp.arange(prompt_total, dtype=jnp.int32) // PROMPT_LEN
    prompt_seen = token_prompt[:, None] == key_prompt[None, :]
    position = jnp.arange(tokens_here, dtype=jnp.int32)
    own_seen = (segments[:, None] == segments[None, :]) & (position[None, :] <= position[:, None])
    return jnp.concatenate([prompt_seen, own_seen], axis=1)


def attend(query_rows, cotangent_rows, key_rows, value_rows, visible):
    tokens_here = query_rows.shape[0]
    key_total = key_rows.shape[0]
    group_size = HEADS // KV_HEADS
    score_scale = HEAD_DIM ** -0.5
    query_heads = query_rows.reshape(tokens_here, KV_HEADS, group_size, HEAD_DIM).astype(jnp.float32)
    cotangent_heads = cotangent_rows.reshape(tokens_here, KV_HEADS, group_size, HEAD_DIM).astype(jnp.float32)
    key_heads = key_rows.reshape(key_total, KV_HEADS, HEAD_DIM).astype(jnp.float32)
    value_heads = value_rows.reshape(key_total, KV_HEADS, HEAD_DIM).astype(jnp.float32)
    scores = jnp.einsum('tkgd,skd->kgts', query_heads, key_heads) * score_scale
    scores = jnp.where(visible[None, None], scores, -1e30)
    row_top = jnp.max(scores, axis=-1, keepdims=True)
    powers = jnp.exp(scores - row_top)
    softmax_full = powers / jnp.sum(powers, axis=-1, keepdims=True)
    softmax_low = lax.optimization_barrier(softmax_full.astype(jnp.bfloat16)).astype(jnp.float32)
    mixture = jnp.einsum('kgts,skd->kgtd', softmax_low, value_heads)
    row_delta = jnp.einsum('tkgd,kgtd->kgt', cotangent_heads, mixture)
    grad_softmax = jnp.einsum('tkgd,skd->kgts', cotangent_heads, value_heads)
    grad_scores = softmax_full * (grad_softmax - row_delta[..., None])
    grad_low = lax.optimization_barrier(grad_scores.astype(jnp.bfloat16)).astype(jnp.float32)
    key_grads = jnp.einsum('kgts,tkgd->skd', grad_low, query_heads) * score_scale
    value_grads = jnp.einsum('kgts,tkgd->skd', softmax_low, cotangent_heads)
    return (key_grads.reshape(key_total, KV_HEADS * HEAD_DIM),
            value_grads.reshape(key_total, KV_HEADS * HEAD_DIM))


def contract_final_axis(left, right):
    return lax.dot_general(left, right, (((1,), (1,)), ((), ())), preferred_element_type=jnp.float32)


def contract_first(left, right):
    return lax.dot_general(left, right, (((0,), (0,)), ((), ())), preferred_element_type=jnp.float32)


def back_project(value_low_rank, row_block, down_projection, frozen_value_weight, value_adapter_down, value_adapter_up):
    low_rank_backward = contract_final_axis(value_low_rank, value_adapter_up).astype(jnp.bfloat16)
    output_gradient = contract_final_axis(value_low_rank, frozen_value_weight) + adapter_scale * contract_final_axis(low_rank_backward, value_adapter_down)
    first_part = contract_first(row_block, low_rank_backward)
    second_part = contract_first(down_projection, value_low_rank)
    return output_gradient.astype(jnp.bfloat16), first_part, second_part


def reference(response_rows, prompt_rows, queries, response_keys, prompt_keys, cotangent, segment_index, prompt_choice, frozen_value_weight, value_adapter_down, value_adapter_up):
    kv_width = KV_HEADS * HEAD_DIM
    group_prompt = PROMPTS * PROMPT_LEN
    response_split = response_rows.reshape(N_GROUP, N_SAMPLE, RESP_DEV, D)
    query_split = queries.reshape(N_GROUP, N_SAMPLE, RESP_DEV, HEADS * HEAD_DIM)
    rkey_split = response_keys.reshape(N_GROUP, N_SAMPLE, RESP_DEV, kv_width)
    cot_split = cotangent.reshape(N_GROUP, N_SAMPLE, RESP_DEV, HEADS * HEAD_DIM)
    seg_split = segment_index.reshape(N_GROUP, N_SAMPLE, RESP_DEV)
    choice_split = prompt_choice.reshape(N_GROUP, N_SAMPLE, RESPONSES)
    prompt_split = prompt_rows.reshape(N_GROUP, group_prompt, D)
    pkey_split = prompt_keys.reshape(N_GROUP, group_prompt, kv_width)

    def one_group(items):
        g_resp, g_query, g_rkey, g_cot, g_seg, g_choice, g_prompt, g_pkey = items
        p_first, p_values = project(g_prompt, frozen_value_weight, value_adapter_down, value_adapter_up)

        def one_device(inner):
            row_block, query_block, rkey_block, cot_block, seg_block, choice_block = inner
            r_first, r_values = project(row_block, frozen_value_weight, value_adapter_down, value_adapter_up)
            visible = visibility(seg_block, choice_block, group_prompt)
            key_rows = jnp.concatenate([g_pkey, rkey_block], axis=0)
            value_rows = jnp.concatenate([p_values, r_values], axis=0)
            key_grads, value_grads = attend(query_block, cot_block, key_rows, value_rows, visible)
            value_low_rank = value_grads[group_prompt:].astype(jnp.bfloat16)
            output_gradient, first_part, second_part = back_project(value_low_rank, row_block, r_first, frozen_value_weight, value_adapter_down, value_adapter_up)
            return (output_gradient, key_grads[group_prompt:].astype(jnp.bfloat16), key_grads[:group_prompt],
                    value_grads[:group_prompt], first_part, second_part)

        output_gradient, rkey_grads, pkey_parts, pvalue_parts, first_parts, second_parts = lax.map(
            one_device, (g_resp, g_query, g_rkey, g_cot, g_seg, g_choice))
        prompt_value_low = jnp.sum(pvalue_parts, axis=0).astype(jnp.bfloat16)
        prompt_key_low = jnp.sum(pkey_parts, axis=0).astype(jnp.bfloat16)
        p_grads, p_first_part, p_second_part = back_project(prompt_value_low, g_prompt, p_first, frozen_value_weight, value_adapter_down, value_adapter_up)
        return (output_gradient, p_grads, rkey_grads, prompt_key_low,
                jnp.sum(first_parts, axis=0) + p_first_part, jnp.sum(second_parts, axis=0) + p_second_part)

    output_gradient, p_grads, rkey_grads, pkey_grads, first_sums, second_sums = lax.map(
        one_group, (response_split, query_split, rkey_split, cot_split, seg_split, choice_split, prompt_split, pkey_split))
    adapter_factor = adapter_scale * TOKEN_TOTAL ** -0.5
    return (output_gradient.reshape(RESP_TOK, D), p_grads.reshape(PROMPT_ROWS, D),
            rkey_grads.reshape(RESP_TOK, kv_width), pkey_grads.reshape(PROMPT_ROWS, kv_width),
            jnp.sum(first_sums, axis=0) * adapter_factor, jnp.sum(second_sums, axis=0) * adapter_factor)
```

```python
import jax
import jax.numpy as jnp
import numpy as np
from jax import lax
from jax.experimental import pallas as pl
from jax.experimental.pallas import tpu as pltpu
from jax.sharding import Mesh, PartitionSpec as P

HEADS = 32
KV_HEADS = 4
HEAD_DIM = 128
GROUP_SIZE = HEADS // KV_HEADS
PROMPT_LEN = 128
PROMPTS = 4
RANK = 16
TOKENS = 128
D = 4096
SCALE = HEAD_DIM**-0.5
ADAPTER_SCALE = 2.0
AXES = ("x", "zl", "y", "zh", "c")
SAMPLE = ("y", "zh", "c")
GROUP = ("x", "zl")
PAIR = 2 * TOKENS
F32 = jnp.float32
BF16 = jnp.bfloat16


def swap(array, axis):
    return lax.all_to_all(array, axis, 0, 0, tiled=True)


def gather(array, axis):
    n = lax.axis_size(axis)
    return swap(jnp.broadcast_to(array[None], (n,) + array.shape), axis)


def nt(left, right):
    return lax.dot_general(left, right, (((1,), (1,)), ((), ())), preferred_element_type=F32)


def tn(left, right):
    return lax.dot_general(left, right, (((0,), (0,)), ((), ())), preferred_element_type=F32)


def nn(left, right):
    return jnp.dot(left, right, preferred_element_type=F32)


def expand(rows, chosen):
    zero = jnp.zeros_like(rows)
    return jnp.concatenate([jnp.where(chosen == p, rows, zero) for p in range(PROMPTS)], axis=1)


def pair_rows(ref, pair):
    first = 2 * pair * HEAD_DIM
    return jnp.concatenate(
        [ref[:, first : first + HEAD_DIM], ref[:, first + HEAD_DIM : first + 2 * HEAD_DIM]], axis=0
    )


def prompt_block(ref):
    return jnp.concatenate(
        [
            jnp.concatenate([ref[c, p, zh] for zh in range(4) for c in range(2)], axis=0)
            for p in range(PROMPTS)
        ],
        axis=1,
    )


def spread(ref, row, block):
    for p in range(PROMPTS):
        for zh in range(4):
            for c in range(2):
                s = (zh * 2 + c) * 16
                ref[c, p, zh, pl.ds(row, 16), :] = block[
                    s : s + 16, p * HEAD_DIM : (p + 1) * HEAD_DIM
                ].astype(ref.dtype)


def softmax_pair(key_cat, own_key, expanded, rows, bias):
    seen = nt(key_cat, expanded) * SCALE
    own = nt(own_key, rows) * SCALE + bias
    top = jnp.maximum(jnp.max(seen, axis=0, keepdims=True), jnp.max(own, axis=0, keepdims=True))
    seen, own = jnp.exp(seen - top), jnp.exp(own - top)
    total = jnp.sum(seen, axis=0, keepdims=True) + jnp.sum(own, axis=0, keepdims=True)
    return seen / total, own / total


def forward_kernel(
    q_ref, cot_ref, key_ref, own_key_ref, chosen_ref, bias_ref, x_ref, up_ref,
    send_ref, low_ref, back_ref,
    probs, own_probs, cots, back,
):
    k = pl.program_id(0)
    key_cat = prompt_block(key_ref)
    own_key = own_key_ref[...]
    chosen = chosen_ref[...]
    bias = bias_ref[...]
    for pair in range(GROUP_SIZE // 2):
        rows = pair_rows(q_ref, pair)
        seen, own = softmax_pair(key_cat, own_key, expand(rows, chosen), rows, bias)
        at = pl.ds(pair * PAIR, PAIR)
        probs[:, at] = seen.astype(BF16)
        own_probs[:, at] = own.astype(BF16)
        cot = pair_rows(cot_ref, pair)
        cots[at, : PROMPTS * HEAD_DIM] = expand(cot, chosen)
        cots[at, PROMPTS * HEAD_DIM :] = cot
    spread(send_ref, pl.multiple_of(k * 16, 16), nn(probs[...], cots[:, : PROMPTS * HEAD_DIM]))
    low = nn(own_probs[...], cots[:, PROMPTS * HEAD_DIM :]).astype(BF16)
    low_ref[...] = low

    @pl.when(k == 0)
    def _():
        back[...] = jnp.zeros_like(back)

    back[...] += nt(up_ref[...], low)

    @pl.when(k == KV_HEADS - 1)
    def _():
        back_low = back[...].astype(BF16)
        back_ref[...] = back_low
        first = nn(back_low, x_ref[...])
        for y in range(4):
            for zh in range(4):
                for c in range(2):
                    at = ((y * 4 + zh) * 2 + c) * 128
                    send_ref[c, y, zh, KV_HEADS * 16 :, :] = first[:, at : at + 128].astype(BF16)


def backward_kernel(
    q_ref, cot_ref, key_ref, value_ref, own_key_ref, own_value_ref, chosen_ref, bias_ref,
    send_ref, own_ref,
    grads, own_grads, queries,
):
    k = pl.program_id(0)
    key_cat, value_cat = prompt_block(key_ref), prompt_block(value_ref)
    own_key, own_value = own_key_ref[...], own_value_ref[...]
    chosen = chosen_ref[...]
    bias = bias_ref[...]
    for pair in range(GROUP_SIZE // 2):
        rows = pair_rows(q_ref, pair)
        expanded = expand(rows, chosen)
        at = pl.ds(pair * PAIR, PAIR)
        queries[at, : PROMPTS * HEAD_DIM] = expanded
        queries[at, PROMPTS * HEAD_DIM :] = rows
        seen, own = softmax_pair(key_cat, own_key, expanded, rows, bias)
        cot = pair_rows(cot_ref, pair)
        seen_grad = nt(value_cat, expand(cot, chosen))
        own_grad = nt(own_value, cot)
        delta = jnp.sum(seen.astype(BF16).astype(F32) * seen_grad, axis=0, keepdims=True) + jnp.sum(
            own.astype(BF16).astype(F32) * own_grad, axis=0, keepdims=True
        )
        grads[:, at] = (seen * (seen_grad - delta)).astype(BF16)
        own_grads[:, at] = (own * (own_grad - delta)).astype(BF16)
    spread(
        send_ref,
        pl.multiple_of(k * 16, 16),
        nn(grads[...], queries[:, : PROMPTS * HEAD_DIM]) * SCALE,
    )
    own_ref[...] = (nn(own_grads[...], queries[:, PROMPTS * HEAD_DIM :]) * SCALE).astype(BF16)


def whole(shape):
    return pl.BlockSpec(shape, lambda k: (0,) * len(shape))


def heads_of(rows, width):
    return pl.BlockSpec((rows, width), lambda k: (0, k))


PROMPT_SPEC = pl.BlockSpec((2, 4, 4, 16, HEAD_DIM), lambda k: (0, 0, 0, k, 0))
WIDE = GROUP_SIZE * HEAD_DIM
ROWS = GROUP_SIZE * TOKENS


def attend_forward(queries, cotangent, keys, own_keys, chosen, bias, rows, up):
    return pl.pallas_call(
        forward_kernel,
        grid=(KV_HEADS,),
        in_specs=[
            heads_of(TOKENS, WIDE),
            heads_of(TOKENS, WIDE),
            PROMPT_SPEC,
            heads_of(TOKENS, HEAD_DIM),
            whole((PAIR, HEAD_DIM)),
            whole((TOKENS, PAIR)),
            whole((TOKENS, D)),
            heads_of(RANK, HEAD_DIM),
        ],
        out_specs=[
            whole((2, 4, 4, KV_HEADS * 16 + RANK, HEAD_DIM)),
            heads_of(TOKENS, HEAD_DIM),
            whole((RANK, TOKENS)),
        ],
        out_shape=[
            jax.ShapeDtypeStruct((2, 4, 4, KV_HEADS * 16 + RANK, HEAD_DIM), BF16),
            jax.ShapeDtypeStruct((TOKENS, KV_HEADS * HEAD_DIM), BF16),
            jax.ShapeDtypeStruct((RANK, TOKENS), BF16),
        ],
        scratch_shapes=[
            pltpu.VMEM((TOKENS, ROWS), BF16),
            pltpu.VMEM((TOKENS, ROWS), BF16),
            pltpu.VMEM((ROWS, (PROMPTS + 1) * HEAD_DIM), BF16),
            pltpu.VMEM((RANK, TOKENS), F32),
        ],
        compiler_params=pltpu.CompilerParams(
            vmem_limit_bytes=40 << 20, dimension_semantics=("arbitrary",)
        ),
        cost_estimate=pl.CostEstimate(
            flops=2_000_000_000, bytes_accessed=5 << 20, transcendentals=1 << 20
        ),
        name="attend_forward",
    )(queries, cotangent, keys, own_keys, chosen, bias, rows, up)


def attend_backward(queries, cotangent, keys, values, own_keys, own_values, chosen, bias):
    return pl.pallas_call(
        backward_kernel,
        grid=(KV_HEADS,),
        in_specs=[
            heads_of(TOKENS, WIDE),
            heads_of(TOKENS, WIDE),
            PROMPT_SPEC,
            PROMPT_SPEC,
            heads_of(TOKENS, HEAD_DIM),
            heads_of(TOKENS, HEAD_DIM),
            whole((PAIR, HEAD_DIM)),
            whole((TOKENS, PAIR)),
        ],
        out_specs=[
            whole((2, 4, 4, KV_HEADS * 16, HEAD_DIM)),
            heads_of(TOKENS, HEAD_DIM),
        ],
        out_shape=[
            jax.ShapeDtypeStruct((2, 4, 4, KV_HEADS * 16, HEAD_DIM), BF16),
            jax.ShapeDtypeStruct((TOKENS, KV_HEADS * HEAD_DIM), BF16),
        ],
        scratch_shapes=[
            pltpu.VMEM((TOKENS, ROWS), BF16),
            pltpu.VMEM((TOKENS, ROWS), BF16),
            pltpu.VMEM((ROWS, (PROMPTS + 1) * HEAD_DIM), BF16),
        ],
        compiler_params=pltpu.CompilerParams(
            vmem_limit_bytes=40 << 20, dimension_semantics=("arbitrary",)
        ),
        cost_estimate=pl.CostEstimate(
            flops=3_000_000_000, bytes_accessed=5 << 20, transcendentals=1 << 20
        ),
        name="attend_backward",
    )(queries, cotangent, keys, values, own_keys, own_values, chosen, bias)


def reduce_parts(parts):
    shape = parts.shape[3:]
    got = swap(parts, "c").astype(F32)
    part = (got[0] + got[1]).astype(BF16)
    part = jnp.sum(swap(part, "y").astype(F32), axis=0).astype(BF16)
    part = jnp.sum(swap(part, "zh").astype(F32), axis=0)
    return part.reshape(shape)


def gather_parts(part):
    return gather(gather(gather(part, "zh"), "y"), "c")


def heads_first(rows):
    return rows.reshape(16, KV_HEADS, HEAD_DIM).transpose(1, 0, 2).reshape(KV_HEADS * 16, HEAD_DIM)


def heads_last(parts):
    return parts.reshape(KV_HEADS, 16, HEAD_DIM).transpose(1, 0, 2).reshape(16, KV_HEADS * HEAD_DIM)


def on_device(
    response_rows,
    prompt_rows,
    queries,
    response_keys,
    prompt_keys,
    cotangent,
    segment_index,
    prompt_choice,
    frozen_value_weight,
    value_adapter_down,
    value_adapter_up,
):
    segments = segment_index.reshape(TOKENS)
    onehot = (segments[:, None] == jnp.arange(8, dtype=jnp.int32)[None, :]).astype(jnp.int32)
    token_prompt = jnp.sum(onehot * prompt_choice.reshape(1, 8), axis=1)
    chosen = jnp.broadcast_to(jnp.tile(token_prompt, 2)[:, None], (PAIR, HEAD_DIM))
    position = jnp.arange(TOKENS, dtype=jnp.int32)
    own_seen = (segments[:, None] == segments[None, :]) & (position[:, None] <= position[None, :])
    bias = jnp.tile(jnp.where(own_seen, 0.0, -1e30).astype(F32), (1, 2))

    down_t = value_adapter_down.T
    key_part = jnp.concatenate([heads_first(prompt_keys), down_t], axis=0)
    key_all = gather_parts(key_part)
    own_columns = lax.dynamic_slice_in_dim(
        frozen_value_weight, lax.axis_index("x") * HEAD_DIM, HEAD_DIM, 1
    )
    weight = gather(gather(gather(gather(own_columns, "zh"), "x"), "y"), "c")
    weight = weight.transpose(1, 3, 0, 4, 2, 5).reshape(D, KV_HEADS * HEAD_DIM)
    prompt_columns = swap(prompt_rows.reshape(16, 32, 128).transpose(1, 0, 2), SAMPLE)

    send, low, back_t = attend_forward(
        queries, cotangent, key_all, response_keys, chosen, bias, response_rows, value_adapter_up
    )
    got = reduce_parts(send)
    prompt_low = heads_last(got[: KV_HEADS * 16].astype(BF16))
    first_sum = got[KV_HEADS * 16 :]

    down_full = key_all[:, :, :, KV_HEADS * 16 :].transpose(3, 1, 2, 0, 4).reshape(RANK, D)
    local_rows = jnp.concatenate([response_rows, prompt_rows], axis=0)
    first_proj = nt(local_rows, down_full).astype(BF16)
    value_low = jnp.concatenate([low, prompt_low], axis=0)
    prompt_back = nt(prompt_low, value_adapter_up).astype(BF16)
    back_low = jnp.concatenate([back_t.T, prompt_back], axis=0)

    second_part = tn(first_proj, value_low)
    packed = jnp.concatenate(
        [
            second_part.reshape(RANK, 32, 16).transpose(1, 0, 2),
            jnp.broadcast_to(prompt_back.astype(F32)[None], (32, 16, RANK)),
            jnp.zeros((32, 16, 96), F32),
        ],
        axis=2,
    )
    packed = swap(packed, SAMPLE)
    second_sum = jnp.sum(packed[:, :, :16], axis=0)
    first_sum = first_sum + tn(
        packed[:, :, 16:32].reshape(512, RANK).astype(BF16), prompt_columns.reshape(512, 128)
    )
    both = jnp.concatenate([first_sum, second_sum, jnp.zeros((RANK, 112), F32)], axis=1)
    both = jnp.sum(gather(both, GROUP), axis=0)
    factor = ADAPTER_SCALE * float(73728) ** (-0.5)
    first_grad = both[:, :128].T * factor
    second_grad = gather(both[:, 128:] * factor, SAMPLE)[:, :, :16]
    second_grad = second_grad.transpose(1, 0, 2).reshape(RANK, KV_HEADS * HEAD_DIM)

    values = (nn(local_rows, weight) + ADAPTER_SCALE * nn(first_proj, value_adapter_up)).astype(BF16)
    value_all = gather_parts(heads_first(values[TOKENS:]))
    key_send, own_key_grad = attend_backward(
        queries, cotangent, key_all, value_all, response_keys, values[:TOKENS], chosen, bias
    )
    prompt_key_grad = heads_last(reduce_parts(key_send).astype(BF16))
    grads = (nt(value_low, weight) + ADAPTER_SCALE * nn(back_low, down_full)).astype(BF16)
    return (
        grads[:TOKENS],
        grads[TOKENS:],
        own_key_grad,
        prompt_key_grad,
        first_grad,
        second_grad,
    )


def solution(mesh):
    fine = Mesh(np.asarray(mesh.devices).reshape(4, 4, 4, 4, 2), AXES)
    rows = P(AXES, None)
    in_specs = (rows,) * 8 + (P(SAMPLE, None), P(SAMPLE, None), P())
    out_specs = (rows,) * 4 + (P(SAMPLE, None), P())
    return jax.shard_map(
        on_device, mesh=fine, in_specs=in_specs, out_specs=out_specs, check_vma=False
    )
```

```python
import jax
import jax.numpy as jnp
import numpy as np
from jax import lax
from jax.experimental import pallas as pl
from jax.experimental.pallas import tpu as pltpu
from jax.sharding import Mesh, PartitionSpec as P

HEADS = 32
KV_HEADS = 4
HEAD_DIM = 128
GROUP_SIZE = HEADS // KV_HEADS
PROMPT_LEN = 128
PROMPTS = 4
RANK = 16
TOKENS = 128
D = 4096
SCALE = HEAD_DIM**-0.5
ADAPTER_SCALE = 2.0
AXES = ("x", "zl", "y", "zh", "c")
SAMPLE = ("y", "zh", "c")
GROUP = ("x", "zl")
PAIR = 2 * TOKENS
F32 = jnp.float32
BF16 = jnp.bfloat16


def swap(array, axis):
    return lax.all_to_all(array, axis, 0, 0, tiled=True)


def gather(array, axis):
    n = lax.axis_size(axis)
    return swap(jnp.broadcast_to(array[None], (n,) + array.shape), axis)


def nt(left, right):
    return lax.dot_general(left, right, (((1,), (1,)), ((), ())), preferred_element_type=F32)


def tn(left, right):
    return lax.dot_general(left, right, (((0,), (0,)), ((), ())), preferred_element_type=F32)


def nn(left, right):
    return jnp.dot(left, right, preferred_element_type=F32)


def expand(rows, chosen):
    zero = jnp.zeros_like(rows)
    return jnp.concatenate([jnp.where(chosen == p, rows, zero) for p in range(PROMPTS)], axis=1)


def pair_rows(ref, pair):
    first = 2 * pair * HEAD_DIM
    return jnp.concatenate(
        [ref[:, first : first + HEAD_DIM], ref[:, first + HEAD_DIM : first + 2 * HEAD_DIM]], axis=0
    )


def prompt_block(ref):
    return jnp.concatenate(
        [
            jnp.concatenate([ref[c, p, zh] for zh in range(4) for c in range(2)], axis=0)
            for p in range(PROMPTS)
        ],
        axis=1,
    )


def value_block(ref, k):
    def part(c, p, zh):
        return ref[c, pl.ds(pl.multiple_of((p * 4 + zh) * 64 + k * 16, 16), 16), :]

    return jnp.concatenate(
        [
            jnp.concatenate([part(c, p, zh) for zh in range(4) for c in range(2)], axis=0)
            for p in range(PROMPTS)
        ],
        axis=1,
    )


def spread(ref, row, block):
    for p in range(PROMPTS):
        for zh in range(4):
            for c in range(2):
                s = (zh * 2 + c) * 16
                ref[c, p, zh, pl.ds(row, 16), :] = block[
                    s : s + 16, p * HEAD_DIM : (p + 1) * HEAD_DIM
                ].astype(ref.dtype)


def softmax_pair(key_cat, own_key, expanded, rows, bias):
    seen = nt(key_cat, expanded) * SCALE
    own = nt(own_key, rows) * SCALE + bias
    top = jnp.maximum(jnp.max(seen, axis=0, keepdims=True), jnp.max(own, axis=0, keepdims=True))
    seen, own = jnp.exp(seen - top), jnp.exp(own - top)
    total = jnp.sum(seen, axis=0, keepdims=True) + jnp.sum(own, axis=0, keepdims=True)
    return seen / total, own / total


BLOCKS = [
    (((y * 4 + zh) * 2 + c) * 128, y, zh, c) for y in range(4) for zh in range(4) for c in range(2)
]


def forward_kernel(
    q_ref, cot_ref, key_ref, down_ref, own_key_ref, chosen_ref, bias_ref, x_ref, prompt_ref, up_ref,
    send_ref, low_ref, back_ref, first_ref, down_out_ref,
    probs, own_probs, cots, back,
):
    k = pl.program_id(0)
    key_cat = prompt_block(key_ref)
    own_key = own_key_ref[...]
    chosen = chosen_ref[...]
    bias = bias_ref[...]
    for pair in range(GROUP_SIZE // 2):
        rows = pair_rows(q_ref, pair)
        seen, own = softmax_pair(key_cat, own_key, expand(rows, chosen), rows, bias)
        at = pl.ds(pair * PAIR, PAIR)
        probs[:, at] = seen.astype(BF16)
        own_probs[:, at] = own.astype(BF16)
        cot = pair_rows(cot_ref, pair)
        cots[at, : PROMPTS * HEAD_DIM] = expand(cot, chosen)
        cots[at, PROMPTS * HEAD_DIM :] = cot
    spread(send_ref, pl.multiple_of(k * 16, 16), nn(probs[...], cots[:, : PROMPTS * HEAD_DIM]))
    low = nn(own_probs[...], cots[:, PROMPTS * HEAD_DIM :]).astype(BF16)
    low_ref[...] = low

    @pl.when(k == 0)
    def _():
        back[...] = jnp.zeros_like(back)
        for at, y, zh, c in BLOCKS:
            down_out_ref[:, at : at + 128] = down_ref[c, y, zh]
        down = down_out_ref[...]
        first_ref[:TOKENS, :] = nt(x_ref[...], down).astype(BF16)
        first_ref[TOKENS:, :] = nt(prompt_ref[...], down).astype(BF16)

    back[...] += nt(up_ref[...], low)

    @pl.when(k == KV_HEADS - 1)
    def _():
        back_ref[...] = back[...].astype(BF16)


def adapter_kernel(
    low_ref, back_ref, got_ref, first_ref, up_ref, x_ref, prompt_ref,
    prompt_low_ref, prompt_back_ref, send_ref,
):
    got = got_ref[...].astype(F32)
    total = ((got[0] + got[1]) + (got[2] + got[3])).astype(BF16)
    up = up_ref[...]
    first = first_ref[...]
    prompt_back = jnp.zeros((RANK, 16), F32)
    for k in range(KV_HEADS):
        at = slice(k * HEAD_DIM, (k + 1) * HEAD_DIM)
        low = total[k * 16 : (k + 1) * 16]
        prompt_low_ref[:, at] = low
        prompt_back = prompt_back + nt(up[:, at], low)
        second = (tn(first[:TOKENS], low_ref[:, at]) + tn(first[TOKENS:], low)).astype(BF16)
        for zh in range(4):
            send_ref[zh, 128 + k * 16 : 128 + (k + 1) * 16, :] = second
    prompt_back = prompt_back.astype(BF16)
    prompt_back_ref[...] = prompt_back
    grad = (nn(back_ref[...], x_ref[...]) + nn(prompt_back, prompt_ref[...])).astype(BF16)
    for at, y, zh, c in BLOCKS:
        row = (y * 2 + c) * 16
        send_ref[zh, row : row + 16, :] = grad[:, at : at + 128]


def project_kernel(
    x_ref, prompt_ref, weight_ref, first_ref, up_ref, adapter_ref,
    values_ref, send_ref, weight_out_ref,
    rows,
):
    k = pl.program_id(0)

    @pl.when(k == 0)
    def _():
        rows[:TOKENS, :] = x_ref[...]
        rows[TOKENS:, :] = prompt_ref[...]
        send_ref[:, KV_HEADS * 16 :, :] = adapter_ref[...]

    for at, y, zh, c in BLOCKS:
        weight_out_ref[at : at + 128, :] = weight_ref[0, y, c, zh]
    values = nn(rows[...], weight_out_ref[...]) + ADAPTER_SCALE * nn(first_ref[...], up_ref[...])
    values = values.astype(BF16)
    values_ref[...] = values[:TOKENS]
    for zh in range(4):
        send_ref[zh, pl.ds(pl.multiple_of(k * 16, 16), 16), :] = values[TOKENS:]


def total_of(parts):
    parts = parts.astype(F32)
    total = parts[0]
    for i in range(1, parts.shape[0]):
        total = total + parts[i]
    return total


def after_zh_kernel(got_ref, send_ref):
    second = total_of(got_ref[:, 192:, :]).astype(BF16)
    for y in range(4):
        for zh in range(4):
            send_ref[y, zh * 64 : (zh + 1) * 64, :] = got_ref[zh, :64, :]
        first = total_of(got_ref[:, 64 + y * 32 : 64 + (y + 1) * 32, :])
        send_ref[y, 256:288, :] = first.astype(BF16)
        send_ref[y, 288:, :] = second


def after_y_kernel(got_ref, send_ref):
    second = total_of(got_ref[:, 288:, :]).astype(BF16)
    for c in range(2):
        for y in range(4):
            send_ref[c, y * 256 : (y + 1) * 256, :] = got_ref[y, :256, :]
        first = total_of(got_ref[:, 256 + c * 16 : 256 + (c + 1) * 16, :])
        send_ref[c, 1024:1040, :] = first.astype(BF16)
        send_ref[c, 1040:, :] = second


def in_vmem(kernel, shape, name):
    return pl.pallas_call(
        kernel,
        in_specs=[pl.BlockSpec(memory_space=pltpu.VMEM)],
        out_specs=pl.BlockSpec(memory_space=pltpu.VMEM),
        out_shape=jax.ShapeDtypeStruct(shape, BF16),
        compiler_params=pltpu.CompilerParams(vmem_limit_bytes=16 << 20),
        name=name,
    )


def backward_kernel(
    q_ref, cot_ref, key_ref, value_ref, own_key_ref, own_value_ref, chosen_ref, bias_ref,
    send_ref, own_ref,
    grads, own_grads, queries,
):
    k = pl.program_id(0)
    key_cat, value_cat = prompt_block(key_ref), value_block(value_ref, k)
    own_key, own_value = own_key_ref[...], own_value_ref[...]
    chosen = chosen_ref[...]
    bias = bias_ref[...]
    for pair in range(GROUP_SIZE // 2):
        rows = pair_rows(q_ref, pair)
        expanded = expand(rows, chosen)
        at = pl.ds(pair * PAIR, PAIR)
        queries[at, : PROMPTS * HEAD_DIM] = expanded
        queries[at, PROMPTS * HEAD_DIM :] = rows
        seen, own = softmax_pair(key_cat, own_key, expanded, rows, bias)
        cot = pair_rows(cot_ref, pair)
        seen_grad = nt(value_cat, expand(cot, chosen))
        own_grad = nt(own_value, cot)
        delta = jnp.sum(seen.astype(BF16).astype(F32) * seen_grad, axis=0, keepdims=True) + jnp.sum(
            own.astype(BF16).astype(F32) * own_grad, axis=0, keepdims=True
        )
        grads[:, at] = (seen * (seen_grad - delta)).astype(BF16)
        own_grads[:, at] = (own * (own_grad - delta)).astype(BF16)
    spread(
        send_ref,
        pl.multiple_of(k * 16, 16),
        nn(grads[...], queries[:, : PROMPTS * HEAD_DIM]) * SCALE,
    )
    own_ref[...] = (nn(own_grads[...], queries[:, PROMPTS * HEAD_DIM :]) * SCALE).astype(BF16)


def whole(shape):
    return pl.BlockSpec(shape, lambda k: (0,) * len(shape))


def heads_of(rows, width):
    return pl.BlockSpec((rows, width), lambda k: (0, k))


PROMPT_SPEC = pl.BlockSpec((2, 4, 4, 16, HEAD_DIM), lambda k: (0, 0, 0, k, 0))
WIDE = GROUP_SIZE * HEAD_DIM
ROWS = GROUP_SIZE * TOKENS


DOWN_SPEC = pl.BlockSpec((2, 4, 4, 16, HEAD_DIM), lambda k: (0, 0, 0, KV_HEADS, 0))
PARAMS = pltpu.CompilerParams(vmem_limit_bytes=40 << 20, dimension_semantics=("arbitrary",))


def attend_forward(queries, cotangent, keys, own_keys, chosen, bias, rows, prompt_rows, up):
    return pl.pallas_call(
        forward_kernel,
        grid=(KV_HEADS,),
        in_specs=[
            heads_of(TOKENS, WIDE),
            heads_of(TOKENS, WIDE),
            PROMPT_SPEC,
            DOWN_SPEC,
            heads_of(TOKENS, HEAD_DIM),
            whole((PAIR, HEAD_DIM)),
            whole((TOKENS, PAIR)),
            whole((TOKENS, D)),
            whole((16, D)),
            heads_of(RANK, HEAD_DIM),
        ],
        out_specs=[
            whole((2, 4, 4, KV_HEADS * 16, HEAD_DIM)),
            heads_of(TOKENS, HEAD_DIM),
            whole((RANK, TOKENS)),
            whole((TOKENS + 16, RANK)),
            whole((RANK, D)),
        ],
        out_shape=[
            jax.ShapeDtypeStruct((2, 4, 4, KV_HEADS * 16, HEAD_DIM), BF16),
            jax.ShapeDtypeStruct((TOKENS, KV_HEADS * HEAD_DIM), BF16),
            jax.ShapeDtypeStruct((RANK, TOKENS), BF16),
            jax.ShapeDtypeStruct((TOKENS + 16, RANK), BF16),
            jax.ShapeDtypeStruct((RANK, D), BF16),
        ],
        scratch_shapes=[
            pltpu.VMEM((TOKENS, ROWS), BF16),
            pltpu.VMEM((TOKENS, ROWS), BF16),
            pltpu.VMEM((ROWS, (PROMPTS + 1) * HEAD_DIM), BF16),
            pltpu.VMEM((RANK, TOKENS), F32),
        ],
        compiler_params=PARAMS,
        cost_estimate=pl.CostEstimate(
            flops=2_000_000_000, bytes_accessed=5 << 20, transcendentals=1 << 20
        ),
        name="attend_forward",
    )(queries, cotangent, keys, keys, own_keys, chosen, bias, rows, prompt_rows, up)


def adapter_terms(low, back, got, first, up, rows, prompt_rows):
    return pl.pallas_call(
        adapter_kernel,
        in_specs=[pl.BlockSpec(memory_space=pltpu.VMEM)] * 7,
        out_specs=[pl.BlockSpec(memory_space=pltpu.VMEM)] * 3,
        out_shape=[
            jax.ShapeDtypeStruct((16, KV_HEADS * HEAD_DIM), BF16),
            jax.ShapeDtypeStruct((RANK, 16), BF16),
            jax.ShapeDtypeStruct((4, 128 + KV_HEADS * 16, HEAD_DIM), BF16),
        ],
        compiler_params=pltpu.CompilerParams(vmem_limit_bytes=16 << 20),
        name="adapter_terms",
    )(low, back, got, first, up, rows, prompt_rows)


def project(rows, prompt_rows, weight, first, up, adapter):
    width = KV_HEADS * HEAD_DIM
    return pl.pallas_call(
        project_kernel,
        grid=(KV_HEADS,),
        in_specs=[
            whole((TOKENS, D)),
            whole((16, D)),
            pl.BlockSpec((1, 4, 2, 4, 128, HEAD_DIM), lambda k: (k, 0, 0, 0, 0, 0)),
            whole((TOKENS + 16, RANK)),
            heads_of(RANK, HEAD_DIM),
            whole((4, 192, HEAD_DIM)),
        ],
        out_specs=[
            heads_of(TOKENS, HEAD_DIM),
            whole((4, 256, HEAD_DIM)),
            heads_of(D, HEAD_DIM),
        ],
        out_shape=[
            jax.ShapeDtypeStruct((TOKENS, width), BF16),
            jax.ShapeDtypeStruct((4, 256, HEAD_DIM), BF16),
            jax.ShapeDtypeStruct((D, width), BF16),
        ],
        scratch_shapes=[pltpu.VMEM((TOKENS + 16, D), BF16)],
        compiler_params=PARAMS,
        cost_estimate=pl.CostEstimate(
            flops=600_000_000, bytes_accessed=10 << 20, transcendentals=0
        ),
        name="project",
    )(rows, prompt_rows, weight, first, up, adapter)


def attend_backward(queries, cotangent, keys, values, own_keys, own_values, chosen, bias):
    return pl.pallas_call(
        backward_kernel,
        grid=(KV_HEADS,),
        in_specs=[
            heads_of(TOKENS, WIDE),
            heads_of(TOKENS, WIDE),
            PROMPT_SPEC,
            whole((2, 1104, HEAD_DIM)),
            heads_of(TOKENS, HEAD_DIM),
            heads_of(TOKENS, HEAD_DIM),
            whole((PAIR, HEAD_DIM)),
            whole((TOKENS, PAIR)),
        ],
        out_specs=[
            whole((2, 4, 4, KV_HEADS * 16, HEAD_DIM)),
            heads_of(TOKENS, HEAD_DIM),
        ],
        out_shape=[
            jax.ShapeDtypeStruct((2, 4, 4, KV_HEADS * 16, HEAD_DIM), BF16),
            jax.ShapeDtypeStruct((TOKENS, KV_HEADS * HEAD_DIM), BF16),
        ],
        scratch_shapes=[
            pltpu.VMEM((TOKENS, ROWS), BF16),
            pltpu.VMEM((TOKENS, ROWS), BF16),
            pltpu.VMEM((ROWS, (PROMPTS + 1) * HEAD_DIM), BF16),
        ],
        compiler_params=pltpu.CompilerParams(
            vmem_limit_bytes=40 << 20, dimension_semantics=("arbitrary",)
        ),
        cost_estimate=pl.CostEstimate(
            flops=3_000_000_000, bytes_accessed=5 << 20, transcendentals=1 << 20
        ),
        name="attend_backward",
    )(queries, cotangent, keys, values, own_keys, own_values, chosen, bias)


def sum_first(parts):
    return jnp.sum(parts.astype(F32), axis=0)


def reduce_to_zh(parts):
    part = sum_first(swap(parts, "c")).astype(BF16)
    part = sum_first(swap(part, "y")).astype(BF16)
    return swap(part, "zh")


def heads_first(rows):
    return rows.reshape(16, KV_HEADS, HEAD_DIM).transpose(1, 0, 2).reshape(KV_HEADS * 16, HEAD_DIM)


def heads_last(parts):
    return parts.reshape(KV_HEADS, 16, HEAD_DIM).transpose(1, 0, 2).reshape(16, KV_HEADS * HEAD_DIM)


def sum_ring(part, axis):
    total = part
    for step in range(1, 4):
        total = total + lax.ppermute(part, axis, [(i, (i + step) % 4) for i in range(4)])
    return total


def on_device(
    response_rows,
    prompt_rows,
    queries,
    response_keys,
    prompt_keys,
    cotangent,
    segment_index,
    prompt_choice,
    frozen_value_weight,
    value_adapter_down,
    value_adapter_up,
):
    segments = segment_index.reshape(TOKENS)
    onehot = (segments[:, None] == jnp.arange(8, dtype=jnp.int32)[None, :]).astype(jnp.int32)
    token_prompt = jnp.sum(onehot * prompt_choice.reshape(1, 8), axis=1)
    chosen = jnp.broadcast_to(jnp.tile(token_prompt, 2)[:, None], (PAIR, HEAD_DIM))
    position = jnp.arange(TOKENS, dtype=jnp.int32)
    own_seen = (segments[:, None] == segments[None, :]) & (position[:, None] <= position[None, :])
    bias = jnp.tile(jnp.where(own_seen, 0.0, -1e30).astype(F32), (1, 2))

    own_columns = lax.dynamic_slice_in_dim(
        frozen_value_weight, lax.axis_index("x") * HEAD_DIM, HEAD_DIM, 1
    )
    start = gather(
        jnp.concatenate([own_columns, heads_first(prompt_keys), value_adapter_down.T], axis=0), "zh"
    )
    weight = lax.all_gather(start[:, :128], ("x", "y", "c"))
    weight = weight.reshape(4, 4, 2, 4, 128, HEAD_DIM)
    key_all = gather(gather(start[:, 128:], "y"), "c")

    send, low, back, first_proj, down = attend_forward(
        queries, cotangent, key_all, response_keys, chosen, bias, response_rows, prompt_rows,
        value_adapter_up,
    )
    prompt_low, prompt_back, adapter = adapter_terms(
        low, back, reduce_to_zh(send), first_proj, value_adapter_up, response_rows, prompt_rows
    )
    values, part, weight = project(
        response_rows, prompt_rows, weight, first_proj, value_adapter_up, adapter
    )
    part = in_vmem(after_zh_kernel, (4, 352, HEAD_DIM), "after_zh")(swap(part, "zh"))
    part = in_vmem(after_y_kernel, (2, 1104, HEAD_DIM), "after_y")(swap(part, "y"))
    part = swap(part, "c")
    key_send, own_key_grad = attend_backward(
        queries, cotangent, key_all, part, response_keys, values, chosen, bias
    )
    prompt_key_grad = heads_last(sum_first(reduce_to_zh(key_send)).astype(BF16))

    factor = ADAPTER_SCALE * float(73728) ** (-0.5)
    both = sum_ring(sum_ring(sum_first(part[:, 1024:]), "x"), "zl") * factor
    first_grad = both[:16].T
    second_grad = heads_last(both[16:])

    response_grad = nt(low, weight) + ADAPTER_SCALE * tn(back, down)
    prompt_grad = nt(prompt_low, weight) + ADAPTER_SCALE * tn(prompt_back, down)
    return (
        response_grad.astype(BF16),
        prompt_grad.astype(BF16),
        own_key_grad,
        prompt_key_grad,
        first_grad,
        second_grad,
    )


def solution(mesh):
    fine = Mesh(np.asarray(mesh.devices).reshape(4, 4, 4, 4, 2), AXES)
    rows = P(AXES, None)
    in_specs = (rows,) * 8 + (P(SAMPLE, None), P(SAMPLE, None), P())
    out_specs = (rows,) * 4 + (P(SAMPLE, None), P())
    return jax.shard_map(
        on_device, mesh=fine, in_specs=in_specs, out_specs=out_specs, check_vma=False
    )
```

```python
import jax
import jax.numpy as jnp
import numpy as np
from jax import lax
from jax.experimental import pallas as pl
from jax.experimental.pallas import tpu as pltpu
from jax.sharding import Mesh, PartitionSpec as P

HEADS = 32
KV_HEADS = 4
HEAD_DIM = 128
GROUP_SIZE = HEADS // KV_HEADS
PROMPT_LEN = 128
PROMPTS = 4
RANK = 16
TOKENS = 128
D = 4096
SCALE = HEAD_DIM**-0.5
ADAPTER_SCALE = 2.0
FACTOR = ADAPTER_SCALE * float(73728) ** (-0.5)
AXES = ("x", "zl", "y", "zh", "c")
SAMPLE = ("y", "zh", "c")
GROUP = ("x", "zl")
OWNERS = ("y", "c")
PAIR = 2 * TOKENS
F32 = jnp.float32
BF16 = jnp.bfloat16


def swap(array, axis):
    return lax.all_to_all(array, axis, 0, 0, tiled=True)


def gather(array, axis):
    n = lax.axis_size(axis)
    return swap(jnp.broadcast_to(array[None], (n,) + array.shape), axis)


def nt(left, right):
    return lax.dot_general(left, right, (((1,), (1,)), ((), ())), preferred_element_type=F32)


def tn(left, right):
    return lax.dot_general(left, right, (((0,), (0,)), ((), ())), preferred_element_type=F32)


def nn(left, right):
    return jnp.dot(left, right, preferred_element_type=F32)


def expand(rows, chosen):
    zero = jnp.zeros_like(rows)
    return jnp.concatenate([jnp.where(chosen == p, rows, zero) for p in range(PROMPTS)], axis=1)


def pair_rows(ref, pair):
    first = 2 * pair * HEAD_DIM
    return jnp.concatenate(
        [ref[:, first : first + HEAD_DIM], ref[:, first + HEAD_DIM : first + 2 * HEAD_DIM]], axis=0
    )


def prompt_block(ref):
    return jnp.concatenate(
        [
            jnp.concatenate([ref[p, c, zh] for zh in range(4) for c in range(2)], axis=0)
            for p in range(PROMPTS)
        ],
        axis=1,
    )


def value_block(ref, k):
    def part(c, p, zh):
        return ref[p * 2 + c, pl.ds(pl.multiple_of(zh * 64 + k * 16, 16), 16), :]

    return jnp.concatenate(
        [
            jnp.concatenate([part(c, p, zh) for zh in range(4) for c in range(2)], axis=0)
            for p in range(PROMPTS)
        ],
        axis=1,
    )


def spread(ref, k, block):
    for p in range(PROMPTS):
        for zh in range(4):
            for c in range(2):
                s = (zh * 2 + c) * 16
                row = pl.multiple_of(zh * 64 + k * 16, 16)
                ref[p * 2 + c, pl.ds(row, 16), :] = block[
                    s : s + 16, p * HEAD_DIM : (p + 1) * HEAD_DIM
                ].astype(ref.dtype)


def softmax_pair(key_cat, own_key, expanded, rows, bias):
    seen = nt(key_cat, expanded) * SCALE
    own = nt(own_key, rows) * SCALE + bias
    top = jnp.maximum(jnp.max(seen, axis=0, keepdims=True), jnp.max(own, axis=0, keepdims=True))
    seen, own = jnp.exp(seen - top), jnp.exp(own - top)
    total = jnp.sum(seen, axis=0, keepdims=True) + jnp.sum(own, axis=0, keepdims=True)
    return seen / total, own / total


BLOCKS = [
    (((y * 4 + zh) * 2 + c) * 128, y, zh, c) for y in range(4) for zh in range(4) for c in range(2)
]


def forward_kernel(
    q_ref, cot_ref, key_ref, down_ref, own_key_ref, chosen_ref, bias_ref, x_ref, up_ref,
    send_ref, low_ref, back_ref, first_ref, down_out_ref, softmax_ref,
    probs, own_probs, cots, back,
):
    k = pl.program_id(0)
    key_cat = prompt_block(key_ref)
    own_key = own_key_ref[...]
    chosen = chosen_ref[...]
    bias = bias_ref[...]
    for pair in range(GROUP_SIZE // 2):
        rows = pair_rows(q_ref, pair)
        seen, own = softmax_pair(key_cat, own_key, expand(rows, chosen), rows, bias)
        at = pl.ds(pair * PAIR, PAIR)
        softmax_ref[0, :TOKENS, at] = seen
        softmax_ref[0, TOKENS:, at] = own
        probs[:, at] = seen.astype(BF16)
        own_probs[:, at] = own.astype(BF16)
        cot = pair_rows(cot_ref, pair)
        cots[at, : PROMPTS * HEAD_DIM] = expand(cot, chosen)
        cots[at, PROMPTS * HEAD_DIM :] = cot
    spread(send_ref, k, nn(probs[...], cots[:, : PROMPTS * HEAD_DIM]))
    low = nn(own_probs[...], cots[:, PROMPTS * HEAD_DIM :]).astype(BF16)
    low_ref[...] = low

    @pl.when(k == 0)
    def _():
        back[...] = jnp.zeros_like(back)
        for at, y, zh, c in BLOCKS:
            down_out_ref[:, at : at + 128] = down_ref[y, c, zh]
        first_ref[...] = nt(x_ref[...], down_out_ref[...]).astype(BF16)

    back[...] += nt(up_ref[...], low)

    @pl.when(k == KV_HEADS - 1)
    def _():
        back_ref[...] = back[...].astype(BF16)


def place_before(place, step):
    return lax.rem(place + (4 - step), 4)


def adapter_kernel(
    place_ref, low_ref, back_ref, got_ref, first_ref, up_ref, down_ref, x_ref,
    prompt_ref, prompt1_ref, prompt2_ref, prompt3_ref,
    part_ref, send_ref,
    total,
):
    total[...] = total_of(got_ref[...]).astype(BF16)
    for zh in range(4):
        part_ref[zh] = total[zh * 64 : (zh + 1) * 64, :]
    up = up_ref[...]
    first = first_ref[...]
    prompts = jnp.concatenate(
        [prompt_ref[...], prompt1_ref[...], prompt2_ref[...], prompt3_ref[...]], axis=0
    )
    prompt_first = nt(prompts, down_ref[...]).astype(BF16)
    prompt_back = jnp.zeros((RANK, 64), F32)
    for k in range(KV_HEADS):
        at = slice(k * HEAD_DIM, (k + 1) * HEAD_DIM)
        starts = [place_before(place_ref[2], step) * 64 + k * 16 for step in range(4)]
        low = jnp.concatenate(
            [total[pl.ds(pl.multiple_of(row, 16), 16), :] for row in starts], axis=0
        )
        prompt_back = prompt_back + nt(up[:, at], low)
        second = tn(first, low_ref[:, at]) + tn(prompt_first, low)
        send_ref[512 + k * 16 : 512 + (k + 1) * 16, :] = second.astype(BF16)
    grad = nn(back_ref[...], x_ref[...]) + nn(prompt_back.astype(BF16), prompts)
    grad = grad.astype(BF16)
    for at, y, zh, c in BLOCKS:
        row = ((y * 2 + c) * 4 + zh) * 16
        send_ref[row : row + 16, :] = grad[:, at : at + 128]


def project_kernel(
    place_ref, x_ref, prompt_ref, prompt1_ref, prompt2_ref, prompt3_ref,
    weight_ref, other_ref, down_ref, up_ref,
    values_ref, send_ref, weight_out_ref,
    rows, first,
):
    k = pl.program_id(0)

    @pl.when(k == 0)
    def _():
        rows[:TOKENS, :] = x_ref[...]
        for step, ref in enumerate((prompt_ref, prompt1_ref, prompt2_ref, prompt3_ref)):
            rows[TOKENS + step * 16 : TOKENS + (step + 1) * 16, :] = ref[...]
        first[...] = nt(rows[...], down_ref[...]).astype(BF16)

    for y in range(4):
        for zh in range(4):
            for ref, c in ((weight_ref, place_ref[3]), (other_ref, 1 - place_ref[3])):
                row = pl.multiple_of(((y * 4 + zh) * 2 + c) * 128, 128)
                weight_out_ref[pl.ds(row, 128), :] = ref[0, y, zh]
    values = nn(rows[...], weight_out_ref[...]) + ADAPTER_SCALE * nn(first[...], up_ref[...])
    values = values.astype(BF16)
    values_ref[...] = values[:TOKENS]
    for step in range(4):
        row = place_before(place_ref[2], step) * 64 + k * 16
        part = values[TOKENS + step * 16 : TOKENS + (step + 1) * 16]
        for owner in range(8):
            send_ref[owner, pl.ds(pl.multiple_of(row, 16), 16), :] = part


def total_of(parts):
    parts = parts.astype(F32)
    total = parts[0]
    for i in range(1, parts.shape[0]):
        total = total + parts[i]
    return total


def keys_y_kernel(got_ref, value_ref, send_ref):
    second = total_of(got_ref[:, 320:, :]).astype(BF16)
    for zh in range(4):
        send_ref[zh, :64, :] = total_of(got_ref[:, zh * 64 : (zh + 1) * 64, :]).astype(BF16)
        send_ref[zh, 64:128, :] = value_ref[zh]
        at = 256 + zh * 16
        send_ref[zh, 128:144, :] = total_of(got_ref[:, at : at + 16, :]).astype(BF16)
        send_ref[zh, 144:, :] = second


def keys_zh_kernel(got_ref, key_ref, low_ref, send_ref):
    total = total_of(got_ref[...])
    for k in range(KV_HEADS):
        at = slice(k * HEAD_DIM, (k + 1) * HEAD_DIM)
        key_ref[:, at] = total[k * 16 : (k + 1) * 16].astype(BF16)
        low_ref[:, at] = total[64 + k * 16 : 64 + (k + 1) * 16].astype(BF16)
    terms = total[128:].astype(BF16)
    for g in range(16):
        send_ref[g] = terms


def group_kernel(got_ref, first_ref, second_ref):
    total = total_of(got_ref[...]) * FACTOR
    first_ref[...] = total[:16]
    for k in range(KV_HEADS):
        second_ref[:, k * HEAD_DIM : (k + 1) * HEAD_DIM] = total[16 + k * 16 : 16 + (k + 1) * 16]


def prompt_kernel(low_ref, up_ref, down_ref, weight_ref, grad_ref, back):
    @pl.when(pl.program_id(0) == 0)
    def _():
        back[...] = nt(low_ref[...], up_ref[...]).astype(BF16)

    grad = nt(low_ref[...], weight_ref[...]) + ADAPTER_SCALE * nn(back[...], down_ref[...])
    grad_ref[...] = grad.astype(BF16)


def in_vmem(kernel, n, shapes, name):
    return pl.pallas_call(
        kernel,
        in_specs=[pl.BlockSpec(memory_space=pltpu.VMEM)] * n,
        out_specs=jax.tree.map(lambda _: pl.BlockSpec(memory_space=pltpu.VMEM), shapes),
        out_shape=shapes,
        compiler_params=pltpu.CompilerParams(vmem_limit_bytes=16 << 20),
        name=name,
    )


def sent(*shape):
    return jax.ShapeDtypeStruct(shape, BF16)


def backward_kernel(
    q_ref, cot_ref, softmax_ref, value_ref, own_value_ref, chosen_ref, adapter_ref,
    send_ref, own_ref,
    grads, own_grads, queries,
):
    k = pl.program_id(0)

    @pl.when(k == 0)
    def _():
        for owner in range(8):
            send_ref[owner, 256:320, :] = adapter_ref[owner * 64 : (owner + 1) * 64, :]
            send_ref[owner, 320:, :] = adapter_ref[512:, :]

    value_cat = value_block(value_ref, k)
    own_value = own_value_ref[...]
    chosen = chosen_ref[...]
    for pair in range(GROUP_SIZE // 2):
        rows = pair_rows(q_ref, pair)
        at = pl.ds(pair * PAIR, PAIR)
        queries[at, : PROMPTS * HEAD_DIM] = expand(rows, chosen)
        queries[at, PROMPTS * HEAD_DIM :] = rows
        seen = softmax_ref[0, :TOKENS, at]
        own = softmax_ref[0, TOKENS:, at]
        cot = pair_rows(cot_ref, pair)
        seen_grad = nt(value_cat, expand(cot, chosen))
        own_grad = nt(own_value, cot)
        delta = jnp.sum(seen.astype(BF16).astype(F32) * seen_grad, axis=0, keepdims=True) + jnp.sum(
            own.astype(BF16).astype(F32) * own_grad, axis=0, keepdims=True
        )
        grads[:, at] = (seen * (seen_grad - delta)).astype(BF16)
        own_grads[:, at] = (own * (own_grad - delta)).astype(BF16)
    spread(send_ref, k, nn(grads[...], queries[:, : PROMPTS * HEAD_DIM]) * SCALE)
    own_ref[...] = (nn(own_grads[...], queries[:, PROMPTS * HEAD_DIM :]) * SCALE).astype(BF16)


def whole(shape):
    return pl.BlockSpec(shape, lambda k: (0,) * len(shape))


def heads_of(rows, width):
    return pl.BlockSpec((rows, width), lambda k: (0, k))


PROMPT_SPEC = pl.BlockSpec((4, 2, 4, 16, HEAD_DIM), lambda k: (0, 0, 0, k, 0))
WIDE = GROUP_SIZE * HEAD_DIM
ROWS = GROUP_SIZE * TOKENS


DOWN_SPEC = pl.BlockSpec((4, 2, 4, 16, HEAD_DIM), lambda k: (0, 0, 0, KV_HEADS, 0))
PARAMS = pltpu.CompilerParams(vmem_limit_bytes=56 << 20, dimension_semantics=("arbitrary",))


def attend_forward(queries, cotangent, keys, own_keys, chosen, bias, rows, up):
    return pl.pallas_call(
        forward_kernel,
        grid=(KV_HEADS,),
        in_specs=[
            heads_of(TOKENS, WIDE),
            heads_of(TOKENS, WIDE),
            PROMPT_SPEC,
            DOWN_SPEC,
            heads_of(TOKENS, HEAD_DIM),
            whole((PAIR, HEAD_DIM)),
            whole((TOKENS, PAIR)),
            whole((TOKENS, D)),
            heads_of(RANK, HEAD_DIM),
        ],
        out_specs=[
            whole((8, 256, HEAD_DIM)),
            heads_of(TOKENS, HEAD_DIM),
            whole((RANK, TOKENS)),
            whole((TOKENS, RANK)),
            whole((RANK, D)),
            pl.BlockSpec((1, 2 * TOKENS, ROWS), lambda k: (k, 0, 0)),
        ],
        out_shape=[
            sent(8, 256, HEAD_DIM),
            sent(TOKENS, KV_HEADS * HEAD_DIM),
            sent(RANK, TOKENS),
            sent(TOKENS, RANK),
            sent(RANK, D),
            jax.ShapeDtypeStruct((KV_HEADS, 2 * TOKENS, ROWS), F32),
        ],
        scratch_shapes=[
            pltpu.VMEM((TOKENS, ROWS), BF16),
            pltpu.VMEM((TOKENS, ROWS), BF16),
            pltpu.VMEM((ROWS, (PROMPTS + 1) * HEAD_DIM), BF16),
            pltpu.VMEM((RANK, TOKENS), F32),
        ],
        compiler_params=PARAMS,
        cost_estimate=pl.CostEstimate(
            flops=2_000_000_000, bytes_accessed=5 << 20, transcendentals=1 << 20
        ),
        name="attend_forward",
    )(queries, cotangent, keys, keys, own_keys, chosen, bias, rows, up)


def adapter_terms(place, low, back, got, first, up, down, rows, prompts):
    vmem = pl.BlockSpec(memory_space=pltpu.VMEM)
    return pl.pallas_call(
        adapter_kernel,
        in_specs=[pl.BlockSpec(memory_space=pltpu.SMEM)] + [vmem] * 11,
        out_specs=[vmem] * 2,
        out_shape=[sent(4, 64, HEAD_DIM), sent(576, HEAD_DIM)],
        scratch_shapes=[pltpu.VMEM((256, HEAD_DIM), BF16)],
        compiler_params=pltpu.CompilerParams(vmem_limit_bytes=24 << 20),
        name="adapter_terms",
    )(place, low, back, got, first, up, down, rows, *prompts)


def project(place, rows, prompts, weight, other, down, up):
    width = KV_HEADS * HEAD_DIM

    def const(*shape):
        return pl.BlockSpec(shape, lambda k, place: (0,) * len(shape))

    def head(rows):
        return pl.BlockSpec((rows, HEAD_DIM), lambda k, place: (0, k))

    block = pl.BlockSpec((1, 4, 4, 128, HEAD_DIM), lambda k, place: (k, 0, 0, 0, 0))
    return pl.pallas_call(
        project_kernel,
        grid_spec=pltpu.PrefetchScalarGridSpec(
            num_scalar_prefetch=1,
            grid=(KV_HEADS,),
            in_specs=[
                const(TOKENS, D),
                const(16, D),
                const(16, D),
                const(16, D),
                const(16, D),
                block,
                block,
                const(RANK, D),
                head(RANK),
            ],
            out_specs=[head(TOKENS), const(8, 256, HEAD_DIM), head(D)],
            scratch_shapes=[
                pltpu.VMEM((TOKENS + 64, D), BF16),
                pltpu.VMEM((TOKENS + 64, RANK), BF16),
            ],
        ),
        out_shape=[sent(TOKENS, width), sent(8, 256, HEAD_DIM), sent(D, width)],
        compiler_params=PARAMS,
        cost_estimate=pl.CostEstimate(
            flops=600_000_000, bytes_accessed=10 << 20, transcendentals=0
        ),
        name="project",
    )(place, rows, *prompts, weight, other, down, up)


def prompt_gradient(low, up, down, weight):
    width = KV_HEADS * HEAD_DIM
    return pl.pallas_call(
        prompt_kernel,
        grid=(4,),
        in_specs=[
            whole((16, width)),
            whole((RANK, width)),
            heads_of(RANK, 1024),
            pl.BlockSpec((1024, width), lambda k: (k, 0)),
        ],
        out_specs=heads_of(16, 1024),
        out_shape=sent(16, D),
        scratch_shapes=[pltpu.VMEM((16, RANK), BF16)],
        compiler_params=PARAMS,
        name="prompt_gradient",
    )(low, up, down, weight)


def attend_backward(queries, cotangent, softmax, values, own_values, chosen, adapter):
    return pl.pallas_call(
        backward_kernel,
        grid=(KV_HEADS,),
        in_specs=[
            heads_of(TOKENS, WIDE),
            heads_of(TOKENS, WIDE),
            pl.BlockSpec((1, 2 * TOKENS, ROWS), lambda k: (k, 0, 0)),
            whole((8, 256, HEAD_DIM)),
            heads_of(TOKENS, HEAD_DIM),
            whole((PAIR, HEAD_DIM)),
            whole((576, HEAD_DIM)),
        ],
        out_specs=[whole((8, 384, HEAD_DIM)), heads_of(TOKENS, HEAD_DIM)],
        out_shape=[sent(8, 384, HEAD_DIM), sent(TOKENS, KV_HEADS * HEAD_DIM)],
        scratch_shapes=[
            pltpu.VMEM((TOKENS, ROWS), BF16),
            pltpu.VMEM((TOKENS, ROWS), BF16),
            pltpu.VMEM((ROWS, (PROMPTS + 1) * HEAD_DIM), BF16),
        ],
        compiler_params=PARAMS,
        cost_estimate=pl.CostEstimate(
            flops=3_000_000_000, bytes_accessed=9 << 20, transcendentals=0
        ),
        name="attend_backward",
    )(queries, cotangent, softmax, values, own_values, chosen, adapter)


def heads_first(rows):
    return rows.reshape(16, KV_HEADS, HEAD_DIM).transpose(1, 0, 2).reshape(KV_HEADS * 16, HEAD_DIM)


def from_others(part, axis):
    return [
        lax.ppermute(part, axis, [(i, (i + step) % 4) for i in range(4)]) for step in range(1, 4)
    ]


def after(array, *others):
    return lax.optimization_barrier((array, *others))[0]


def on_device(
    response_rows,
    prompt_rows,
    queries,
    response_keys,
    prompt_keys,
    cotangent,
    segment_index,
    prompt_choice,
    frozen_value_weight,
    value_adapter_down,
    value_adapter_up,
):
    segments = segment_index.reshape(TOKENS)
    onehot = (segments[:, None] == jnp.arange(8, dtype=jnp.int32)[None, :]).astype(jnp.int32)
    token_prompt = jnp.sum(onehot * prompt_choice.reshape(1, 8), axis=1)
    chosen = jnp.broadcast_to(jnp.tile(token_prompt, 2)[:, None], (PAIR, HEAD_DIM))
    position = jnp.arange(TOKENS, dtype=jnp.int32)
    own_seen = (segments[:, None] == segments[None, :]) & (position[:, None] <= position[None, :])
    bias = jnp.tile(jnp.where(own_seen, 0.0, -1e30).astype(F32), (1, 2))

    own_columns = lax.dynamic_slice_in_dim(
        frozen_value_weight, lax.axis_index("x") * HEAD_DIM, HEAD_DIM, 1
    )
    start = gather(
        jnp.concatenate([own_columns, heads_first(prompt_keys), value_adapter_down.T], axis=0), "zh"
    )
    place = jnp.stack([lax.axis_index(axis) for axis in ("x", "y", "zh", "c")]).astype(jnp.int32)
    key_all = gather(start[:, 128:], OWNERS).reshape(4, 2, 4, 80, HEAD_DIM)
    weight_part, prompt_part = lax.optimization_barrier((start[:, :128], prompt_rows, key_all))[:2]
    prompts = [prompt_rows, *from_others(prompt_part, "zh")]
    weight = gather(weight_part, ("x", "y")).reshape(4, 4, 4, 128, HEAD_DIM)

    send, low, back, first_proj, down, softmax = attend_forward(
        queries, cotangent, key_all, response_keys, chosen, bias, response_rows, value_adapter_up
    )
    other = lax.ppermute(after(weight, low, *prompts), "c", [(0, 1), (1, 0)])
    value_part, adapter = adapter_terms(
        place, low, back, swap(send, OWNERS), first_proj, value_adapter_up, down, response_rows,
        prompts,
    )
    values, part, weight = project(
        place, response_rows, prompts, weight, other, down, value_adapter_up
    )
    key_send, own_key_grad = attend_backward(
        queries, cotangent, softmax, swap(part, OWNERS), values, chosen, adapter
    )
    part = in_vmem(keys_y_kernel, 2, sent(4, 208, HEAD_DIM), "keys_y")(
        swap(key_send, OWNERS), value_part
    )
    response_grad = nt(low, weight) + ADAPTER_SCALE * tn(back, down)
    response_grad = response_grad.astype(BF16)
    part, response_grad = lax.optimization_barrier((swap(part, "zh"), response_grad))
    prompt_key_grad, prompt_low, part = in_vmem(
        keys_zh_kernel,
        1,
        [sent(16, KV_HEADS * HEAD_DIM), sent(16, KV_HEADS * HEAD_DIM), sent(16, 80, HEAD_DIM)],
        "keys_zh",
    )(part)
    first_grad, second_grad = in_vmem(
        group_kernel,
        1,
        [
            jax.ShapeDtypeStruct((RANK, 128), F32),
            jax.ShapeDtypeStruct((RANK, KV_HEADS * HEAD_DIM), F32),
        ],
        "over_group",
    )(swap(part, GROUP))
    return (
        response_grad,
        prompt_gradient(prompt_low, value_adapter_up, down, weight),
        own_key_grad,
        prompt_key_grad,
        first_grad.T,
        second_grad,
    )


def solution(mesh):
    fine = Mesh(np.asarray(mesh.devices).reshape(4, 4, 4, 4, 2), AXES)
    rows = P(AXES, None)
    in_specs = (rows,) * 8 + (P(SAMPLE, None), P(SAMPLE, None), P())
    out_specs = (rows,) * 4 + (P(SAMPLE, None), P())
    return jax.shard_map(
        on_device, mesh=fine, in_specs=in_specs, out_specs=out_specs, check_vma=False
    )
```

```python
import jax
import jax.numpy as jnp
import numpy as np
from jax import lax
from jax.experimental import pallas as pl
from jax.experimental.pallas import tpu as pltpu
from jax.sharding import Mesh, PartitionSpec as P

HEADS = 32
KV_HEADS = 4
HEAD_DIM = 128
GROUP_SIZE = HEADS // KV_HEADS
PROMPT_LEN = 128
PROMPTS = 4
RANK = 16
TOKENS = 128
D = 4096
SCALE = HEAD_DIM**-0.5
ADAPTER_SCALE = 2.0
FACTOR = ADAPTER_SCALE * float(73728) ** (-0.5)
AXES = ("x", "zl", "y", "zh", "c")
SAMPLE = ("y", "zh", "c")
GROUP = ("x", "zl")
OWNERS = ("y", "c")
PAIR = 2 * TOKENS
F32 = jnp.float32
BF16 = jnp.bfloat16


def swap(array, axis):
    return lax.all_to_all(array, axis, 0, 0, tiled=True)


def gather(array, axis):
    n = lax.axis_size(axis)
    return swap(jnp.broadcast_to(array[None], (n,) + array.shape), axis)


def nt(left, right):
    return lax.dot_general(left, right, (((1,), (1,)), ((), ())), preferred_element_type=F32)


def tn(left, right):
    return lax.dot_general(left, right, (((0,), (0,)), ((), ())), preferred_element_type=F32)


def nn(left, right):
    return jnp.dot(left, right, preferred_element_type=F32)


def expand(rows, chosen):
    zero = jnp.zeros_like(rows)
    return jnp.concatenate([jnp.where(chosen == p, rows, zero) for p in range(PROMPTS)], axis=1)


def pair_rows(ref, pair):
    first = 2 * pair * HEAD_DIM
    return jnp.concatenate(
        [ref[:, first : first + HEAD_DIM], ref[:, first + HEAD_DIM : first + 2 * HEAD_DIM]], axis=0
    )


def prompt_block(ref):
    return jnp.concatenate(
        [
            jnp.concatenate([ref[p, c, zh] for zh in range(4) for c in range(2)], axis=0)
            for p in range(PROMPTS)
        ],
        axis=1,
    )


def value_block(ref, k):
    def part(c, p, zh):
        return ref[p * 2 + c, pl.ds(pl.multiple_of(zh * 64 + k * 16, 16), 16), :]

    return jnp.concatenate(
        [
            jnp.concatenate([part(c, p, zh) for zh in range(4) for c in range(2)], axis=0)
            for p in range(PROMPTS)
        ],
        axis=1,
    )


def spread(ref, k, block):
    for p in range(PROMPTS):
        for zh in range(4):
            for c in range(2):
                s = (zh * 2 + c) * 16
                row = pl.multiple_of(zh * 64 + k * 16, 16)
                ref[p * 2 + c, pl.ds(row, 16), :] = block[
                    s : s + 16, p * HEAD_DIM : (p + 1) * HEAD_DIM
                ].astype(ref.dtype)


def softmax_pair(key_cat, own_key, expanded, rows, bias):
    seen = nt(key_cat, expanded) * SCALE
    own = nt(own_key, rows) * SCALE + bias
    top = jnp.maximum(jnp.max(seen, axis=0, keepdims=True), jnp.max(own, axis=0, keepdims=True))
    seen, own = jnp.exp(seen - top), jnp.exp(own - top)
    total = jnp.sum(seen, axis=0, keepdims=True) + jnp.sum(own, axis=0, keepdims=True)
    return seen / total, own / total


BLOCKS = [
    (((y * 4 + zh) * 2 + c) * 128, y, zh, c) for y in range(4) for zh in range(4) for c in range(2)
]


def forward_kernel(
    q_ref, cot_ref, key_ref, own_key_ref, chosen_ref, bias_ref, x_ref, up_ref, down_ref,
    send_ref, low_ref, back_ref, grad_ref, second_ref, softmax_ref,
    probs, own_probs, cots, back, first,
):
    k = pl.program_id(0)
    key_cat = prompt_block(key_ref)
    own_key = own_key_ref[...]
    chosen = chosen_ref[...]
    bias = bias_ref[...]
    for pair in range(GROUP_SIZE // 2):
        rows = pair_rows(q_ref, pair)
        seen, own = softmax_pair(key_cat, own_key, expand(rows, chosen), rows, bias)
        at = pl.ds(pair * PAIR, PAIR)
        softmax_ref[0, :TOKENS, at] = seen
        softmax_ref[0, TOKENS:, at] = own
        probs[:, at] = seen.astype(BF16)
        own_probs[:, at] = own.astype(BF16)
        cot = pair_rows(cot_ref, pair)
        cots[at, : PROMPTS * HEAD_DIM] = expand(cot, chosen)
        cots[at, PROMPTS * HEAD_DIM :] = cot
    spread(send_ref, k, nn(probs[...], cots[:, : PROMPTS * HEAD_DIM]))
    low = nn(own_probs[...], cots[:, PROMPTS * HEAD_DIM :]).astype(BF16)
    low_ref[...] = low

    @pl.when(k == 0)
    def _():
        back[...] = jnp.zeros_like(back)
        first[...] = nt(x_ref[...], down_ref[...]).astype(BF16)

    back[...] += nt(up_ref[...], low)
    second_ref[...] = tn(first[...], low)

    @pl.when(k == KV_HEADS - 1)
    def _():
        back_ref[...] = back[...].astype(BF16)
        grad_ref[...] = nn(back_ref[...], x_ref[...])


def place_before(place, step):
    return lax.rem(place + (4 - step), 4)


def adapter_kernel(
    place_ref, keys_ref, got_ref, grad_ref, second_ref, up_ref, down_ref,
    prompt_ref, prompt1_ref, prompt2_ref, prompt3_ref,
    part_ref, send_ref,
    total,
):
    total[...] = total_of(got_ref[...]).astype(BF16)
    for zh in range(4):
        part_ref[zh] = total[zh * 64 : (zh + 1) * 64, :]
    up = up_ref[...]
    prompts = jnp.concatenate(
        [prompt_ref[...], prompt1_ref[...], prompt2_ref[...], prompt3_ref[...]], axis=0
    )
    prompt_first = nt(prompts, down_ref[...]).astype(BF16)
    prompt_back = jnp.zeros((RANK, 64), F32)
    for k in range(KV_HEADS):
        at = slice(k * HEAD_DIM, (k + 1) * HEAD_DIM)
        starts = [place_before(place_ref[2], step) * 64 + k * 16 for step in range(4)]
        low = jnp.concatenate(
            [total[pl.ds(pl.multiple_of(row, 16), 16), :] for row in starts], axis=0
        )
        prompt_back = prompt_back + nt(up[:, at], low)
        second = (second_ref[:, at] + tn(prompt_first, low)).astype(BF16)
        for owner in range(8):
            send_ref[owner, 320 + k * 16 : 320 + (k + 1) * 16, :] = second
    grad = (grad_ref[...] + nn(prompt_back.astype(BF16), prompts)).astype(BF16)
    for at, y, zh, c in BLOCKS:
        row = 256 + zh * 16
        send_ref[y * 2 + c, row : row + 16, :] = grad[:, at : at + 128]
    send_ref[:, :256, :] = keys_ref[...]


def project_kernel(
    place_ref, x_ref, prompt_ref, prompt1_ref, prompt2_ref, prompt3_ref,
    weight_ref, other_ref, up_ref,
    values_ref, send_ref, weight_out_ref, down_ref,
    rows, first,
):
    k = pl.program_id(0)

    @pl.when(k == 0)
    def _():
        rows[:TOKENS, :] = x_ref[...]
        for step, ref in enumerate((prompt_ref, prompt1_ref, prompt2_ref, prompt3_ref)):
            rows[TOKENS + step * 16 : TOKENS + (step + 1) * 16, :] = ref[...]
        for y in range(4):
            for zh in range(4):
                for ref, c in ((weight_ref, place_ref[3]), (other_ref, 1 - place_ref[3])):
                    at = pl.multiple_of(((y * 4 + zh) * 2 + c) * 128, 128)
                    down_ref[:, pl.ds(at, 128)] = ref[0, y, zh, 128:, :]
        first[...] = nt(rows[...], down_ref[...]).astype(BF16)

    for y in range(4):
        for zh in range(4):
            for ref, c in ((weight_ref, place_ref[3]), (other_ref, 1 - place_ref[3])):
                row = pl.multiple_of(((y * 4 + zh) * 2 + c) * 128, 128)
                weight_out_ref[pl.ds(row, 128), :] = ref[0, y, zh, :128, :]
    values = nn(rows[...], weight_out_ref[...]) + ADAPTER_SCALE * nn(first[...], up_ref[...])
    values = values.astype(BF16)
    values_ref[...] = values[:TOKENS]
    for step in range(4):
        row = place_before(place_ref[2], step) * 64 + k * 16
        part = values[TOKENS + step * 16 : TOKENS + (step + 1) * 16]
        for owner in range(8):
            send_ref[owner, pl.ds(pl.multiple_of(row, 16), 16), :] = part


def total_of(parts):
    parts = parts.astype(F32)
    total = parts[0]
    for i in range(1, parts.shape[0]):
        total = total + parts[i]
    return total


def keys_y_kernel(got_ref, value_ref, send_ref):
    second = total_of(got_ref[:, 320:, :]).astype(BF16)
    for zh in range(4):
        send_ref[zh, :64, :] = total_of(got_ref[:, zh * 64 : (zh + 1) * 64, :]).astype(BF16)
        send_ref[zh, 64:128, :] = value_ref[zh]
        at = 256 + zh * 16
        send_ref[zh, 128:144, :] = total_of(got_ref[:, at : at + 16, :]).astype(BF16)
        send_ref[zh, 144:, :] = second


def keys_zh_kernel(got_ref, key_ref, low_ref, send_ref):
    total = total_of(got_ref[...])
    for k in range(KV_HEADS):
        at = slice(k * HEAD_DIM, (k + 1) * HEAD_DIM)
        key_ref[:, at] = total[k * 16 : (k + 1) * 16].astype(BF16)
        low_ref[:, at] = total[64 + k * 16 : 64 + (k + 1) * 16].astype(BF16)
    terms = total[128:].astype(BF16)
    for g in range(16):
        send_ref[g] = terms


def group_kernel(got_ref, first_ref, second_ref):
    total = total_of(got_ref[...]) * FACTOR
    first_ref[...] = total[:16]
    for k in range(KV_HEADS):
        second_ref[:, k * HEAD_DIM : (k + 1) * HEAD_DIM] = total[16 + k * 16 : 16 + (k + 1) * 16]


def prompt_kernel(low_ref, up_ref, down_ref, weight_ref, grad_ref, back):
    @pl.when(pl.program_id(0) == 0)
    def _():
        back[...] = nt(low_ref[...], up_ref[...]).astype(BF16)

    grad = nt(low_ref[...], weight_ref[...]) + ADAPTER_SCALE * nn(back[...], down_ref[...])
    grad_ref[...] = grad.astype(BF16)


def in_vmem(kernel, n, shapes, name):
    return pl.pallas_call(
        kernel,
        in_specs=[pl.BlockSpec(memory_space=pltpu.VMEM)] * n,
        out_specs=jax.tree.map(lambda _: pl.BlockSpec(memory_space=pltpu.VMEM), shapes),
        out_shape=shapes,
        compiler_params=pltpu.CompilerParams(vmem_limit_bytes=16 << 20),
        name=name,
    )


def sent(*shape):
    return jax.ShapeDtypeStruct(shape, BF16)


def backward_kernel(
    q_ref, cot_ref, softmax_ref, value_ref, own_value_ref, chosen_ref,
    send_ref, own_ref,
    grads, own_grads, queries,
):
    k = pl.program_id(0)
    value_cat = value_block(value_ref, k)
    own_value = own_value_ref[...]
    chosen = chosen_ref[...]
    for pair in range(GROUP_SIZE // 2):
        rows = pair_rows(q_ref, pair)
        at = pl.ds(pair * PAIR, PAIR)
        queries[at, : PROMPTS * HEAD_DIM] = expand(rows, chosen)
        queries[at, PROMPTS * HEAD_DIM :] = rows
        seen = softmax_ref[0, :TOKENS, at]
        own = softmax_ref[0, TOKENS:, at]
        cot = pair_rows(cot_ref, pair)
        seen_grad = nt(value_cat, expand(cot, chosen))
        own_grad = nt(own_value, cot)
        delta = jnp.sum(seen.astype(BF16).astype(F32) * seen_grad, axis=0, keepdims=True) + jnp.sum(
            own.astype(BF16).astype(F32) * own_grad, axis=0, keepdims=True
        )
        grads[:, at] = (seen * (seen_grad - delta)).astype(BF16)
        own_grads[:, at] = (own * (own_grad - delta)).astype(BF16)
    spread(send_ref, k, nn(grads[...], queries[:, : PROMPTS * HEAD_DIM]) * SCALE)
    own_ref[...] = (nn(own_grads[...], queries[:, PROMPTS * HEAD_DIM :]) * SCALE).astype(BF16)


def whole(shape):
    return pl.BlockSpec(shape, lambda k: (0,) * len(shape))


def heads_of(rows, width):
    return pl.BlockSpec((rows, width), lambda k: (0, k))


PROMPT_SPEC = pl.BlockSpec((4, 2, 4, 16, HEAD_DIM), lambda k: (0, 0, 0, k, 0))
WIDE = GROUP_SIZE * HEAD_DIM
ROWS = GROUP_SIZE * TOKENS


PARAMS = pltpu.CompilerParams(vmem_limit_bytes=56 << 20, dimension_semantics=("arbitrary",))


def attend_forward(queries, cotangent, keys, own_keys, chosen, bias, rows, up, down):
    return pl.pallas_call(
        forward_kernel,
        grid=(KV_HEADS,),
        in_specs=[
            heads_of(TOKENS, WIDE),
            heads_of(TOKENS, WIDE),
            PROMPT_SPEC,
            heads_of(TOKENS, HEAD_DIM),
            whole((PAIR, HEAD_DIM)),
            whole((TOKENS, PAIR)),
            whole((TOKENS, D)),
            heads_of(RANK, HEAD_DIM),
            whole((RANK, D)),
        ],
        out_specs=[
            whole((8, 256, HEAD_DIM)),
            heads_of(TOKENS, HEAD_DIM),
            whole((RANK, TOKENS)),
            whole((RANK, D)),
            heads_of(RANK, HEAD_DIM),
            pl.BlockSpec((1, 2 * TOKENS, ROWS), lambda k: (k, 0, 0)),
        ],
        out_shape=[
            sent(8, 256, HEAD_DIM),
            sent(TOKENS, KV_HEADS * HEAD_DIM),
            sent(RANK, TOKENS),
            jax.ShapeDtypeStruct((RANK, D), F32),
            jax.ShapeDtypeStruct((RANK, KV_HEADS * HEAD_DIM), F32),
            jax.ShapeDtypeStruct((KV_HEADS, 2 * TOKENS, ROWS), F32),
        ],
        scratch_shapes=[
            pltpu.VMEM((TOKENS, ROWS), BF16),
            pltpu.VMEM((TOKENS, ROWS), BF16),
            pltpu.VMEM((ROWS, (PROMPTS + 1) * HEAD_DIM), BF16),
            pltpu.VMEM((RANK, TOKENS), F32),
            pltpu.VMEM((TOKENS, RANK), BF16),
        ],
        compiler_params=PARAMS,
        cost_estimate=pl.CostEstimate(
            flops=2_000_000_000, bytes_accessed=5 << 20, transcendentals=1 << 20
        ),
        name="attend_forward",
    )(queries, cotangent, keys, own_keys, chosen, bias, rows, up, down)


def adapter_terms(place, keys, got, grad, second, up, down, prompts):
    vmem = pl.BlockSpec(memory_space=pltpu.VMEM)
    return pl.pallas_call(
        adapter_kernel,
        in_specs=[pl.BlockSpec(memory_space=pltpu.SMEM)] + [vmem] * 10,
        out_specs=[vmem] * 2,
        out_shape=[sent(4, 64, HEAD_DIM), sent(8, 384, HEAD_DIM)],
        scratch_shapes=[pltpu.VMEM((256, HEAD_DIM), BF16)],
        compiler_params=pltpu.CompilerParams(vmem_limit_bytes=24 << 20),
        name="adapter_terms",
    )(place, keys, got, grad, second, up, down, *prompts)


def project(place, rows, prompts, weight, other, up):
    width = KV_HEADS * HEAD_DIM

    def const(*shape):
        return pl.BlockSpec(shape, lambda k, place: (0,) * len(shape))

    def head(rows):
        return pl.BlockSpec((rows, HEAD_DIM), lambda k, place: (0, k))

    block = pl.BlockSpec((1, 4, 4, 144, HEAD_DIM), lambda k, place: (k, 0, 0, 0, 0))
    return pl.pallas_call(
        project_kernel,
        grid_spec=pltpu.PrefetchScalarGridSpec(
            num_scalar_prefetch=1,
            grid=(KV_HEADS,),
            in_specs=[
                const(TOKENS, D),
                const(16, D),
                const(16, D),
                const(16, D),
                const(16, D),
                block,
                block,
                head(RANK),
            ],
            out_specs=[head(TOKENS), const(8, 256, HEAD_DIM), head(D), const(RANK, D)],
            scratch_shapes=[
                pltpu.VMEM((TOKENS + 64, D), BF16),
                pltpu.VMEM((TOKENS + 64, RANK), BF16),
            ],
        ),
        out_shape=[sent(TOKENS, width), sent(8, 256, HEAD_DIM), sent(D, width), sent(RANK, D)],
        compiler_params=PARAMS,
        cost_estimate=pl.CostEstimate(
            flops=600_000_000, bytes_accessed=10 << 20, transcendentals=0
        ),
        name="project",
    )(place, rows, *prompts, weight, other, up)


def prompt_gradient(low, up, down, weight):
    width = KV_HEADS * HEAD_DIM
    return pl.pallas_call(
        prompt_kernel,
        grid=(4,),
        in_specs=[
            whole((16, width)),
            whole((RANK, width)),
            heads_of(RANK, 1024),
            pl.BlockSpec((1024, width), lambda k: (k, 0)),
        ],
        out_specs=heads_of(16, 1024),
        out_shape=sent(16, D),
        scratch_shapes=[pltpu.VMEM((16, RANK), BF16)],
        compiler_params=PARAMS,
        name="prompt_gradient",
    )(low, up, down, weight)


def attend_backward(queries, cotangent, softmax, values, own_values, chosen):
    return pl.pallas_call(
        backward_kernel,
        grid=(KV_HEADS,),
        in_specs=[
            heads_of(TOKENS, WIDE),
            heads_of(TOKENS, WIDE),
            pl.BlockSpec((1, 2 * TOKENS, ROWS), lambda k: (k, 0, 0)),
            whole((8, 256, HEAD_DIM)),
            heads_of(TOKENS, HEAD_DIM),
            whole((PAIR, HEAD_DIM)),
        ],
        out_specs=[whole((8, 256, HEAD_DIM)), heads_of(TOKENS, HEAD_DIM)],
        out_shape=[sent(8, 256, HEAD_DIM), sent(TOKENS, KV_HEADS * HEAD_DIM)],
        scratch_shapes=[
            pltpu.VMEM((TOKENS, ROWS), BF16),
            pltpu.VMEM((TOKENS, ROWS), BF16),
            pltpu.VMEM((ROWS, (PROMPTS + 1) * HEAD_DIM), BF16),
        ],
        compiler_params=PARAMS,
        cost_estimate=pl.CostEstimate(
            flops=3_000_000_000, bytes_accessed=9 << 20, transcendentals=0
        ),
        name="attend_backward",
    )(queries, cotangent, softmax, values, own_values, chosen)


def heads_first(rows):
    return rows.reshape(16, KV_HEADS, HEAD_DIM).transpose(1, 0, 2).reshape(KV_HEADS * 16, HEAD_DIM)


def move(part, axis, step):
    return lax.ppermute(part, axis, [(i, (i + step) % 4) for i in range(4)])


def after(array, *others):
    return lax.optimization_barrier((array, *others))[0]


def on_device(
    response_rows,
    prompt_rows,
    queries,
    response_keys,
    prompt_keys,
    cotangent,
    segment_index,
    prompt_choice,
    frozen_value_weight,
    value_adapter_down,
    value_adapter_up,
):
    segments = segment_index.reshape(TOKENS)
    onehot = (segments[:, None] == jnp.arange(8, dtype=jnp.int32)[None, :]).astype(jnp.int32)
    token_prompt = jnp.sum(onehot * prompt_choice.reshape(1, 8), axis=1)
    chosen = jnp.broadcast_to(jnp.tile(token_prompt, 2)[:, None], (PAIR, HEAD_DIM))
    position = jnp.arange(TOKENS, dtype=jnp.int32)
    own_seen = (segments[:, None] == segments[None, :]) & (position[:, None] <= position[None, :])
    bias = jnp.tile(jnp.where(own_seen, 0.0, -1e30).astype(F32), (1, 2))

    own_columns = lax.dynamic_slice_in_dim(
        frozen_value_weight, lax.axis_index("x") * HEAD_DIM, HEAD_DIM, 1
    )
    start = gather(
        jnp.concatenate([own_columns, value_adapter_down.T, heads_first(prompt_keys)], axis=0), "zh"
    )
    place = jnp.stack([lax.axis_index(axis) for axis in ("x", "y", "zh", "c")]).astype(jnp.int32)
    weight = gather(start[:, :144], ("x", "y")).reshape(4, 4, 4, 144, HEAD_DIM)
    before, behind = lax.optimization_barrier((prompt_rows, prompt_rows, start))[:2]
    before, behind = move(before, "zh", 1), move(behind, "zh", 3)
    prompts = [prompt_rows, before, move(before, "zh", 1), behind]
    other = lax.ppermute(after(weight, *prompts), "c", [(0, 1), (1, 0)])
    key_all = gather(after(start[:, 144:], weight), OWNERS).reshape(4, 2, 4, 64, HEAD_DIM)

    values, part, weight, down = project(
        place, response_rows, prompts, weight, other, value_adapter_up
    )
    value_all = swap(after(part, key_all), OWNERS)
    send, low, back, token_grad, token_second, softmax = attend_forward(
        queries, cotangent, key_all, response_keys, chosen, bias, response_rows, value_adapter_up,
        down,
    )
    got = swap(after(send, value_all), OWNERS)
    key_send, own_key_grad = attend_backward(
        queries, cotangent, softmax, value_all, values, chosen
    )
    value_part, key_send = adapter_terms(
        place, key_send, got, token_grad, token_second, value_adapter_up, down, prompts
    )
    part = in_vmem(keys_y_kernel, 2, sent(4, 208, HEAD_DIM), "keys_y")(
        swap(key_send, OWNERS), value_part
    )
    response_grad = nt(low, weight) + ADAPTER_SCALE * tn(back, down)
    response_grad = response_grad.astype(BF16)
    part, response_grad = lax.optimization_barrier((swap(part, "zh"), response_grad))
    prompt_key_grad, prompt_low, part = in_vmem(
        keys_zh_kernel,
        1,
        [sent(16, KV_HEADS * HEAD_DIM), sent(16, KV_HEADS * HEAD_DIM), sent(16, 80, HEAD_DIM)],
        "keys_zh",
    )(part)
    first_grad, second_grad = in_vmem(
        group_kernel,
        1,
        [
            jax.ShapeDtypeStruct((RANK, 128), F32),
            jax.ShapeDtypeStruct((RANK, KV_HEADS * HEAD_DIM), F32),
        ],
        "over_group",
    )(swap(part, GROUP))
    return (
        response_grad,
        prompt_gradient(prompt_low, value_adapter_up, down, weight),
        own_key_grad,
        prompt_key_grad,
        first_grad.T,
        second_grad,
    )


def solution(mesh):
    fine = Mesh(np.asarray(mesh.devices).reshape(4, 4, 4, 4, 2), AXES)
    rows = P(AXES, None)
    in_specs = (rows,) * 8 + (P(SAMPLE, None), P(SAMPLE, None), P())
    out_specs = (rows,) * 4 + (P(SAMPLE, None), P())
    return jax.shard_map(
        on_device, mesh=fine, in_specs=in_specs, out_specs=out_specs, check_vma=False
    )
```

```python
import jax
import jax.numpy as jnp
import numpy as np
from jax import lax
from jax.experimental import pallas as pl
from jax.experimental.pallas import tpu as pltpu
from jax.sharding import Mesh, PartitionSpec as P

HEADS = 32
KV_HEADS = 4
HEAD_DIM = 128
GROUP_SIZE = HEADS // KV_HEADS
PROMPT_LEN = 128
PROMPTS = 4
RANK = 16
TOKENS = 128
D = 4096
HALF = D // 2
SCALE = HEAD_DIM**-0.5
ADAPTER_SCALE = 2.0
FACTOR = ADAPTER_SCALE * float(73728) ** (-0.5)
AXES = ("x", "zl", "y", "zh", "c")
SAMPLE = ("y", "zh", "c")
GROUP = ("x", "zl")
OWNERS = ("y", "c")
PAIR = 2 * TOKENS
F32 = jnp.float32
BF16 = jnp.bfloat16


def swap(array, axis):
    return lax.all_to_all(array, axis, 0, 0, tiled=True)


def gather(array, axis):
    n = lax.axis_size(axis)
    return swap(jnp.broadcast_to(array[None], (n,) + array.shape), axis)


def nt(left, right):
    return lax.dot_general(left, right, (((1,), (1,)), ((), ())), preferred_element_type=F32)


def tn(left, right):
    return lax.dot_general(left, right, (((0,), (0,)), ((), ())), preferred_element_type=F32)


def nn(left, right):
    return jnp.dot(left, right, preferred_element_type=F32)


def expand(rows, mask, axis=1):
    return jnp.concatenate([rows * mask[p] for p in range(PROMPTS)], axis=axis)


def masks_of(segment_ref, choice_ref, mask_ref, mask_t_ref):
    segment = segment_ref[...]
    prompt = jnp.zeros_like(segment)
    for i in range(choice_ref.shape[1]):
        prompt = jnp.where(segment == i, choice_ref[0, i], prompt)
    chosen = jnp.broadcast_to(jnp.concatenate([prompt, prompt], axis=1), (HEAD_DIM, PAIR))
    for p in range(PROMPTS):
        mask = jnp.where(chosen == p, 1.0, 0.0).astype(F32)
        mask_t_ref[p] = mask.astype(BF16)
        mask_ref[p] = mask.T.astype(BF16)


def own_bias(segment_ref):
    segment = jnp.broadcast_to(segment_ref[...], (TOKENS, TOKENS))
    row = lax.broadcasted_iota(jnp.int32, (TOKENS, TOKENS), 0)
    column = lax.broadcasted_iota(jnp.int32, (TOKENS, TOKENS), 1)
    bias = jnp.where((segment.T == segment) & (row <= column), 0.0, -1e30).astype(F32)
    return jnp.concatenate([bias, bias], axis=1)


def pair_rows(ref, pair):
    first = 2 * pair * HEAD_DIM
    return jnp.concatenate(
        [ref[:, first : first + HEAD_DIM], ref[:, first + HEAD_DIM : first + 2 * HEAD_DIM]], axis=0
    )


def prompt_block(ref):
    return jnp.concatenate(
        [jnp.concatenate([ref[2 * p], ref[2 * p + 1]], axis=0) for p in range(PROMPTS)], axis=1
    )


def spread(ref, block):
    for p in range(PROMPTS):
        for c in range(2):
            ref[2 * p + c, :64, :] = block[
                c * 64 : (c + 1) * 64, p * HEAD_DIM : (p + 1) * HEAD_DIM
            ].astype(ref.dtype)


def softmax_pair(key_cat, own_key, expanded, columns, bias):
    seen = nn(key_cat, expanded) * SCALE
    own = nn(own_key, columns) * SCALE + bias
    top = jnp.maximum(jnp.max(seen, axis=0, keepdims=True), jnp.max(own, axis=0, keepdims=True))
    seen, own = jnp.exp(seen - top), jnp.exp(own - top)
    total = jnp.sum(seen, axis=0, keepdims=True) + jnp.sum(own, axis=0, keepdims=True)
    share = 1.0 / total
    return seen * share, own * share


BLOCKS = [
    (((y * 4 + zh) * 2 + c) * 128, y, zh, c) for y in range(4) for zh in range(4) for c in range(2)
]


def forward_kernel(
    choice_ref, q_ref, cot_ref, key_ref, own_key_ref, segment_ref, x_ref, up_ref, down_ref,
    send_ref, low_ref, grad_ref, second_ref, softmax_ref,
    cots, back, first, mask, mask_t, bias,
):
    k = pl.program_id(0)
    key_cat = prompt_block(key_ref)
    own_key = own_key_ref[...]

    @pl.when(k == 0)
    def _():
        masks_of(segment_ref, choice_ref, mask, mask_t)
        bias[...] = own_bias(segment_ref)

    for pair in range(GROUP_SIZE // 2):
        columns = pair_rows(q_ref, pair).T
        seen, own = softmax_pair(key_cat, own_key, expand(columns, mask_t, 0), columns, bias[...])
        at = pl.ds(pair * PAIR, PAIR)
        softmax_ref[0, :TOKENS, at] = seen.astype(BF16)
        softmax_ref[0, TOKENS:, at] = own.astype(BF16)
        cot = pair_rows(cot_ref, pair)
        cots[at, : PROMPTS * HEAD_DIM] = expand(cot, mask)
        cots[at, PROMPTS * HEAD_DIM :] = cot
    spread(send_ref, nn(softmax_ref[0, :TOKENS, :], cots[:, : PROMPTS * HEAD_DIM]))
    low = nn(softmax_ref[0, TOKENS:, :], cots[:, PROMPTS * HEAD_DIM :]).astype(BF16)
    low_ref[...] = low

    @pl.when(k == 0)
    def _():
        back[...] = jnp.zeros_like(back)
        first[...] = nt(x_ref[...], down_ref[...]).astype(BF16)

    back[...] += nt(up_ref[...], low)
    second_ref[...] = tn(first[...], low)

    @pl.when(k == KV_HEADS - 1)
    def _():
        grad_ref[...] = nn(back[...].astype(BF16), x_ref[...])


def place_before(place, step):
    return lax.rem(place + (4 - step), 4)


def adapter_kernel(
    keys_ref, got_ref, grad_ref, second_ref, up_ref, down_ref,
    prompt_ref, prompt1_ref, far_ref, far_rest_ref, prompt3_ref,
    part_ref, send_ref,
):
    low = total_of(got_ref[...]).astype(BF16)
    part_ref[...] = low
    far = jnp.concatenate([far_ref[...], far_rest_ref[:, : D - HALF]], axis=1)
    prompts = jnp.concatenate(
        [prompt_ref[:, :D], prompt1_ref[:, :D], far, prompt3_ref[:, :D]], axis=0
    )
    prompt_first = nt(prompts, down_ref[...]).astype(BF16)
    prompt_back = nt(up_ref[...], low).astype(BF16)
    second = (second_ref[...] + tn(prompt_first, low)).astype(BF16)
    grad = (grad_ref[...] + nn(prompt_back, prompts)).astype(BF16)
    send_ref[:, :64, :] = keys_ref[...]
    for at, y, zh, c in BLOCKS:
        send_ref[y * 2 + c, 64:80, zh * 128 : (zh + 1) * 128] = grad[:, at : at + 128]
    for owner in range(8):
        send_ref[owner, 80:, :] = second


def project_kernel(
    x_ref, prompt_ref, prompt1_ref, far_ref, far_rest_ref, prompt3_ref, up_ref,
    factor_ref, other_factor_ref, *refs,
):
    parts, (values_ref, send_ref, down_ref, rows, first, weight) = refs[:8], refs[8:]
    k = pl.program_id(0)
    core = lax.axis_index("c")
    places = [(i % 4, core if i < 4 else 1 - core, ref) for i, ref in enumerate(parts)]

    @pl.when(k == 0)
    def _():
        rows[:TOKENS, :] = x_ref[...]
        for step, ref in ((0, prompt_ref), (1, prompt1_ref), (3, prompt3_ref)):
            rows[TOKENS + step * 16 : TOKENS + (step + 1) * 16, :] = ref[...]
        rows[TOKENS + 32 : TOKENS + 48, :HALF] = far_ref[...]
        rows[TOKENS + 32 : TOKENS + 48, HALF:] = far_rest_ref[...]
        for ref, c in ((factor_ref, core), (other_factor_ref, 1 - core)):
            for y in range(4):
                for zh in range(4):
                    at = pl.multiple_of(((y * 4 + zh) * 2 + c) * 128, 128)
                    down_ref[:, pl.ds(at, 128)] = ref[zh, y]
        first[...] = nt(rows[...], down_ref[...]).astype(BF16)

    for y, c, ref in places:
        for zh in range(4):
            row = pl.multiple_of(((y * 4 + zh) * 2 + c) * 128, 128)
            weight[pl.ds(row, 128), :] = ref[0, 0, zh * 128 : (zh + 1) * 128, :]
    values = nn(rows[...], weight[...]) + ADAPTER_SCALE * nn(first[...], up_ref[...])
    values = values.astype(BF16)
    values_ref[...] = values[:TOKENS]
    for owner in range(8):
        send_ref[owner] = values[TOKENS:]


def total_of(parts):
    parts = parts.astype(F32)
    total = parts[0]
    for i in range(1, parts.shape[0]):
        total = total + parts[i]
    return total


def keys_y_kernel(got_ref, value_ref, send_ref):
    total = total_of(got_ref[...]).astype(BF16)
    value = value_ref[...]
    for zh in range(4):
        owner = place_before(lax.axis_index("zh"), zh)
        for k in range(KV_HEADS):
            at = slice(k * HEAD_DIM, (k + 1) * HEAD_DIM)
            rows = slice(zh * 16, (zh + 1) * 16)
            send_ref[owner, k * 16 : (k + 1) * 16, :] = total[rows, at]
            send_ref[owner, 64 + k * 16 : 64 + (k + 1) * 16, :] = value[rows, at]
            send_ref[zh, 144 + k * 16 : 144 + (k + 1) * 16, :] = total[80:, at]
        send_ref[zh, 128:144, :] = total[64:80, zh * 128 : (zh + 1) * 128]


def keys_zh_kernel(got_ref, key_ref, low_ref, send_ref):
    total = total_of(got_ref[...])
    for k in range(KV_HEADS):
        at = slice(k * HEAD_DIM, (k + 1) * HEAD_DIM)
        key_ref[:, at] = total[k * 16 : (k + 1) * 16].astype(BF16)
        low_ref[:, at] = total[64 + k * 16 : 64 + (k + 1) * 16].astype(BF16)
    terms = total[128:].astype(BF16)
    for g in range(16):
        send_ref[g] = terms


def weight_copies_kernel(start_ref, send_ref, part, sems):
    for zh in range(4):
        part[zh * 128 : (zh + 1) * 128, :] = start_ref[zh, :128, :]
    part[512:, :] = start_ref[lax.axis_index("x"), 128:, :]
    copies = [
        pltpu.make_async_copy(part, send_ref.at[i], sems.at[i]) for i in range(send_ref.shape[0])
    ]
    for copy in copies:
        copy.start()
    for copy in copies:
        copy.wait()


def key_copies_kernel(key_ref, key1_ref, key2_ref, key3_ref, send_ref):
    for step, ref in enumerate((key_ref, key1_ref, key2_ref, key3_ref)):
        for owner in range(8):
            send_ref[owner, step * 16 : (step + 1) * 16, :] = ref[...]


def group_kernel(got_ref, first_ref, second_ref):
    total = total_of(got_ref[...]) * FACTOR
    first_ref[...] = total[:16]
    for k in range(KV_HEADS):
        second_ref[:, k * HEAD_DIM : (k + 1) * HEAD_DIM] = total[16 + k * 16 : 16 + (k + 1) * 16]


def gradient_kernel(low_ref, up_ref, down_ref, *refs):
    parts, (grad_ref, back, weight) = refs[:8], refs[8:]

    @pl.when(pl.program_id(0) == 0)
    def _():
        back[...] = nt(low_ref[...], up_ref[...]).astype(BF16)

    core = lax.axis_index("c")
    for i, ref in enumerate(parts):
        c = core if i < 4 else 1 - core
        at = slice(i % 4 * HEAD_DIM, (i % 4 + 1) * HEAD_DIM)
        for zh in range(4):
            row = pl.multiple_of((zh * 2 + c) * 128, 128)
            weight[pl.ds(row, 128), at] = ref[0, 0, zh * 128 : (zh + 1) * 128, :]
    grad = nt(weight[...], low_ref[...]).T + ADAPTER_SCALE * nn(back[...], down_ref[...])
    grad_ref[...] = grad.astype(BF16)


def in_vmem(kernel, n, shapes, name):
    return pl.pallas_call(
        kernel,
        in_specs=[pl.BlockSpec(memory_space=pltpu.VMEM)] * n,
        out_specs=jax.tree.map(lambda _: pl.BlockSpec(memory_space=pltpu.VMEM), shapes),
        out_shape=shapes,
        compiler_params=pltpu.CompilerParams(vmem_limit_bytes=24 << 20),
        name=name,
    )


def sent(*shape):
    return jax.ShapeDtypeStruct(shape, BF16)


def backward_kernel(
    choice_ref, q_ref, cot_ref, softmax_ref, value_ref, own_value_ref, segment_ref,
    send_ref, own_ref,
    grads, own_grads, queries, mask, mask_t,
):
    @pl.when(pl.program_id(0) == 0)
    def _():
        masks_of(segment_ref, choice_ref, mask, mask_t)

    value_cat = prompt_block(value_ref)
    own_value = own_value_ref[...]
    for pair in range(GROUP_SIZE // 2):
        rows = pair_rows(q_ref, pair)
        at = pl.ds(pair * PAIR, PAIR)
        queries[at, : PROMPTS * HEAD_DIM] = expand(rows, mask)
        queries[at, PROMPTS * HEAD_DIM :] = rows
        seen = softmax_ref[0, :TOKENS, at].astype(F32)
        own = softmax_ref[0, TOKENS:, at].astype(F32)
        columns = pair_rows(cot_ref, pair).T
        seen_grad = nn(value_cat, expand(columns, mask_t, 0))
        own_grad = nn(own_value, columns)
        delta = jnp.sum(seen * seen_grad, axis=0, keepdims=True) + jnp.sum(
            own * own_grad, axis=0, keepdims=True
        )
        grads[:, at] = (seen * (seen_grad - delta)).astype(BF16)
        own_grads[:, at] = (own * (own_grad - delta)).astype(BF16)
    spread(send_ref, nn(grads[...], queries[:, : PROMPTS * HEAD_DIM]) * SCALE)
    own_ref[...] = (nn(own_grads[...], queries[:, PROMPTS * HEAD_DIM :]) * SCALE).astype(BF16)


def whole(shape):
    return pl.BlockSpec(shape, lambda k: (0,) * len(shape))


def heads_of(rows, width):
    return pl.BlockSpec((rows, width), lambda k: (0, k))


PROMPT_SPEC = pl.BlockSpec((8, 64, HEAD_DIM), lambda k: (0, 0, k))
WIDE = GROUP_SIZE * HEAD_DIM
ROWS = GROUP_SIZE * TOKENS


MASKS = [
    pltpu.VMEM((PROMPTS, PAIR, HEAD_DIM), BF16),
    pltpu.VMEM((PROMPTS, HEAD_DIM, PAIR), BF16),
]
PARAMS = pltpu.CompilerParams(vmem_limit_bytes=56 << 20, dimension_semantics=("arbitrary",))


def attend_forward(choice, queries, cotangent, keys, own_keys, segments, rows, up, down):
    return pl.pallas_call(
        forward_kernel,
        grid=(KV_HEADS,),
        in_specs=[
            pl.BlockSpec(memory_space=pltpu.SMEM),
            heads_of(TOKENS, WIDE),
            heads_of(TOKENS, WIDE),
            PROMPT_SPEC,
            heads_of(TOKENS, HEAD_DIM),
            whole((1, TOKENS)),
            whole((TOKENS, D)),
            heads_of(RANK, HEAD_DIM),
            whole((RANK, D)),
        ],
        out_specs=[
            PROMPT_SPEC,
            heads_of(TOKENS, HEAD_DIM),
            whole((RANK, D)),
            heads_of(RANK, HEAD_DIM),
            pl.BlockSpec((1, 2 * TOKENS, ROWS), lambda k: (k, 0, 0)),
        ],
        out_shape=[
            sent(8, 64, KV_HEADS * HEAD_DIM),
            sent(TOKENS, KV_HEADS * HEAD_DIM),
            jax.ShapeDtypeStruct((RANK, D), F32),
            jax.ShapeDtypeStruct((RANK, KV_HEADS * HEAD_DIM), F32),
            sent(KV_HEADS, 2 * TOKENS, ROWS),
        ],
        scratch_shapes=[
            pltpu.VMEM((ROWS, (PROMPTS + 1) * HEAD_DIM), BF16),
            pltpu.VMEM((RANK, TOKENS), F32),
            pltpu.VMEM((TOKENS, RANK), BF16),
            *MASKS,
            pltpu.VMEM((TOKENS, PAIR), F32),
        ],
        compiler_params=PARAMS,
        cost_estimate=pl.CostEstimate(
            flops=2_000_000_000, bytes_accessed=5 << 20, transcendentals=1 << 20
        ),
        name="attend_forward",
    )(choice, queries, cotangent, keys, own_keys, segments, rows, up, down)


def adapter_terms(keys, got, grad, second, up, down, prompts):
    width = KV_HEADS * HEAD_DIM
    return in_vmem(
        adapter_kernel, 11, [sent(64, width), sent(8, 96, width)], "adapter_terms"
    )(keys, got, grad, second, up, down, *prompts)


def weight_copies(start):
    return pl.pallas_call(
        weight_copies_kernel,
        in_specs=[pl.BlockSpec(memory_space=pltpu.VMEM)],
        out_specs=pl.BlockSpec(memory_space=pl.ANY),
        out_shape=sent(16, 528, HEAD_DIM),
        scratch_shapes=[pltpu.VMEM((528, HEAD_DIM), BF16), pltpu.SemaphoreType.DMA((16,))],
        name="weight_copies",
    )(start)


def key_copies(parts):
    width = KV_HEADS * HEAD_DIM
    return pl.pallas_call(
        key_copies_kernel,
        grid=(1,),
        in_specs=[
            pl.BlockSpec((16, width), lambda i, at=p.shape[1] // width - 1: (0, at)) for p in parts
        ],
        out_specs=whole((8, 64, width)),
        out_shape=sent(8, 64, width),
        name="key_copies",
    )(*parts)


def project(rows, prompts, weight, other, up):
    width = KV_HEADS * HEAD_DIM

    def run(y):
        return pl.BlockSpec((1, 1, 512, HEAD_DIM), lambda k: (k, y, 0, 0))

    runs = [run(y) for y in range(4)]
    factor = pl.BlockSpec((4, 4, RANK, HEAD_DIM), lambda k: (0, 0, 512 // RANK, 0))
    return pl.pallas_call(
        project_kernel,
        grid=(KV_HEADS,),
        in_specs=[
            whole((TOKENS, D)),
            whole((16, D)),
            whole((16, D)),
            whole((16, HALF)),
            whole((16, D - HALF)),
            whole((16, D)),
            heads_of(RANK, HEAD_DIM),
            factor,
            factor,
            *runs,
            *runs,
        ],
        out_specs=[
            heads_of(TOKENS, HEAD_DIM),
            PROMPT_SPEC,
            whole((RANK, D)),
        ],
        out_shape=[
            sent(TOKENS, width),
            sent(8, 64, width),
            sent(RANK, D),
        ],
        scratch_shapes=[
            pltpu.VMEM((TOKENS + 64, D), BF16),
            pltpu.VMEM((TOKENS + 64, RANK), BF16),
            pltpu.VMEM((D, HEAD_DIM), BF16),
        ],
        compiler_params=PARAMS,
        cost_estimate=pl.CostEstimate(
            flops=600_000_000, bytes_accessed=10 << 20, transcendentals=0
        ),
        name="project",
    )(rows, *prompts, up, weight, other, *[weight] * 4, *[other] * 4)


def input_gradient(low, up, down, weight, other):
    rows, width = low.shape

    def head(k):
        return pl.BlockSpec((1, 1, 512, HEAD_DIM), lambda y: (k, y, 0, 0))

    heads = [head(k) for k in range(KV_HEADS)]
    return pl.pallas_call(
        gradient_kernel,
        grid=(4,),
        in_specs=[
            whole((rows, width)),
            whole((RANK, width)),
            heads_of(RANK, 1024),
            *heads,
            *heads,
        ],
        out_specs=heads_of(rows, 1024),
        out_shape=sent(rows, D),
        scratch_shapes=[pltpu.VMEM((rows, RANK), BF16), pltpu.VMEM((1024, width), BF16)],
        compiler_params=PARAMS,
        cost_estimate=pl.CostEstimate(
            flops=rows * D * width * 2, bytes_accessed=5 << 20, transcendentals=0
        ),
        name="input_gradient",
    )(low, up, down, *[weight] * 4, *[other] * 4)


def attend_backward(choice, queries, cotangent, softmax, values, own_values, segments):
    return pl.pallas_call(
        backward_kernel,
        grid=(KV_HEADS,),
        in_specs=[
            pl.BlockSpec(memory_space=pltpu.SMEM),
            heads_of(TOKENS, WIDE),
            heads_of(TOKENS, WIDE),
            pl.BlockSpec((1, 2 * TOKENS, ROWS), lambda k: (k, 0, 0)),
            PROMPT_SPEC,
            heads_of(TOKENS, HEAD_DIM),
            whole((1, TOKENS)),
        ],
        out_specs=[PROMPT_SPEC, heads_of(TOKENS, HEAD_DIM)],
        out_shape=[sent(8, 64, KV_HEADS * HEAD_DIM), sent(TOKENS, KV_HEADS * HEAD_DIM)],
        scratch_shapes=[
            pltpu.VMEM((TOKENS, ROWS), BF16),
            pltpu.VMEM((TOKENS, ROWS), BF16),
            pltpu.VMEM((ROWS, (PROMPTS + 1) * HEAD_DIM), BF16),
            *MASKS,
        ],
        compiler_params=PARAMS,
        cost_estimate=pl.CostEstimate(
            flops=3_000_000_000, bytes_accessed=9 << 20, transcendentals=0
        ),
        name="attend_backward",
    )(choice, queries, cotangent, softmax, values, own_values, segments)


def move(part, axis, step):
    return lax.ppermute(part, axis, [(i, (i + step) % 4) for i in range(4)])


def after(array, *others):
    return lax.optimization_barrier((array, *others))[0]


def on_device(
    response_rows,
    prompt_rows,
    queries,
    response_keys,
    prompt_keys,
    cotangent,
    segment_index,
    prompt_choice,
    frozen_value_weight,
    value_adapter_down,
    value_adapter_up,
):
    own_columns = lax.dynamic_slice_in_dim(
        frozen_value_weight, lax.axis_index("x") * HEAD_DIM, HEAD_DIM, 1
    )
    start = gather(jnp.concatenate([own_columns, value_adapter_down.T], axis=0), "zh")
    own_prompts = after(jnp.concatenate([prompt_rows, prompt_keys], axis=1), start)
    weight = swap(weight_copies(start), ("x", "y"))
    before, behind = move(own_prompts, "zh", 1), move(own_prompts, "zh", 3)
    far, far_rest = move(before[:, :HALF], "zh", 1), move(behind[:, HALF:], "zh", 3)
    prompts = [own_prompts, before, far, far_rest, behind]
    weight, *prompts = lax.optimization_barrier((weight, *prompts))
    other = lax.ppermute(weight, "c", [(0, 1), (1, 0)])
    key_all = swap(key_copies([own_prompts, before, far_rest, behind]), OWNERS)

    shape = (4, 4, 528, HEAD_DIM)
    weights = [weight.reshape(shape), other.reshape(shape)]
    values, part, down = project(response_rows, prompts, *weights, value_adapter_up)
    value_all = swap(after(part, key_all), OWNERS)
    send, low, token_grad, token_second, softmax = attend_forward(
        prompt_choice, queries, cotangent, key_all, response_keys, segment_index, response_rows,
        value_adapter_up, down,
    )
    got = swap(after(send, value_all), OWNERS)
    key_send, own_key_grad = attend_backward(
        prompt_choice, queries, cotangent, softmax, value_all, values, segment_index
    )
    value_part, key_send = adapter_terms(
        key_send, got, token_grad, token_second, value_adapter_up, down, prompts
    )
    part = in_vmem(keys_y_kernel, 2, sent(4, 208, HEAD_DIM), "keys_y")(
        swap(key_send, OWNERS), value_part
    )
    response_grad = input_gradient(low, value_adapter_up, down, *weights)
    part, response_grad = lax.optimization_barrier((swap(part, "zh"), response_grad))
    prompt_key_grad, prompt_low, part = in_vmem(
        keys_zh_kernel,
        1,
        [sent(16, KV_HEADS * HEAD_DIM), sent(16, KV_HEADS * HEAD_DIM), sent(16, 80, HEAD_DIM)],
        "keys_zh",
    )(part)
    first_grad, second_grad = in_vmem(
        group_kernel,
        1,
        [
            jax.ShapeDtypeStruct((RANK, 128), F32),
            jax.ShapeDtypeStruct((RANK, KV_HEADS * HEAD_DIM), F32),
        ],
        "over_group",
    )(swap(part, GROUP))
    return (
        response_grad,
        input_gradient(prompt_low, value_adapter_up, down, *weights),
        own_key_grad,
        prompt_key_grad,
        first_grad.T,
        second_grad,
    )


def solution(mesh):
    fine = Mesh(np.asarray(mesh.devices).reshape(4, 4, 4, 4, 2), AXES)
    rows = P(AXES, None)
    in_specs = (rows,) * 8 + (P(SAMPLE, None), P(SAMPLE, None), P())
    out_specs = (rows,) * 4 + (P(SAMPLE, None), P())
    return jax.shard_map(
        on_device, mesh=fine, in_specs=in_specs, out_specs=out_specs, check_vma=False
    )
```

```python
import jax
import jax.numpy as jnp
import numpy as np
from jax import lax
from jax.experimental import pallas as pl
from jax.experimental.pallas import tpu as pltpu
from jax.sharding import Mesh, PartitionSpec as P

HEADS = 32
KV_HEADS = 4
HEAD_DIM = 128
GROUP_SIZE = HEADS // KV_HEADS
PROMPT_LEN = 128
PROMPTS = 4
RANK = 16
TOKENS = 128
D = 4096
SCALE = HEAD_DIM**-0.5
ADAPTER_SCALE = 2.0
FACTOR = ADAPTER_SCALE * float(73728) ** (-0.5)
AXES = ("x", "zl", "y", "zh", "c")
SAMPLE = ("y", "zh", "c")
GROUP = ("x", "zl")
OWNERS = ("y", "c")
PAIR = 2 * TOKENS
F32 = jnp.float32
BF16 = jnp.bfloat16


def swap(array, axis):
    return lax.all_to_all(array, axis, 0, 0, tiled=True)


def gather(array, axis):
    n = lax.axis_size(axis)
    return swap(jnp.broadcast_to(array[None], (n,) + array.shape), axis)


def nt(left, right):
    return lax.dot_general(left, right, (((1,), (1,)), ((), ())), preferred_element_type=F32)


def tn(left, right):
    return lax.dot_general(left, right, (((0,), (0,)), ((), ())), preferred_element_type=F32)


def nn(left, right):
    return jnp.dot(left, right, preferred_element_type=F32)


def expand(rows, chosen):
    zero = jnp.zeros_like(rows)
    return jnp.concatenate([jnp.where(chosen == p, rows, zero) for p in range(PROMPTS)], axis=1)


def chosen_of(segment_ref, choice_ref, chosen_ref):
    segment = segment_ref[...]
    prompt = jnp.zeros_like(segment)
    for i in range(choice_ref.shape[1]):
        prompt = jnp.where(segment == i, choice_ref[0, i], prompt)
    chosen_ref[...] = jnp.broadcast_to(
        jnp.concatenate([prompt, prompt], axis=1), (HEAD_DIM, PAIR)
    ).T


def own_bias(segment_ref):
    segment = jnp.broadcast_to(segment_ref[...], (TOKENS, TOKENS))
    row = lax.broadcasted_iota(jnp.int32, (TOKENS, TOKENS), 0)
    column = lax.broadcasted_iota(jnp.int32, (TOKENS, TOKENS), 1)
    bias = jnp.where((segment.T == segment) & (row <= column), 0.0, -1e30).astype(F32)
    return jnp.concatenate([bias, bias], axis=1)


def pair_rows(ref, pair):
    first = 2 * pair * HEAD_DIM
    return jnp.concatenate(
        [ref[:, first : first + HEAD_DIM], ref[:, first + HEAD_DIM : first + 2 * HEAD_DIM]], axis=0
    )


def prompt_block(ref):
    return jnp.concatenate(
        [
            jnp.concatenate([ref[p, c, zh] for zh in range(4) for c in range(2)], axis=0)
            for p in range(PROMPTS)
        ],
        axis=1,
    )


def value_block(ref, k):
    def part(c, p, zh):
        return ref[p * 2 + c, pl.ds(pl.multiple_of(zh * 64 + k * 16, 16), 16), :]

    return jnp.concatenate(
        [
            jnp.concatenate([part(c, p, zh) for zh in range(4) for c in range(2)], axis=0)
            for p in range(PROMPTS)
        ],
        axis=1,
    )


def spread(ref, k, block):
    for p in range(PROMPTS):
        for zh in range(4):
            for c in range(2):
                s = (zh * 2 + c) * 16
                row = pl.multiple_of(zh * 64 + k * 16, 16)
                ref[p * 2 + c, pl.ds(row, 16), :] = block[
                    s : s + 16, p * HEAD_DIM : (p + 1) * HEAD_DIM
                ].astype(ref.dtype)


def softmax_pair(key_cat, own_key, expanded, rows, bias):
    seen = nt(key_cat, expanded) * SCALE
    own = nt(own_key, rows) * SCALE + bias
    top = jnp.maximum(jnp.max(seen, axis=0, keepdims=True), jnp.max(own, axis=0, keepdims=True))
    seen, own = jnp.exp(seen - top), jnp.exp(own - top)
    total = jnp.sum(seen, axis=0, keepdims=True) + jnp.sum(own, axis=0, keepdims=True)
    return seen / total, own / total


BLOCKS = [
    (((y * 4 + zh) * 2 + c) * 128, y, zh, c) for y in range(4) for zh in range(4) for c in range(2)
]


def forward_kernel(
    choice_ref, q_ref, cot_ref, key_ref, own_key_ref, segment_ref, x_ref, up_ref, down_ref,
    send_ref, low_ref, back_ref, grad_ref, second_ref, softmax_ref,
    probs, own_probs, cots, back, first, chosen_rows, bias_rows,
):
    k = pl.program_id(0)
    key_cat = prompt_block(key_ref)
    own_key = own_key_ref[...]

    @pl.when(k == 0)
    def _():
        chosen_of(segment_ref, choice_ref, chosen_rows)
        bias_rows[...] = own_bias(segment_ref)

    chosen = chosen_rows[...]
    bias = bias_rows[...]
    for pair in range(GROUP_SIZE // 2):
        rows = pair_rows(q_ref, pair)
        seen, own = softmax_pair(key_cat, own_key, expand(rows, chosen), rows, bias)
        at = pl.ds(pair * PAIR, PAIR)
        softmax_ref[0, :TOKENS, at] = seen
        softmax_ref[0, TOKENS:, at] = own
        probs[:, at] = seen.astype(BF16)
        own_probs[:, at] = own.astype(BF16)
        cot = pair_rows(cot_ref, pair)
        cots[at, : PROMPTS * HEAD_DIM] = expand(cot, chosen)
        cots[at, PROMPTS * HEAD_DIM :] = cot
    spread(send_ref, k, nn(probs[...], cots[:, : PROMPTS * HEAD_DIM]))
    low = nn(own_probs[...], cots[:, PROMPTS * HEAD_DIM :]).astype(BF16)
    low_ref[...] = low

    @pl.when(k == 0)
    def _():
        back[...] = jnp.zeros_like(back)
        first[...] = nt(x_ref[...], down_ref[...]).astype(BF16)

    back[...] += nt(up_ref[...], low)
    second_ref[...] = tn(first[...], low)

    @pl.when(k == KV_HEADS - 1)
    def _():
        back_ref[...] = back[...].astype(BF16)
        grad_ref[...] = nn(back_ref[...], x_ref[...])


def weight_copies_kernel(start_ref, send_ref, part, sems):
    for zh in range(4):
        part[zh * 128 : (zh + 1) * 128, :] = start_ref[zh, :128, :]
    part[512:, :] = start_ref[lax.axis_index("x"), 128:144, :]
    copies = [
        pltpu.make_async_copy(part, send_ref.at[i], sems.at[i]) for i in range(send_ref.shape[0])
    ]
    for copy in copies:
        copy.start()
    for copy in copies:
        copy.wait()


def place_before(place, step):
    return lax.rem(place + (4 - step), 4)


def adapter_kernel(
    keys_ref, got_ref, grad_ref, second_ref, up_ref, down_ref,
    prompt_ref, prompt1_ref, prompt2_ref, prompt3_ref,
    part_ref, send_ref,
    total,
):
    total[...] = total_of(got_ref[...]).astype(BF16)
    for zh in range(4):
        part_ref[zh] = total[zh * 64 : (zh + 1) * 64, :]
    up = up_ref[...]
    prompts = jnp.concatenate(
        [prompt_ref[...], prompt1_ref[...], prompt2_ref[...], prompt3_ref[...]], axis=0
    )
    prompt_first = nt(prompts, down_ref[...]).astype(BF16)
    prompt_back = jnp.zeros((RANK, 64), F32)
    for k in range(KV_HEADS):
        at = slice(k * HEAD_DIM, (k + 1) * HEAD_DIM)
        starts = [place_before(lax.axis_index("zh"), step) * 64 + k * 16 for step in range(4)]
        low = jnp.concatenate(
            [total[pl.ds(pl.multiple_of(row, 16), 16), :] for row in starts], axis=0
        )
        prompt_back = prompt_back + nt(up[:, at], low)
        second = (second_ref[:, at] + tn(prompt_first, low)).astype(BF16)
        for owner in range(8):
            send_ref[owner, 320 + k * 16 : 320 + (k + 1) * 16, :] = second
    grad = (grad_ref[...] + nn(prompt_back.astype(BF16), prompts)).astype(BF16)
    for at, y, zh, c in BLOCKS:
        row = 256 + zh * 16
        send_ref[y * 2 + c, row : row + 16, :] = grad[:, at : at + 128]
    send_ref[:, :256, :] = keys_ref[...]


def project_kernel(
    x_ref, prompt_ref, prompt1_ref, prompt2_ref, prompt3_ref,
    weight_ref, other_ref, up_ref, factor_ref, other_factor_ref,
    values_ref, send_ref, weight_out_ref, down_ref,
    rows, first,
):
    k = pl.program_id(0)

    @pl.when(k == 0)
    def _():
        rows[:TOKENS, :] = x_ref[...]
        for step, ref in enumerate((prompt_ref, prompt1_ref, prompt2_ref, prompt3_ref)):
            rows[TOKENS + step * 16 : TOKENS + (step + 1) * 16, :] = ref[...]
        for y in range(4):
            for zh in range(4):
                for ref, c in ((factor_ref, lax.axis_index("c")), (other_factor_ref, 1 - lax.axis_index("c"))):
                    at = pl.multiple_of(((y * 4 + zh) * 2 + c) * 128, 128)
                    down_ref[:, pl.ds(at, 128)] = ref[zh, y]
        first[...] = nt(rows[...], down_ref[...]).astype(BF16)

    for y in range(4):
        for zh in range(4):
            for ref, c in ((weight_ref, lax.axis_index("c")), (other_ref, 1 - lax.axis_index("c"))):
                row = pl.multiple_of(((y * 4 + zh) * 2 + c) * 128, 128)
                weight_out_ref[pl.ds(row, 128), :] = ref[0, y, zh * 128 : (zh + 1) * 128, :]
    values = nn(rows[...], weight_out_ref[...]) + ADAPTER_SCALE * nn(first[...], up_ref[...])
    values = values.astype(BF16)
    values_ref[...] = values[:TOKENS]
    for step in range(4):
        row = place_before(lax.axis_index("zh"), step) * 64 + k * 16
        part = values[TOKENS + step * 16 : TOKENS + (step + 1) * 16]
        for owner in range(8):
            send_ref[owner, pl.ds(pl.multiple_of(row, 16), 16), :] = part


def total_of(parts):
    parts = parts.astype(F32)
    total = parts[0]
    for i in range(1, parts.shape[0]):
        total = total + parts[i]
    return total


def keys_y_kernel(got_ref, value_ref, send_ref):
    second = total_of(got_ref[:, 320:, :]).astype(BF16)
    for zh in range(4):
        send_ref[zh, :64, :] = total_of(got_ref[:, zh * 64 : (zh + 1) * 64, :]).astype(BF16)
        send_ref[zh, 64:128, :] = value_ref[zh]
        at = 256 + zh * 16
        send_ref[zh, 128:144, :] = total_of(got_ref[:, at : at + 16, :]).astype(BF16)
        send_ref[zh, 144:, :] = second


def keys_zh_kernel(got_ref, key_ref, low_ref, send_ref):
    total = total_of(got_ref[...])
    for k in range(KV_HEADS):
        at = slice(k * HEAD_DIM, (k + 1) * HEAD_DIM)
        key_ref[:, at] = total[k * 16 : (k + 1) * 16].astype(BF16)
        low_ref[:, at] = total[64 + k * 16 : 64 + (k + 1) * 16].astype(BF16)
    terms = total[128:].astype(BF16)
    for g in range(16):
        send_ref[g] = terms


def group_kernel(got_ref, first_ref, second_ref):
    total = total_of(got_ref[...]) * FACTOR
    first_ref[...] = total[:16]
    for k in range(KV_HEADS):
        second_ref[:, k * HEAD_DIM : (k + 1) * HEAD_DIM] = total[16 + k * 16 : 16 + (k + 1) * 16]


def prompt_kernel(low_ref, up_ref, down_ref, weight_ref, grad_ref, back):
    @pl.when(pl.program_id(0) == 0)
    def _():
        back[...] = nt(low_ref[...], up_ref[...]).astype(BF16)

    grad = nt(low_ref[...], weight_ref[...]) + ADAPTER_SCALE * nn(back[...], down_ref[...])
    grad_ref[...] = grad.astype(BF16)


def in_vmem(kernel, n, shapes, name):
    return pl.pallas_call(
        kernel,
        in_specs=[pl.BlockSpec(memory_space=pltpu.VMEM)] * n,
        out_specs=jax.tree.map(lambda _: pl.BlockSpec(memory_space=pltpu.VMEM), shapes),
        out_shape=shapes,
        compiler_params=pltpu.CompilerParams(vmem_limit_bytes=16 << 20),
        name=name,
    )


def sent(*shape):
    return jax.ShapeDtypeStruct(shape, BF16)


def backward_kernel(
    choice_ref, q_ref, cot_ref, softmax_ref, value_ref, own_value_ref, segment_ref,
    send_ref, own_ref,
    grads, own_grads, queries, chosen_rows,
):
    k = pl.program_id(0)
    value_cat = value_block(value_ref, k)
    own_value = own_value_ref[...]

    @pl.when(k == 0)
    def _():
        chosen_of(segment_ref, choice_ref, chosen_rows)

    chosen = chosen_rows[...]
    for pair in range(GROUP_SIZE // 2):
        rows = pair_rows(q_ref, pair)
        at = pl.ds(pair * PAIR, PAIR)
        queries[at, : PROMPTS * HEAD_DIM] = expand(rows, chosen)
        queries[at, PROMPTS * HEAD_DIM :] = rows
        seen = softmax_ref[0, :TOKENS, at]
        own = softmax_ref[0, TOKENS:, at]
        cot = pair_rows(cot_ref, pair)
        seen_grad = nt(value_cat, expand(cot, chosen))
        own_grad = nt(own_value, cot)
        delta = jnp.sum(seen.astype(BF16).astype(F32) * seen_grad, axis=0, keepdims=True) + jnp.sum(
            own.astype(BF16).astype(F32) * own_grad, axis=0, keepdims=True
        )
        grads[:, at] = (seen * (seen_grad - delta)).astype(BF16)
        own_grads[:, at] = (own * (own_grad - delta)).astype(BF16)
    spread(send_ref, k, nn(grads[...], queries[:, : PROMPTS * HEAD_DIM]) * SCALE)
    own_ref[...] = (nn(own_grads[...], queries[:, PROMPTS * HEAD_DIM :]) * SCALE).astype(BF16)


def whole(shape):
    return pl.BlockSpec(shape, lambda k: (0,) * len(shape))


def heads_of(rows, width):
    return pl.BlockSpec((rows, width), lambda k: (0, k))


PROMPT_SPEC = pl.BlockSpec((4, 2, 4, 16, HEAD_DIM), lambda k: (0, 0, 0, k, 0))
WIDE = GROUP_SIZE * HEAD_DIM
ROWS = GROUP_SIZE * TOKENS


PARAMS = pltpu.CompilerParams(vmem_limit_bytes=56 << 20, dimension_semantics=("arbitrary",))


def attend_forward(choice, queries, cotangent, keys, own_keys, segments, rows, up, down):
    return pl.pallas_call(
        forward_kernel,
        grid=(KV_HEADS,),
        in_specs=[
            pl.BlockSpec(memory_space=pltpu.SMEM),
            heads_of(TOKENS, WIDE),
            heads_of(TOKENS, WIDE),
            PROMPT_SPEC,
            heads_of(TOKENS, HEAD_DIM),
            whole((1, TOKENS)),
            whole((TOKENS, D)),
            heads_of(RANK, HEAD_DIM),
            whole((RANK, D)),
        ],
        out_specs=[
            whole((8, 256, HEAD_DIM)),
            heads_of(TOKENS, HEAD_DIM),
            whole((RANK, TOKENS)),
            whole((RANK, D)),
            heads_of(RANK, HEAD_DIM),
            pl.BlockSpec((1, 2 * TOKENS, ROWS), lambda k: (k, 0, 0)),
        ],
        out_shape=[
            sent(8, 256, HEAD_DIM),
            sent(TOKENS, KV_HEADS * HEAD_DIM),
            sent(RANK, TOKENS),
            jax.ShapeDtypeStruct((RANK, D), F32),
            jax.ShapeDtypeStruct((RANK, KV_HEADS * HEAD_DIM), F32),
            jax.ShapeDtypeStruct((KV_HEADS, 2 * TOKENS, ROWS), F32),
        ],
        scratch_shapes=[
            pltpu.VMEM((TOKENS, ROWS), BF16),
            pltpu.VMEM((TOKENS, ROWS), BF16),
            pltpu.VMEM((ROWS, (PROMPTS + 1) * HEAD_DIM), BF16),
            pltpu.VMEM((RANK, TOKENS), F32),
            pltpu.VMEM((TOKENS, RANK), BF16),
            pltpu.VMEM((PAIR, HEAD_DIM), jnp.int32),
            pltpu.VMEM((TOKENS, PAIR), F32),
        ],
        compiler_params=PARAMS,
        cost_estimate=pl.CostEstimate(
            flops=2_000_000_000, bytes_accessed=5 << 20, transcendentals=1 << 20
        ),
        name="attend_forward",
    )(choice, queries, cotangent, keys, own_keys, segments, rows, up, down)


def adapter_terms(keys, got, grad, second, up, down, prompts):
    vmem = pl.BlockSpec(memory_space=pltpu.VMEM)
    return pl.pallas_call(
        adapter_kernel,
        in_specs=[vmem] * 10,
        out_specs=[vmem] * 2,
        out_shape=[sent(4, 64, HEAD_DIM), sent(8, 384, HEAD_DIM)],
        scratch_shapes=[pltpu.VMEM((256, HEAD_DIM), BF16)],
        compiler_params=pltpu.CompilerParams(vmem_limit_bytes=24 << 20),
        name="adapter_terms",
    )(keys, got, grad, second, up, down, *prompts)


def weight_copies(start):
    return pl.pallas_call(
        weight_copies_kernel,
        in_specs=[pl.BlockSpec(memory_space=pltpu.VMEM)],
        out_specs=pl.BlockSpec(memory_space=pl.ANY),
        out_shape=sent(16, 528, HEAD_DIM),
        scratch_shapes=[pltpu.VMEM((528, HEAD_DIM), BF16), pltpu.SemaphoreType.DMA((16,))],
        name="weight_copies",
    )(start)


def project(rows, prompts, weight, other, up):
    width = KV_HEADS * HEAD_DIM

    def const(*shape):
        return pl.BlockSpec(shape, lambda k: (0,) * len(shape))

    def head(rows):
        return pl.BlockSpec((rows, HEAD_DIM), lambda k: (0, k))

    block = pl.BlockSpec((1, 4, 512, HEAD_DIM), lambda k: (k, 0, 0, 0))
    factor = pl.BlockSpec((4, 4, RANK, HEAD_DIM), lambda k: (0, 0, 512 // RANK, 0))
    return pl.pallas_call(
        project_kernel,
        grid=(KV_HEADS,),
        in_specs=[
            const(TOKENS, D),
            const(16, D),
            const(16, D),
            const(16, D),
            const(16, D),
            block,
            block,
            head(RANK),
            factor,
            factor,
        ],
        out_specs=[head(TOKENS), const(8, 256, HEAD_DIM), head(D), const(RANK, D)],
        scratch_shapes=[
            pltpu.VMEM((TOKENS + 64, D), BF16),
            pltpu.VMEM((TOKENS + 64, RANK), BF16),
        ],
        out_shape=[sent(TOKENS, width), sent(8, 256, HEAD_DIM), sent(D, width), sent(RANK, D)],
        compiler_params=PARAMS,
        cost_estimate=pl.CostEstimate(
            flops=600_000_000, bytes_accessed=10 << 20, transcendentals=0
        ),
        name="project",
    )(rows, *prompts, weight, other, up, weight, other)


def prompt_gradient(low, up, down, weight):
    width = KV_HEADS * HEAD_DIM
    return pl.pallas_call(
        prompt_kernel,
        grid=(4,),
        in_specs=[
            whole((16, width)),
            whole((RANK, width)),
            heads_of(RANK, 1024),
            pl.BlockSpec((1024, width), lambda k: (k, 0)),
        ],
        out_specs=heads_of(16, 1024),
        out_shape=sent(16, D),
        scratch_shapes=[pltpu.VMEM((16, RANK), BF16)],
        compiler_params=PARAMS,
        name="prompt_gradient",
    )(low, up, down, weight)


def attend_backward(choice, queries, cotangent, softmax, values, own_values, segments):
    return pl.pallas_call(
        backward_kernel,
        grid=(KV_HEADS,),
        in_specs=[
            pl.BlockSpec(memory_space=pltpu.SMEM),
            heads_of(TOKENS, WIDE),
            heads_of(TOKENS, WIDE),
            pl.BlockSpec((1, 2 * TOKENS, ROWS), lambda k: (k, 0, 0)),
            whole((8, 256, HEAD_DIM)),
            heads_of(TOKENS, HEAD_DIM),
            whole((1, TOKENS)),
        ],
        out_specs=[whole((8, 256, HEAD_DIM)), heads_of(TOKENS, HEAD_DIM)],
        out_shape=[sent(8, 256, HEAD_DIM), sent(TOKENS, KV_HEADS * HEAD_DIM)],
        scratch_shapes=[
            pltpu.VMEM((TOKENS, ROWS), BF16),
            pltpu.VMEM((TOKENS, ROWS), BF16),
            pltpu.VMEM((ROWS, (PROMPTS + 1) * HEAD_DIM), BF16),
            pltpu.VMEM((PAIR, HEAD_DIM), jnp.int32),
        ],
        compiler_params=PARAMS,
        cost_estimate=pl.CostEstimate(
            flops=3_000_000_000, bytes_accessed=9 << 20, transcendentals=0
        ),
        name="attend_backward",
    )(choice, queries, cotangent, softmax, values, own_values, segments)


def heads_first(rows):
    return rows.reshape(16, KV_HEADS, HEAD_DIM).transpose(1, 0, 2).reshape(KV_HEADS * 16, HEAD_DIM)


def move(part, axis, step):
    return lax.ppermute(part, axis, [(i, (i + step) % 4) for i in range(4)])


def after(array, *others):
    return lax.optimization_barrier((array, *others))[0]


def on_device(
    response_rows,
    prompt_rows,
    queries,
    response_keys,
    prompt_keys,
    cotangent,
    segment_index,
    prompt_choice,
    frozen_value_weight,
    value_adapter_down,
    value_adapter_up,
):
    own_columns = lax.dynamic_slice_in_dim(
        frozen_value_weight, lax.axis_index("x") * HEAD_DIM, HEAD_DIM, 1
    )
    start = gather(
        jnp.concatenate([own_columns, value_adapter_down.T, heads_first(prompt_keys)], axis=0), "zh"
    )
    weight = swap(weight_copies(start), ("x", "y")).reshape(4, 4, 528, HEAD_DIM)
    before, behind = lax.optimization_barrier((prompt_rows, prompt_rows, start))[:2]
    before, behind = move(before, "zh", 1), move(behind, "zh", 3)
    prompts = [prompt_rows, before, move(before, "zh", 1), behind]
    other = lax.ppermute(after(weight, *prompts), "c", [(0, 1), (1, 0)])
    key_all = gather(after(start[:, 144:], weight), OWNERS).reshape(4, 2, 4, 64, HEAD_DIM)

    values, part, weight, down = project(
        response_rows, prompts, weight, other, value_adapter_up
    )
    value_all = swap(after(part, key_all), OWNERS)
    send, low, back, token_grad, token_second, softmax = attend_forward(
        prompt_choice, queries, cotangent, key_all, response_keys, segment_index, response_rows,
        value_adapter_up, down,
    )
    got = swap(after(send, value_all), OWNERS)
    key_send, own_key_grad = attend_backward(
        prompt_choice, queries, cotangent, softmax, value_all, values, segment_index
    )
    value_part, key_send = adapter_terms(
        key_send, got, token_grad, token_second, value_adapter_up, down, prompts
    )
    part = in_vmem(keys_y_kernel, 2, sent(4, 208, HEAD_DIM), "keys_y")(
        swap(key_send, OWNERS), value_part
    )
    response_grad = nt(low, weight) + ADAPTER_SCALE * tn(back, down)
    response_grad = response_grad.astype(BF16)
    part, response_grad = lax.optimization_barrier((swap(part, "zh"), response_grad))
    prompt_key_grad, prompt_low, part = in_vmem(
        keys_zh_kernel,
        1,
        [sent(16, KV_HEADS * HEAD_DIM), sent(16, KV_HEADS * HEAD_DIM), sent(16, 80, HEAD_DIM)],
        "keys_zh",
    )(part)
    first_grad, second_grad = in_vmem(
        group_kernel,
        1,
        [
            jax.ShapeDtypeStruct((RANK, 128), F32),
            jax.ShapeDtypeStruct((RANK, KV_HEADS * HEAD_DIM), F32),
        ],
        "over_group",
    )(swap(part, GROUP))
    return (
        response_grad,
        prompt_gradient(prompt_low, value_adapter_up, down, weight),
        own_key_grad,
        prompt_key_grad,
        first_grad.T,
        second_grad,
    )


def solution(mesh):
    fine = Mesh(np.asarray(mesh.devices).reshape(4, 4, 4, 4, 2), AXES)
    rows = P(AXES, None)
    in_specs = (rows,) * 8 + (P(SAMPLE, None), P(SAMPLE, None), P())
    out_specs = (rows,) * 4 + (P(SAMPLE, None), P())
    return jax.shard_map(
        on_device, mesh=fine, in_specs=in_specs, out_specs=out_specs, check_vma=False
    )
```

```python
import jax
import jax.numpy as jnp
import numpy as np
from jax import lax
from jax.experimental import pallas as pl
from jax.experimental.pallas import tpu as pltpu
from jax.sharding import Mesh, PartitionSpec as P

HEADS = 32
KV_HEADS = 4
HEAD_DIM = 128
GROUP_SIZE = HEADS // KV_HEADS
PROMPT_LEN = 128
PROMPTS = 4
RANK = 16
TOKENS = 128
D = 4096
SCALE = HEAD_DIM**-0.5
ADAPTER_SCALE = 2.0
FACTOR = ADAPTER_SCALE * float(73728) ** (-0.5)
AXES = ("x", "zl", "y", "zh", "c")
SAMPLE = ("y", "zh", "c")
GROUP = ("x", "zl")
OWNERS = ("y", "c")
PAIR = 2 * TOKENS
F32 = jnp.float32
BF16 = jnp.bfloat16


def swap(array, axis):
    return lax.all_to_all(array, axis, 0, 0, tiled=True)


def gather(array, axis):
    n = lax.axis_size(axis)
    return swap(jnp.broadcast_to(array[None], (n,) + array.shape), axis)


def nt(left, right):
    return lax.dot_general(left, right, (((1,), (1,)), ((), ())), preferred_element_type=F32)


def tn(left, right):
    return lax.dot_general(left, right, (((0,), (0,)), ((), ())), preferred_element_type=F32)


def nn(left, right):
    return jnp.dot(left, right, preferred_element_type=F32)


def expand(rows, chosen):
    zero = jnp.zeros_like(rows)
    return jnp.concatenate([jnp.where(chosen == p, rows, zero) for p in range(PROMPTS)], axis=1)


def chosen_of(segment_ref, choice_ref, chosen_ref):
    segment = segment_ref[...]
    prompt = jnp.zeros_like(segment)
    for i in range(choice_ref.shape[1]):
        prompt = jnp.where(segment == i, choice_ref[0, i], prompt)
    chosen_ref[...] = jnp.broadcast_to(
        jnp.concatenate([prompt, prompt], axis=1), (HEAD_DIM, PAIR)
    ).T


def own_bias(segment_ref):
    segment = jnp.broadcast_to(segment_ref[...], (TOKENS, TOKENS))
    row = lax.broadcasted_iota(jnp.int32, (TOKENS, TOKENS), 0)
    column = lax.broadcasted_iota(jnp.int32, (TOKENS, TOKENS), 1)
    bias = jnp.where((segment.T == segment) & (row <= column), 0.0, -1e30).astype(F32)
    return jnp.concatenate([bias, bias], axis=1)


def pair_rows(ref, pair):
    first = 2 * pair * HEAD_DIM
    return jnp.concatenate(
        [ref[:, first : first + HEAD_DIM], ref[:, first + HEAD_DIM : first + 2 * HEAD_DIM]], axis=0
    )


def prompt_block(ref):
    return jnp.concatenate(
        [
            jnp.concatenate([ref[p, c, zh] for zh in range(4) for c in range(2)], axis=0)
            for p in range(PROMPTS)
        ],
        axis=1,
    )


def value_block(ref, k):
    def part(c, p, zh):
        return ref[p * 2 + c, pl.ds(pl.multiple_of(zh * 64 + k * 16, 16), 16), :]

    return jnp.concatenate(
        [
            jnp.concatenate([part(c, p, zh) for zh in range(4) for c in range(2)], axis=0)
            for p in range(PROMPTS)
        ],
        axis=1,
    )


def spread(ref, k, block):
    for p in range(PROMPTS):
        for zh in range(4):
            for c in range(2):
                s = (zh * 2 + c) * 16
                row = pl.multiple_of(zh * 64 + k * 16, 16)
                ref[p * 2 + c, pl.ds(row, 16), :] = block[
                    s : s + 16, p * HEAD_DIM : (p + 1) * HEAD_DIM
                ].astype(ref.dtype)


def softmax_pair(key_cat, own_key, expanded, rows, bias):
    seen = nt(key_cat, expanded) * SCALE
    own = nt(own_key, rows) * SCALE + bias
    top = jnp.maximum(jnp.max(seen, axis=0, keepdims=True), jnp.max(own, axis=0, keepdims=True))
    seen, own = jnp.exp(seen - top), jnp.exp(own - top)
    total = jnp.sum(seen, axis=0, keepdims=True) + jnp.sum(own, axis=0, keepdims=True)
    return seen / total, own / total


BLOCKS = [
    (((y * 4 + zh) * 2 + c) * 128, y, zh, c) for y in range(4) for zh in range(4) for c in range(2)
]


def forward_kernel(
    choice_ref, q_ref, cot_ref, key_ref, own_key_ref, segment_ref, x_ref, up_ref, down_ref,
    send_ref, low_ref, back_ref, grad_ref, second_ref, softmax_ref,
    probs, own_probs, cots, back, first, chosen_rows, bias_rows,
):
    k = pl.program_id(0)
    key_cat = prompt_block(key_ref)
    own_key = own_key_ref[...]

    @pl.when(k == 0)
    def _():
        chosen_of(segment_ref, choice_ref, chosen_rows)
        bias_rows[...] = own_bias(segment_ref)

    chosen = chosen_rows[...]
    bias = bias_rows[...]
    for pair in range(GROUP_SIZE // 2):
        rows = pair_rows(q_ref, pair)
        seen, own = softmax_pair(key_cat, own_key, expand(rows, chosen), rows, bias)
        at = pl.ds(pair * PAIR, PAIR)
        softmax_ref[0, :TOKENS, at] = seen
        softmax_ref[0, TOKENS:, at] = own
        probs[:, at] = seen.astype(BF16)
        own_probs[:, at] = own.astype(BF16)
        cot = pair_rows(cot_ref, pair)
        cots[at, : PROMPTS * HEAD_DIM] = expand(cot, chosen)
        cots[at, PROMPTS * HEAD_DIM :] = cot
    spread(send_ref, k, nn(probs[...], cots[:, : PROMPTS * HEAD_DIM]))
    low = nn(own_probs[...], cots[:, PROMPTS * HEAD_DIM :]).astype(BF16)
    low_ref[...] = low

    @pl.when(k == 0)
    def _():
        back[...] = jnp.zeros_like(back)
        first[...] = nt(x_ref[...], down_ref[...]).astype(BF16)

    back[...] += nt(up_ref[...], low)
    second_ref[...] = tn(first[...], low)

    @pl.when(k == KV_HEADS - 1)
    def _():
        back_ref[...] = back[...].astype(BF16)
        grad_ref[...] = nn(back_ref[...], x_ref[...])


def weight_copies_kernel(start_ref, send_ref, part, sems):
    for zh in range(4):
        part[zh * 128 : (zh + 1) * 128, :] = start_ref[zh, :128, :]
    part[512:, :] = start_ref[lax.axis_index("x"), 128:144, :]
    copies = [
        pltpu.make_async_copy(part, send_ref.at[i], sems.at[i]) for i in range(send_ref.shape[0])
    ]
    for copy in copies:
        copy.start()
    for copy in copies:
        copy.wait()


def place_before(place, step):
    return lax.rem(place + (4 - step), 4)


def adapter_kernel(
    keys_ref, got_ref, grad_ref, second_ref, up_ref, down_ref,
    prompt_ref, prompt1_ref, prompt2_ref, prompt3_ref,
    part_ref, send_ref,
    total,
):
    total[...] = total_of(got_ref[...]).astype(BF16)
    for zh in range(4):
        part_ref[zh] = total[zh * 64 : (zh + 1) * 64, :]
    up = up_ref[...]
    prompts = jnp.concatenate(
        [prompt_ref[...], prompt1_ref[...], prompt2_ref[...], prompt3_ref[...]], axis=0
    )
    prompt_first = nt(prompts, down_ref[...]).astype(BF16)
    prompt_back = jnp.zeros((RANK, 64), F32)
    for k in range(KV_HEADS):
        at = slice(k * HEAD_DIM, (k + 1) * HEAD_DIM)
        starts = [place_before(lax.axis_index("zh"), step) * 64 + k * 16 for step in range(4)]
        low = jnp.concatenate(
            [total[pl.ds(pl.multiple_of(row, 16), 16), :] for row in starts], axis=0
        )
        prompt_back = prompt_back + nt(up[:, at], low)
        second = (second_ref[:, at] + tn(prompt_first, low)).astype(BF16)
        for owner in range(8):
            send_ref[owner, 320 + k * 16 : 320 + (k + 1) * 16, :] = second
    grad = (grad_ref[...] + nn(prompt_back.astype(BF16), prompts)).astype(BF16)
    for at, y, zh, c in BLOCKS:
        row = 256 + zh * 16
        send_ref[y * 2 + c, row : row + 16, :] = grad[:, at : at + 128]
    send_ref[:, :256, :] = keys_ref[...]


def project_kernel(
    x_ref, prompt_ref, prompt1_ref, prompt2_ref, prompt3_ref,
    weight_ref, other_ref, up_ref, factor_ref, other_factor_ref,
    values_ref, send_ref, weight_out_ref, down_ref,
    rows, first,
):
    k = pl.program_id(0)

    @pl.when(k == 0)
    def _():
        rows[:TOKENS, :] = x_ref[...]
        for step, ref in enumerate((prompt_ref, prompt1_ref, prompt2_ref, prompt3_ref)):
            rows[TOKENS + step * 16 : TOKENS + (step + 1) * 16, :] = ref[...]
        for y in range(4):
            for zh in range(4):
                for ref, c in ((factor_ref, lax.axis_index("c")), (other_factor_ref, 1 - lax.axis_index("c"))):
                    at = pl.multiple_of(((y * 4 + zh) * 2 + c) * 128, 128)
                    down_ref[:, pl.ds(at, 128)] = ref[zh, y]
        first[...] = nt(rows[...], down_ref[...]).astype(BF16)

    for y in range(4):
        for zh in range(4):
            for ref, c in ((weight_ref, lax.axis_index("c")), (other_ref, 1 - lax.axis_index("c"))):
                row = pl.multiple_of(((y * 4 + zh) * 2 + c) * 128, 128)
                weight_out_ref[pl.ds(row, 128), :] = ref[0, y, zh * 128 : (zh + 1) * 128, :]
    values = nn(rows[...], weight_out_ref[...]) + ADAPTER_SCALE * nn(first[...], up_ref[...])
    values = values.astype(BF16)
    values_ref[...] = values[:TOKENS]
    for step in range(4):
        row = place_before(lax.axis_index("zh"), step) * 64 + k * 16
        part = values[TOKENS + step * 16 : TOKENS + (step + 1) * 16]
        for owner in range(8):
            send_ref[owner, pl.ds(pl.multiple_of(row, 16), 16), :] = part


def total_of(parts):
    parts = parts.astype(F32)
    total = parts[0]
    for i in range(1, parts.shape[0]):
        total = total + parts[i]
    return total


def keys_y_kernel(got_ref, value_ref, send_ref):
    second = total_of(got_ref[:, 320:, :]).astype(BF16)
    for zh in range(4):
        send_ref[zh, :64, :] = total_of(got_ref[:, zh * 64 : (zh + 1) * 64, :]).astype(BF16)
        send_ref[zh, 64:128, :] = value_ref[zh]
        at = 256 + zh * 16
        send_ref[zh, 128:144, :] = total_of(got_ref[:, at : at + 16, :]).astype(BF16)
        send_ref[zh, 144:, :] = second


def keys_zh_kernel(got_ref, key_ref, low_ref, send_ref):
    total = total_of(got_ref[...])
    for k in range(KV_HEADS):
        at = slice(k * HEAD_DIM, (k + 1) * HEAD_DIM)
        key_ref[:, at] = total[k * 16 : (k + 1) * 16].astype(BF16)
        low_ref[:, at] = total[64 + k * 16 : 64 + (k + 1) * 16].astype(BF16)
    terms = total[128:].astype(BF16)
    for g in range(16):
        send_ref[g] = terms


def group_kernel(got_ref, first_ref, second_ref):
    total = total_of(got_ref[...]) * FACTOR
    first_ref[...] = total[:16]
    for k in range(KV_HEADS):
        second_ref[:, k * HEAD_DIM : (k + 1) * HEAD_DIM] = total[16 + k * 16 : 16 + (k + 1) * 16]


def prompt_kernel(low_ref, up_ref, down_ref, weight_ref, grad_ref, back):
    @pl.when(pl.program_id(0) == 0)
    def _():
        back[...] = nt(low_ref[...], up_ref[...]).astype(BF16)

    grad = nt(low_ref[...], weight_ref[...]) + ADAPTER_SCALE * nn(back[...], down_ref[...])
    grad_ref[...] = grad.astype(BF16)


def in_vmem(kernel, n, shapes, name):
    return pl.pallas_call(
        kernel,
        in_specs=[pl.BlockSpec(memory_space=pltpu.VMEM)] * n,
        out_specs=jax.tree.map(lambda _: pl.BlockSpec(memory_space=pltpu.VMEM), shapes),
        out_shape=shapes,
        compiler_params=pltpu.CompilerParams(vmem_limit_bytes=16 << 20),
        name=name,
    )


def sent(*shape):
    return jax.ShapeDtypeStruct(shape, BF16)


def backward_kernel(
    choice_ref, q_ref, cot_ref, softmax_ref, value_ref, own_value_ref, segment_ref,
    send_ref, own_ref,
    grads, own_grads, queries, chosen_rows,
):
    k = pl.program_id(0)
    value_cat = value_block(value_ref, k)
    own_value = own_value_ref[...]

    @pl.when(k == 0)
    def _():
        chosen_of(segment_ref, choice_ref, chosen_rows)

    chosen = chosen_rows[...]
    for pair in range(GROUP_SIZE // 2):
        rows = pair_rows(q_ref, pair)
        at = pl.ds(pair * PAIR, PAIR)
        queries[at, : PROMPTS * HEAD_DIM] = expand(rows, chosen)
        queries[at, PROMPTS * HEAD_DIM :] = rows
        seen = softmax_ref[0, :TOKENS, at]
        own = softmax_ref[0, TOKENS:, at]
        cot = pair_rows(cot_ref, pair)
        seen_grad = nt(value_cat, expand(cot, chosen))
        own_grad = nt(own_value, cot)
        delta = jnp.sum(seen.astype(BF16).astype(F32) * seen_grad, axis=0, keepdims=True) + jnp.sum(
            own.astype(BF16).astype(F32) * own_grad, axis=0, keepdims=True
        )
        grads[:, at] = (seen * (seen_grad - delta)).astype(BF16)
        own_grads[:, at] = (own * (own_grad - delta)).astype(BF16)
    spread(send_ref, k, nn(grads[...], queries[:, : PROMPTS * HEAD_DIM]) * SCALE)
    own_ref[...] = (nn(own_grads[...], queries[:, PROMPTS * HEAD_DIM :]) * SCALE).astype(BF16)


def whole(shape):
    return pl.BlockSpec(shape, lambda k: (0,) * len(shape))


def heads_of(rows, width):
    return pl.BlockSpec((rows, width), lambda k: (0, k))


PROMPT_SPEC = pl.BlockSpec((4, 2, 4, 16, HEAD_DIM), lambda k: (0, 0, 0, k, 0))
WIDE = GROUP_SIZE * HEAD_DIM
ROWS = GROUP_SIZE * TOKENS


PARAMS = pltpu.CompilerParams(vmem_limit_bytes=56 << 20, dimension_semantics=("arbitrary",))


def attend_forward(choice, queries, cotangent, keys, own_keys, segments, rows, up, down):
    return pl.pallas_call(
        forward_kernel,
        grid=(KV_HEADS,),
        in_specs=[
            pl.BlockSpec(memory_space=pltpu.SMEM),
            heads_of(TOKENS, WIDE),
            heads_of(TOKENS, WIDE),
            PROMPT_SPEC,
            heads_of(TOKENS, HEAD_DIM),
            whole((1, TOKENS)),
            whole((TOKENS, D)),
            heads_of(RANK, HEAD_DIM),
            whole((RANK, D)),
        ],
        out_specs=[
            whole((8, 256, HEAD_DIM)),
            heads_of(TOKENS, HEAD_DIM),
            whole((RANK, TOKENS)),
            whole((RANK, D)),
            heads_of(RANK, HEAD_DIM),
            pl.BlockSpec((1, 2 * TOKENS, ROWS), lambda k: (k, 0, 0)),
        ],
        out_shape=[
            sent(8, 256, HEAD_DIM),
            sent(TOKENS, KV_HEADS * HEAD_DIM),
            sent(RANK, TOKENS),
            jax.ShapeDtypeStruct((RANK, D), F32),
            jax.ShapeDtypeStruct((RANK, KV_HEADS * HEAD_DIM), F32),
            jax.ShapeDtypeStruct((KV_HEADS, 2 * TOKENS, ROWS), F32),
        ],
        scratch_shapes=[
            pltpu.VMEM((TOKENS, ROWS), BF16),
            pltpu.VMEM((TOKENS, ROWS), BF16),
            pltpu.VMEM((ROWS, (PROMPTS + 1) * HEAD_DIM), BF16),
            pltpu.VMEM((RANK, TOKENS), F32),
            pltpu.VMEM((TOKENS, RANK), BF16),
            pltpu.VMEM((PAIR, HEAD_DIM), jnp.int32),
            pltpu.VMEM((TOKENS, PAIR), F32),
        ],
        compiler_params=PARAMS,
        cost_estimate=pl.CostEstimate(
            flops=2_000_000_000, bytes_accessed=5 << 20, transcendentals=1 << 20
        ),
        name="attend_forward",
    )(choice, queries, cotangent, keys, own_keys, segments, rows, up, down)


def adapter_terms(keys, got, grad, second, up, down, prompts):
    vmem = pl.BlockSpec(memory_space=pltpu.VMEM)
    return pl.pallas_call(
        adapter_kernel,
        in_specs=[vmem] * 10,
        out_specs=[vmem] * 2,
        out_shape=[sent(4, 64, HEAD_DIM), sent(8, 384, HEAD_DIM)],
        scratch_shapes=[pltpu.VMEM((256, HEAD_DIM), BF16)],
        compiler_params=pltpu.CompilerParams(vmem_limit_bytes=24 << 20),
        name="adapter_terms",
    )(keys, got, grad, second, up, down, *prompts)


def weight_copies(start):
    return pl.pallas_call(
        weight_copies_kernel,
        in_specs=[pl.BlockSpec(memory_space=pltpu.VMEM)],
        out_specs=pl.BlockSpec(memory_space=pl.ANY),
        out_shape=sent(16, 528, HEAD_DIM),
        scratch_shapes=[pltpu.VMEM((528, HEAD_DIM), BF16), pltpu.SemaphoreType.DMA((16,))],
        name="weight_copies",
    )(start)


def project(rows, prompts, weight, other, up):
    width = KV_HEADS * HEAD_DIM

    def const(*shape):
        return pl.BlockSpec(shape, lambda k: (0,) * len(shape))

    def head(rows):
        return pl.BlockSpec((rows, HEAD_DIM), lambda k: (0, k))

    block = pl.BlockSpec((1, 4, 512, HEAD_DIM), lambda k: (k, 0, 0, 0))
    factor = pl.BlockSpec((4, 4, RANK, HEAD_DIM), lambda k: (0, 0, 512 // RANK, 0))
    return pl.pallas_call(
        project_kernel,
        grid=(KV_HEADS,),
        in_specs=[
            const(TOKENS, D),
            const(16, D),
            const(16, D),
            const(16, D),
            const(16, D),
            block,
            block,
            head(RANK),
            factor,
            factor,
        ],
        out_specs=[head(TOKENS), const(8, 256, HEAD_DIM), head(D), const(RANK, D)],
        scratch_shapes=[
            pltpu.VMEM((TOKENS + 64, D), BF16),
            pltpu.VMEM((TOKENS + 64, RANK), BF16),
        ],
        out_shape=[sent(TOKENS, width), sent(8, 256, HEAD_DIM), sent(D, width), sent(RANK, D)],
        compiler_params=PARAMS,
        cost_estimate=pl.CostEstimate(
            flops=600_000_000, bytes_accessed=10 << 20, transcendentals=0
        ),
        name="project",
    )(rows, *prompts, weight, other, up, weight, other)


def prompt_gradient(low, up, down, weight):
    width = KV_HEADS * HEAD_DIM
    return pl.pallas_call(
        prompt_kernel,
        grid=(4,),
        in_specs=[
            whole((16, width)),
            whole((RANK, width)),
            heads_of(RANK, 1024),
            pl.BlockSpec((1024, width), lambda k: (k, 0)),
        ],
        out_specs=heads_of(16, 1024),
        out_shape=sent(16, D),
        scratch_shapes=[pltpu.VMEM((16, RANK), BF16)],
        compiler_params=PARAMS,
        name="prompt_gradient",
    )(low, up, down, weight)


def attend_backward(choice, queries, cotangent, softmax, values, own_values, segments):
    return pl.pallas_call(
        backward_kernel,
        grid=(KV_HEADS,),
        in_specs=[
            pl.BlockSpec(memory_space=pltpu.SMEM),
            heads_of(TOKENS, WIDE),
            heads_of(TOKENS, WIDE),
            pl.BlockSpec((1, 2 * TOKENS, ROWS), lambda k: (k, 0, 0)),
            whole((8, 256, HEAD_DIM)),
            heads_of(TOKENS, HEAD_DIM),
            whole((1, TOKENS)),
        ],
        out_specs=[whole((8, 256, HEAD_DIM)), heads_of(TOKENS, HEAD_DIM)],
        out_shape=[sent(8, 256, HEAD_DIM), sent(TOKENS, KV_HEADS * HEAD_DIM)],
        scratch_shapes=[
            pltpu.VMEM((TOKENS, ROWS), BF16),
            pltpu.VMEM((TOKENS, ROWS), BF16),
            pltpu.VMEM((ROWS, (PROMPTS + 1) * HEAD_DIM), BF16),
            pltpu.VMEM((PAIR, HEAD_DIM), jnp.int32),
        ],
        compiler_params=PARAMS,
        cost_estimate=pl.CostEstimate(
            flops=3_000_000_000, bytes_accessed=9 << 20, transcendentals=0
        ),
        name="attend_backward",
    )(choice, queries, cotangent, softmax, values, own_values, segments)


def heads_first(rows):
    return rows.reshape(16, KV_HEADS, HEAD_DIM).transpose(1, 0, 2).reshape(KV_HEADS * 16, HEAD_DIM)


def move(part, axis, step):
    return lax.ppermute(part, axis, [(i, (i + step) % 4) for i in range(4)])


def after(array, *others):
    return lax.optimization_barrier((array, *others))[0]


def on_device(
    response_rows,
    prompt_rows,
    queries,
    response_keys,
    prompt_keys,
    cotangent,
    segment_index,
    prompt_choice,
    frozen_value_weight,
    value_adapter_down,
    value_adapter_up,
):
    own_columns = lax.dynamic_slice_in_dim(
        frozen_value_weight, lax.axis_index("x") * HEAD_DIM, HEAD_DIM, 1
    )
    start = gather(
        jnp.concatenate([own_columns, value_adapter_down.T, heads_first(prompt_keys)], axis=0), "zh"
    )
    weight = swap(weight_copies(start), ("x", "y")).reshape(4, 4, 528, HEAD_DIM)
    before, behind = lax.optimization_barrier((prompt_rows, prompt_rows, start))[:2]
    before, behind = move(before, "zh", 1), move(behind, "zh", 3)
    prompts = [prompt_rows, before, move(before, "zh", 1), behind]
    other = lax.ppermute(after(weight, *prompts), "c", [(0, 1), (1, 0)])
    key_copies = jnp.broadcast_to(start[None, :, 144:], (8, 4, 64, HEAD_DIM))
    key_all = swap(after(key_copies, weight), OWNERS).reshape(4, 2, 4, 64, HEAD_DIM)

    values, part, weight, down = project(
        response_rows, prompts, weight, other, value_adapter_up
    )
    value_all = swap(after(part, key_all), OWNERS)
    send, low, back, token_grad, token_second, softmax = attend_forward(
        prompt_choice, queries, cotangent, key_all, response_keys, segment_index, response_rows,
        value_adapter_up, down,
    )
    got = swap(after(send, value_all), OWNERS)
    key_send, own_key_grad = attend_backward(
        prompt_choice, queries, cotangent, softmax, value_all, values, segment_index
    )
    value_part, key_send = adapter_terms(
        key_send, got, token_grad, token_second, value_adapter_up, down, prompts
    )
    part = in_vmem(keys_y_kernel, 2, sent(4, 208, HEAD_DIM), "keys_y")(
        swap(key_send, OWNERS), value_part
    )
    response_grad = nt(low, weight) + ADAPTER_SCALE * tn(back, down)
    response_grad = response_grad.astype(BF16)
    part, response_grad = lax.optimization_barrier((swap(part, "zh"), response_grad))
    prompt_key_grad, prompt_low, part = in_vmem(
        keys_zh_kernel,
        1,
        [sent(16, KV_HEADS * HEAD_DIM), sent(16, KV_HEADS * HEAD_DIM), sent(16, 80, HEAD_DIM)],
        "keys_zh",
    )(part)
    first_grad, second_grad = in_vmem(
        group_kernel,
        1,
        [
            jax.ShapeDtypeStruct((RANK, 128), F32),
            jax.ShapeDtypeStruct((RANK, KV_HEADS * HEAD_DIM), F32),
        ],
        "over_group",
    )(swap(part, GROUP))
    return (
        response_grad,
        prompt_gradient(prompt_low, value_adapter_up, down, weight),
        own_key_grad,
        prompt_key_grad,
        first_grad.T,
        second_grad,
    )


def solution(mesh):
    fine = Mesh(np.asarray(mesh.devices).reshape(4, 4, 4, 4, 2), AXES)
    rows = P(AXES, None)
    in_specs = (rows,) * 8 + (P(SAMPLE, None), P(SAMPLE, None), P())
    out_specs = (rows,) * 4 + (P(SAMPLE, None), P())
    return jax.shard_map(
        on_device, mesh=fine, in_specs=in_specs, out_specs=out_specs, check_vma=False
    )
```

```python
import jax
import jax.numpy as jnp
import numpy as np
from jax import lax
from jax.experimental import pallas as pl
from jax.experimental.pallas import tpu as pltpu
from jax.sharding import Mesh, PartitionSpec as P

HEADS = 32
KV_HEADS = 4
HEAD_DIM = 128
GROUP_SIZE = HEADS // KV_HEADS
PROMPT_LEN = 128
PROMPTS = 4
RANK = 16
TOKENS = 128
D = 4096
SCALE = HEAD_DIM**-0.5
ADAPTER_SCALE = 2.0
FACTOR = ADAPTER_SCALE * float(73728) ** (-0.5)
AXES = ("x", "zl", "y", "zh", "c")
SAMPLE = ("y", "zh", "c")
GROUP = ("x", "zl")
OWNERS = ("y", "c")
PAIR = 2 * TOKENS
F32 = jnp.float32
BF16 = jnp.bfloat16


def swap(array, axis):
    return lax.all_to_all(array, axis, 0, 0, tiled=True)


def gather(array, axis):
    n = lax.axis_size(axis)
    return swap(jnp.broadcast_to(array[None], (n,) + array.shape), axis)


def nt(left, right):
    return lax.dot_general(left, right, (((1,), (1,)), ((), ())), preferred_element_type=F32)


def tn(left, right):
    return lax.dot_general(left, right, (((0,), (0,)), ((), ())), preferred_element_type=F32)


def nn(left, right):
    return jnp.dot(left, right, preferred_element_type=F32)


def expand(rows, chosen):
    zero = jnp.zeros_like(rows)
    return jnp.concatenate([jnp.where(chosen == p, rows, zero) for p in range(PROMPTS)], axis=1)


def chosen_of(segment_ref, choice_ref, chosen_ref):
    segment = segment_ref[...]
    prompt = jnp.zeros_like(segment)
    for i in range(choice_ref.shape[1]):
        prompt = jnp.where(segment == i, choice_ref[0, i], prompt)
    chosen_ref[...] = jnp.broadcast_to(
        jnp.concatenate([prompt, prompt], axis=1), (HEAD_DIM, PAIR)
    ).T


def own_bias(segment_ref):
    segment = jnp.broadcast_to(segment_ref[...], (TOKENS, TOKENS))
    row = lax.broadcasted_iota(jnp.int32, (TOKENS, TOKENS), 0)
    column = lax.broadcasted_iota(jnp.int32, (TOKENS, TOKENS), 1)
    bias = jnp.where((segment.T == segment) & (row <= column), 0.0, -1e30).astype(F32)
    return jnp.concatenate([bias, bias], axis=1)


def pair_rows(ref, pair):
    first = 2 * pair * HEAD_DIM
    return jnp.concatenate(
        [ref[:, first : first + HEAD_DIM], ref[:, first + HEAD_DIM : first + 2 * HEAD_DIM]], axis=0
    )


def prompt_block(ref):
    return jnp.concatenate(
        [
            jnp.concatenate([ref[p, c, zh] for zh in range(4) for c in range(2)], axis=0)
            for p in range(PROMPTS)
        ],
        axis=1,
    )


def value_block(ref, k):
    def part(c, p, zh):
        return ref[p * 2 + c, pl.ds(pl.multiple_of(zh * 64 + k * 16, 16), 16), :]

    return jnp.concatenate(
        [
            jnp.concatenate([part(c, p, zh) for zh in range(4) for c in range(2)], axis=0)
            for p in range(PROMPTS)
        ],
        axis=1,
    )


def spread(ref, k, block):
    for p in range(PROMPTS):
        for zh in range(4):
            for c in range(2):
                s = (zh * 2 + c) * 16
                row = pl.multiple_of(zh * 64 + k * 16, 16)
                ref[p * 2 + c, pl.ds(row, 16), :] = block[
                    s : s + 16, p * HEAD_DIM : (p + 1) * HEAD_DIM
                ].astype(ref.dtype)


def softmax_pair(key_cat, own_key, expanded, rows, bias):
    seen = nt(key_cat, expanded) * SCALE
    own = nt(own_key, rows) * SCALE + bias
    top = jnp.maximum(jnp.max(seen, axis=0, keepdims=True), jnp.max(own, axis=0, keepdims=True))
    seen, own = jnp.exp(seen - top), jnp.exp(own - top)
    total = jnp.sum(seen, axis=0, keepdims=True) + jnp.sum(own, axis=0, keepdims=True)
    return seen / total, own / total


BLOCKS = [
    (((y * 4 + zh) * 2 + c) * 128, y, zh, c) for y in range(4) for zh in range(4) for c in range(2)
]


def forward_kernel(
    choice_ref, q_ref, cot_ref, key_ref, own_key_ref, segment_ref, x_ref, up_ref, down_ref,
    send_ref, low_ref, back_ref, grad_ref, second_ref, softmax_ref,
    cots, back, first, chosen_rows, bias_rows,
):
    k = pl.program_id(0)
    key_cat = prompt_block(key_ref)
    own_key = own_key_ref[...]

    @pl.when(k == 0)
    def _():
        chosen_of(segment_ref, choice_ref, chosen_rows)
        bias_rows[...] = own_bias(segment_ref)

    chosen = chosen_rows[...]
    bias = bias_rows[...]
    for pair in range(GROUP_SIZE // 2):
        rows = pair_rows(q_ref, pair)
        seen, own = softmax_pair(key_cat, own_key, expand(rows, chosen), rows, bias)
        at = pl.ds(pair * PAIR, PAIR)
        softmax_ref[0, :TOKENS, at] = seen.astype(BF16)
        softmax_ref[0, TOKENS:, at] = own.astype(BF16)
        cot = pair_rows(cot_ref, pair)
        cots[at, : PROMPTS * HEAD_DIM] = expand(cot, chosen)
        cots[at, PROMPTS * HEAD_DIM :] = cot
    spread(send_ref, k, nn(softmax_ref[0, :TOKENS, :], cots[:, : PROMPTS * HEAD_DIM]))
    low = nn(softmax_ref[0, TOKENS:, :], cots[:, PROMPTS * HEAD_DIM :]).astype(BF16)
    low_ref[...] = low

    @pl.when(k == 0)
    def _():
        back[...] = jnp.zeros_like(back)
        first[...] = nt(x_ref[...], down_ref[...]).astype(BF16)

    back[...] += nt(up_ref[...], low)
    second_ref[...] = tn(first[...], low)

    @pl.when(k == KV_HEADS - 1)
    def _():
        back_ref[...] = back[...].astype(BF16)
        grad_ref[...] = nn(back_ref[...], x_ref[...])


def weight_copies_kernel(start_ref, send_ref, part, sems):
    for zh in range(4):
        part[zh * 128 : (zh + 1) * 128, :] = start_ref[zh, :128, :]
    part[512:, :] = start_ref[lax.axis_index("x"), 128:144, :]
    copies = [
        pltpu.make_async_copy(part, send_ref.at[i], sems.at[i]) for i in range(send_ref.shape[0])
    ]
    for copy in copies:
        copy.start()
    for copy in copies:
        copy.wait()


def place_before(place, step):
    return lax.rem(place + (4 - step), 4)


def adapter_kernel(
    keys_ref, got_ref, grad_ref, second_ref, up_ref, down_ref,
    prompt_ref, prompt1_ref, prompt2_ref, prompt3_ref,
    part_ref, send_ref,
    total,
):
    total[...] = total_of(got_ref[...]).astype(BF16)
    for zh in range(4):
        part_ref[zh] = total[zh * 64 : (zh + 1) * 64, :]
    up = up_ref[...]
    prompts = jnp.concatenate(
        [prompt_ref[...], prompt1_ref[...], prompt2_ref[...], prompt3_ref[...]], axis=0
    )
    prompt_first = nt(prompts, down_ref[...]).astype(BF16)
    prompt_back = jnp.zeros((RANK, 64), F32)
    for k in range(KV_HEADS):
        at = slice(k * HEAD_DIM, (k + 1) * HEAD_DIM)
        starts = [place_before(lax.axis_index("zh"), step) * 64 + k * 16 for step in range(4)]
        low = jnp.concatenate(
            [total[pl.ds(pl.multiple_of(row, 16), 16), :] for row in starts], axis=0
        )
        prompt_back = prompt_back + nt(up[:, at], low)
        second = (second_ref[:, at] + tn(prompt_first, low)).astype(BF16)
        for owner in range(8):
            send_ref[owner, 320 + k * 16 : 320 + (k + 1) * 16, :] = second
    grad = (grad_ref[...] + nn(prompt_back.astype(BF16), prompts)).astype(BF16)
    for at, y, zh, c in BLOCKS:
        row = 256 + zh * 16
        send_ref[y * 2 + c, row : row + 16, :] = grad[:, at : at + 128]
    send_ref[:, :256, :] = keys_ref[...]


def project_kernel(
    x_ref, prompt_ref, prompt1_ref, prompt2_ref, prompt3_ref,
    weight_ref, other_ref, up_ref, factor_ref, other_factor_ref,
    values_ref, send_ref, weight_out_ref, down_ref,
    rows, first,
):
    k = pl.program_id(0)

    @pl.when(k == 0)
    def _():
        rows[:TOKENS, :] = x_ref[...]
        for step, ref in enumerate((prompt_ref, prompt1_ref, prompt2_ref, prompt3_ref)):
            rows[TOKENS + step * 16 : TOKENS + (step + 1) * 16, :] = ref[...]
        for y in range(4):
            for zh in range(4):
                for ref, c in ((factor_ref, lax.axis_index("c")), (other_factor_ref, 1 - lax.axis_index("c"))):
                    at = pl.multiple_of(((y * 4 + zh) * 2 + c) * 128, 128)
                    down_ref[:, pl.ds(at, 128)] = ref[zh, y]
        first[...] = nt(rows[...], down_ref[...]).astype(BF16)

    for y in range(4):
        for zh in range(4):
            for ref, c in ((weight_ref, lax.axis_index("c")), (other_ref, 1 - lax.axis_index("c"))):
                row = pl.multiple_of(((y * 4 + zh) * 2 + c) * 128, 128)
                weight_out_ref[pl.ds(row, 128), :] = ref[0, y, zh * 128 : (zh + 1) * 128, :]
    values = nn(rows[...], weight_out_ref[...]) + ADAPTER_SCALE * nn(first[...], up_ref[...])
    values = values.astype(BF16)
    values_ref[...] = values[:TOKENS]
    for step in range(4):
        row = place_before(lax.axis_index("zh"), step) * 64 + k * 16
        part = values[TOKENS + step * 16 : TOKENS + (step + 1) * 16]
        for owner in range(8):
            send_ref[owner, pl.ds(pl.multiple_of(row, 16), 16), :] = part


def total_of(parts):
    parts = parts.astype(F32)
    total = parts[0]
    for i in range(1, parts.shape[0]):
        total = total + parts[i]
    return total


def keys_y_kernel(got_ref, value_ref, send_ref):
    second = total_of(got_ref[:, 320:, :]).astype(BF16)
    for zh in range(4):
        send_ref[zh, :64, :] = total_of(got_ref[:, zh * 64 : (zh + 1) * 64, :]).astype(BF16)
        send_ref[zh, 64:128, :] = value_ref[zh]
        at = 256 + zh * 16
        send_ref[zh, 128:144, :] = total_of(got_ref[:, at : at + 16, :]).astype(BF16)
        send_ref[zh, 144:, :] = second


def keys_zh_kernel(got_ref, key_ref, low_ref, send_ref):
    total = total_of(got_ref[...])
    for k in range(KV_HEADS):
        at = slice(k * HEAD_DIM, (k + 1) * HEAD_DIM)
        key_ref[:, at] = total[k * 16 : (k + 1) * 16].astype(BF16)
        low_ref[:, at] = total[64 + k * 16 : 64 + (k + 1) * 16].astype(BF16)
    terms = total[128:].astype(BF16)
    for g in range(16):
        send_ref[g] = terms


def group_kernel(got_ref, first_ref, second_ref):
    total = total_of(got_ref[...]) * FACTOR
    first_ref[...] = total[:16]
    for k in range(KV_HEADS):
        second_ref[:, k * HEAD_DIM : (k + 1) * HEAD_DIM] = total[16 + k * 16 : 16 + (k + 1) * 16]


def prompt_kernel(low_ref, up_ref, down_ref, weight_ref, grad_ref, back):
    @pl.when(pl.program_id(0) == 0)
    def _():
        back[...] = nt(low_ref[...], up_ref[...]).astype(BF16)

    grad = nt(low_ref[...], weight_ref[...]) + ADAPTER_SCALE * nn(back[...], down_ref[...])
    grad_ref[...] = grad.astype(BF16)


def in_vmem(kernel, n, shapes, name):
    return pl.pallas_call(
        kernel,
        in_specs=[pl.BlockSpec(memory_space=pltpu.VMEM)] * n,
        out_specs=jax.tree.map(lambda _: pl.BlockSpec(memory_space=pltpu.VMEM), shapes),
        out_shape=shapes,
        compiler_params=pltpu.CompilerParams(vmem_limit_bytes=16 << 20),
        name=name,
    )


def sent(*shape):
    return jax.ShapeDtypeStruct(shape, BF16)


def backward_kernel(
    choice_ref, q_ref, cot_ref, softmax_ref, value_ref, own_value_ref, segment_ref,
    send_ref, own_ref,
    grads, own_grads, queries, chosen_rows,
):
    k = pl.program_id(0)
    value_cat = value_block(value_ref, k)
    own_value = own_value_ref[...]

    @pl.when(k == 0)
    def _():
        chosen_of(segment_ref, choice_ref, chosen_rows)

    chosen = chosen_rows[...]
    for pair in range(GROUP_SIZE // 2):
        rows = pair_rows(q_ref, pair)
        at = pl.ds(pair * PAIR, PAIR)
        queries[at, : PROMPTS * HEAD_DIM] = expand(rows, chosen)
        queries[at, PROMPTS * HEAD_DIM :] = rows
        seen = softmax_ref[0, :TOKENS, at].astype(F32)
        own = softmax_ref[0, TOKENS:, at].astype(F32)
        cot = pair_rows(cot_ref, pair)
        seen_grad = nt(value_cat, expand(cot, chosen))
        own_grad = nt(own_value, cot)
        delta = jnp.sum(seen * seen_grad, axis=0, keepdims=True) + jnp.sum(
            own * own_grad, axis=0, keepdims=True
        )
        grads[:, at] = (seen * (seen_grad - delta)).astype(BF16)
        own_grads[:, at] = (own * (own_grad - delta)).astype(BF16)
    spread(send_ref, k, nn(grads[...], queries[:, : PROMPTS * HEAD_DIM]) * SCALE)
    own_ref[...] = (nn(own_grads[...], queries[:, PROMPTS * HEAD_DIM :]) * SCALE).astype(BF16)


def whole(shape):
    return pl.BlockSpec(shape, lambda k: (0,) * len(shape))


def heads_of(rows, width):
    return pl.BlockSpec((rows, width), lambda k: (0, k))


PROMPT_SPEC = pl.BlockSpec((4, 2, 4, 16, HEAD_DIM), lambda k: (0, 0, 0, k, 0))
WIDE = GROUP_SIZE * HEAD_DIM
ROWS = GROUP_SIZE * TOKENS


PARAMS = pltpu.CompilerParams(vmem_limit_bytes=56 << 20, dimension_semantics=("arbitrary",))


def attend_forward(choice, queries, cotangent, keys, own_keys, segments, rows, up, down):
    return pl.pallas_call(
        forward_kernel,
        grid=(KV_HEADS,),
        in_specs=[
            pl.BlockSpec(memory_space=pltpu.SMEM),
            heads_of(TOKENS, WIDE),
            heads_of(TOKENS, WIDE),
            PROMPT_SPEC,
            heads_of(TOKENS, HEAD_DIM),
            whole((1, TOKENS)),
            whole((TOKENS, D)),
            heads_of(RANK, HEAD_DIM),
            whole((RANK, D)),
        ],
        out_specs=[
            whole((8, 256, HEAD_DIM)),
            heads_of(TOKENS, HEAD_DIM),
            whole((RANK, TOKENS)),
            whole((RANK, D)),
            heads_of(RANK, HEAD_DIM),
            pl.BlockSpec((1, 2 * TOKENS, ROWS), lambda k: (k, 0, 0)),
        ],
        out_shape=[
            sent(8, 256, HEAD_DIM),
            sent(TOKENS, KV_HEADS * HEAD_DIM),
            sent(RANK, TOKENS),
            jax.ShapeDtypeStruct((RANK, D), F32),
            jax.ShapeDtypeStruct((RANK, KV_HEADS * HEAD_DIM), F32),
            sent(KV_HEADS, 2 * TOKENS, ROWS),
        ],
        scratch_shapes=[
            pltpu.VMEM((ROWS, (PROMPTS + 1) * HEAD_DIM), BF16),
            pltpu.VMEM((RANK, TOKENS), F32),
            pltpu.VMEM((TOKENS, RANK), BF16),
            pltpu.VMEM((PAIR, HEAD_DIM), jnp.int32),
            pltpu.VMEM((TOKENS, PAIR), F32),
        ],
        compiler_params=PARAMS,
        cost_estimate=pl.CostEstimate(
            flops=2_000_000_000, bytes_accessed=5 << 20, transcendentals=1 << 20
        ),
        name="attend_forward",
    )(choice, queries, cotangent, keys, own_keys, segments, rows, up, down)


def adapter_terms(keys, got, grad, second, up, down, prompts):
    vmem = pl.BlockSpec(memory_space=pltpu.VMEM)
    return pl.pallas_call(
        adapter_kernel,
        in_specs=[vmem] * 10,
        out_specs=[vmem] * 2,
        out_shape=[sent(4, 64, HEAD_DIM), sent(8, 384, HEAD_DIM)],
        scratch_shapes=[pltpu.VMEM((256, HEAD_DIM), BF16)],
        compiler_params=pltpu.CompilerParams(vmem_limit_bytes=24 << 20),
        name="adapter_terms",
    )(keys, got, grad, second, up, down, *prompts)


def weight_copies(start):
    return pl.pallas_call(
        weight_copies_kernel,
        in_specs=[pl.BlockSpec(memory_space=pltpu.VMEM)],
        out_specs=pl.BlockSpec(memory_space=pl.ANY),
        out_shape=sent(16, 528, HEAD_DIM),
        scratch_shapes=[pltpu.VMEM((528, HEAD_DIM), BF16), pltpu.SemaphoreType.DMA((16,))],
        name="weight_copies",
    )(start)


def project(rows, prompts, weight, other, up):
    width = KV_HEADS * HEAD_DIM

    def const(*shape):
        return pl.BlockSpec(shape, lambda k: (0,) * len(shape))

    def head(rows):
        return pl.BlockSpec((rows, HEAD_DIM), lambda k: (0, k))

    block = pl.BlockSpec((1, 4, 512, HEAD_DIM), lambda k: (k, 0, 0, 0))
    factor = pl.BlockSpec((4, 4, RANK, HEAD_DIM), lambda k: (0, 0, 512 // RANK, 0))
    return pl.pallas_call(
        project_kernel,
        grid=(KV_HEADS,),
        in_specs=[
            const(TOKENS, D),
            const(16, D),
            const(16, D),
            const(16, D),
            const(16, D),
            block,
            block,
            head(RANK),
            factor,
            factor,
        ],
        out_specs=[head(TOKENS), const(8, 256, HEAD_DIM), head(D), const(RANK, D)],
        scratch_shapes=[
            pltpu.VMEM((TOKENS + 64, D), BF16),
            pltpu.VMEM((TOKENS + 64, RANK), BF16),
        ],
        out_shape=[sent(TOKENS, width), sent(8, 256, HEAD_DIM), sent(D, width), sent(RANK, D)],
        compiler_params=PARAMS,
        cost_estimate=pl.CostEstimate(
            flops=600_000_000, bytes_accessed=10 << 20, transcendentals=0
        ),
        name="project",
    )(rows, *prompts, weight, other, up, weight, other)


def prompt_gradient(low, up, down, weight):
    width = KV_HEADS * HEAD_DIM
    return pl.pallas_call(
        prompt_kernel,
        grid=(4,),
        in_specs=[
            whole((16, width)),
            whole((RANK, width)),
            heads_of(RANK, 1024),
            pl.BlockSpec((1024, width), lambda k: (k, 0)),
        ],
        out_specs=heads_of(16, 1024),
        out_shape=sent(16, D),
        scratch_shapes=[pltpu.VMEM((16, RANK), BF16)],
        compiler_params=PARAMS,
        name="prompt_gradient",
    )(low, up, down, weight)


def attend_backward(choice, queries, cotangent, softmax, values, own_values, segments):
    return pl.pallas_call(
        backward_kernel,
        grid=(KV_HEADS,),
        in_specs=[
            pl.BlockSpec(memory_space=pltpu.SMEM),
            heads_of(TOKENS, WIDE),
            heads_of(TOKENS, WIDE),
            pl.BlockSpec((1, 2 * TOKENS, ROWS), lambda k: (k, 0, 0)),
            whole((8, 256, HEAD_DIM)),
            heads_of(TOKENS, HEAD_DIM),
            whole((1, TOKENS)),
        ],
        out_specs=[whole((8, 256, HEAD_DIM)), heads_of(TOKENS, HEAD_DIM)],
        out_shape=[sent(8, 256, HEAD_DIM), sent(TOKENS, KV_HEADS * HEAD_DIM)],
        scratch_shapes=[
            pltpu.VMEM((TOKENS, ROWS), BF16),
            pltpu.VMEM((TOKENS, ROWS), BF16),
            pltpu.VMEM((ROWS, (PROMPTS + 1) * HEAD_DIM), BF16),
            pltpu.VMEM((PAIR, HEAD_DIM), jnp.int32),
        ],
        compiler_params=PARAMS,
        cost_estimate=pl.CostEstimate(
            flops=3_000_000_000, bytes_accessed=9 << 20, transcendentals=0
        ),
        name="attend_backward",
    )(choice, queries, cotangent, softmax, values, own_values, segments)


def heads_first(rows):
    return rows.reshape(16, KV_HEADS, HEAD_DIM).transpose(1, 0, 2).reshape(KV_HEADS * 16, HEAD_DIM)


def move(part, axis, step):
    return lax.ppermute(part, axis, [(i, (i + step) % 4) for i in range(4)])


def after(array, *others):
    return lax.optimization_barrier((array, *others))[0]


def on_device(
    response_rows,
    prompt_rows,
    queries,
    response_keys,
    prompt_keys,
    cotangent,
    segment_index,
    prompt_choice,
    frozen_value_weight,
    value_adapter_down,
    value_adapter_up,
):
    own_columns = lax.dynamic_slice_in_dim(
        frozen_value_weight, lax.axis_index("x") * HEAD_DIM, HEAD_DIM, 1
    )
    start = gather(
        jnp.concatenate([own_columns, value_adapter_down.T, heads_first(prompt_keys)], axis=0), "zh"
    )
    weight = swap(weight_copies(start), ("x", "y")).reshape(4, 4, 528, HEAD_DIM)
    before, behind = lax.optimization_barrier((prompt_rows, prompt_rows, start))[:2]
    before, behind = move(before, "zh", 1), move(behind, "zh", 3)
    prompts = [prompt_rows, before, move(before, "zh", 1), behind]
    other = lax.ppermute(after(weight, *prompts), "c", [(0, 1), (1, 0)])
    key_copies = jnp.broadcast_to(start[None, :, 144:], (8, 4, 64, HEAD_DIM))
    key_all = swap(after(key_copies, weight), OWNERS).reshape(4, 2, 4, 64, HEAD_DIM)

    values, part, weight, down = project(
        response_rows, prompts, weight, other, value_adapter_up
    )
    value_all = swap(after(part, key_all), OWNERS)
    send, low, back, token_grad, token_second, softmax = attend_forward(
        prompt_choice, queries, cotangent, key_all, response_keys, segment_index, response_rows,
        value_adapter_up, down,
    )
    got = swap(after(send, value_all), OWNERS)
    key_send, own_key_grad = attend_backward(
        prompt_choice, queries, cotangent, softmax, value_all, values, segment_index
    )
    value_part, key_send = adapter_terms(
        key_send, got, token_grad, token_second, value_adapter_up, down, prompts
    )
    part = in_vmem(keys_y_kernel, 2, sent(4, 208, HEAD_DIM), "keys_y")(
        swap(key_send, OWNERS), value_part
    )
    response_grad = nt(low, weight) + ADAPTER_SCALE * tn(back, down)
    response_grad = response_grad.astype(BF16)
    part, response_grad = lax.optimization_barrier((swap(part, "zh"), response_grad))
    prompt_key_grad, prompt_low, part = in_vmem(
        keys_zh_kernel,
        1,
        [sent(16, KV_HEADS * HEAD_DIM), sent(16, KV_HEADS * HEAD_DIM), sent(16, 80, HEAD_DIM)],
        "keys_zh",
    )(part)
    first_grad, second_grad = in_vmem(
        group_kernel,
        1,
        [
            jax.ShapeDtypeStruct((RANK, 128), F32),
            jax.ShapeDtypeStruct((RANK, KV_HEADS * HEAD_DIM), F32),
        ],
        "over_group",
    )(swap(part, GROUP))
    return (
        response_grad,
        prompt_gradient(prompt_low, value_adapter_up, down, weight),
        own_key_grad,
        prompt_key_grad,
        first_grad.T,
        second_grad,
    )


def solution(mesh):
    fine = Mesh(np.asarray(mesh.devices).reshape(4, 4, 4, 4, 2), AXES)
    rows = P(AXES, None)
    in_specs = (rows,) * 8 + (P(SAMPLE, None), P(SAMPLE, None), P())
    out_specs = (rows,) * 4 + (P(SAMPLE, None), P())
    return jax.shard_map(
        on_device, mesh=fine, in_specs=in_specs, out_specs=out_specs, check_vma=False
    )
```
